32 devices in a mesh: aux: 8 (over z, core), vir: 2 (over x), outer: 2 (over y).
Axes of the slice: x: 2, y: 2, z: 4, core: 2. Of those that a mesh axis runs over, the one named last changes fastest.
Arguments:
- factors: bfloat16 [128, 256, 2048], P(('aux', 'outer'), None, 'vir'), may hold values from -0.125 to 0.125
- trials: float32 [4, 256, 2048], P('vir', None, 'aux'), may hold values from -6 to 6
Outputs:
- sigma: float32 [4, 256, 2048], P('vir', 'outer', 'aux')
The draws below stay inside these ranges and needn't reach their ends.
All inputs are finite; a program needn't handle non-finite values.
Results may differ from the reference program's by a relative error of at most 0.004.
Values may be sent and summed in bfloat16 or wider, within the bound.
No kernel may reach another device: no remote copies, remote signals or barrier semaphores. Data moves between devices by JAX's collectives and lax.ppermute only.
A program may use at most 64 MiB of HBM per device.

```python
import jax
import jax.numpy as jnp
from jax import lax

O = 256
V = 2048
AUXF = 128
TRIALS = 4


def shard_levels(own_key, shape, pieces, low, top_value):
    def one(dim, shards_of):
        draws = jax.random.uniform(jax.random.fold_in(jax.random.fold_in(own_key, 6), dim), (shards_of,), jnp.float32, low / len(pieces), top_value / len(pieces))
        return jnp.repeat(jnp.exp(draws), shape[dim] // shards_of).reshape((-1,) + (1,) * (len(shape) - dim - 1))

    level = one(*pieces[0])
    for cut in pieces[1:]:
        level = level * one(*cut)
    return level


def centred(key, dims, spread, bound, pieces=(), held_as=jnp.bfloat16):
    entries = jax.random.normal(key, dims, jnp.float32) * spread
    if len(pieces) > 0:
        entries = shard_levels(key, dims, pieces, -0.22, 0.18) * entries
    return jnp.clip(entries, min=-bound, max=bound).astype(held_as)


def setup_inputs(seed: int = 0) -> dict:
    key_list = jax.random.split(jax.random.key(seed), 3)
    return {
        "factors": centred(key_list[0], (AUXF, O, V), V ** -0.5, 0.125, ((0, 16), (2, 2))),
        "trials": centred(key_list[1], (TRIALS, O, V), 1.0, 6.0, ((0, 2), (2, 8)), jnp.float32),
    }


def reference(factors, trials):
    whole = factors.astype(jnp.float32)
    trial_b = trials.astype(jnp.bfloat16)

    def single(vector):
        vec32 = vector.astype(jnp.float32)
        pair = jnp.einsum("qib,jb->qij", whole, vec32).astype(jnp.bfloat16)
        pair = lax.optimization_barrier(pair).astype(jnp.float32)
        return jnp.einsum("qij,qja->ia", pair, whole)

    return lax.map(single, trial_b)
```

```python
import jax
import jax.numpy as jnp
from jax import lax
from jax.sharding import PartitionSpec as P

CORES = 2
PIECES = 2


def plain(factors, trials):
    trial_b = trials.astype(jnp.bfloat16)
    gathered = lax.all_gather(trial_b, "aux", axis=2, tiled=True)
    columns = lax.all_gather(factors, "vir", axis=2, tiled=True)
    pairs = jnp.einsum(
        "qib,mjb->mqij", columns, gathered, preferred_element_type=jnp.float32
    ).astype(jnp.bfloat16)
    stacked = jnp.einsum("mqij,qja->mia", pairs, columns, preferred_element_type=jnp.float32)
    slices = lax.psum_scatter(stacked, "aux", scatter_dimension=2, tiled=True)
    return lax.psum_scatter(slices, "outer", scatter_dimension=1, tiled=True)


def shift(array, axis, size, step, stride=1):
    count = size // stride
    pairs = [
        (i, (i // stride + step) % count * stride + i % stride) for i in range(size)
    ]
    return lax.ppermute(array, axis, pairs)


def sibling(array, size):
    return lax.ppermute(array, "aux", [(i, i ^ 1) for i in range(size)])


def part(array, index, size, axis):
    return lax.dynamic_slice_in_dim(array, index * size, size, axis)


def per_device(na, nv, no, factors, trials):
    f32, bf16 = jnp.float32, jnp.bfloat16
    nq, rows, width = factors.shape
    nm, _, cols = trials.shape
    nz = na // CORES
    a, v, o = (lax.axis_index(name) for name in ("aux", "vir", "outer"))
    z, c = a // CORES, a % CORES
    half_m, take = nm // CORES, nq // nv
    block, total = CORES * cols, nv * width

    trial_b = trials.astype(bf16)
    given = sibling(part(trial_b, 1 - c, half_m, 0), na)
    kept = part(trial_b, c, half_m, 0)
    mine = jnp.where(
        c == 0,
        jnp.concatenate([kept, given], axis=2),
        jnp.concatenate([given, kept], axis=2),
    )
    streams = [mine] + [shift(mine, "vir", nv, -r) for r in range(1, nv)]

    sends = [part(factors, (v - r) % nv, take, 0) for r in range(nv)]
    chunks = []
    for k in range(take):
        group = [sends[0][k : k + 1]]
        for r in range(1, nv):
            group.append(shift(sends[r][k : k + 1], "vir", nv, -r))
        group = [jnp.concatenate([g, sibling(g, na)], axis=0) for g in group]
        chunks.append(jnp.concatenate(group, axis=2))

    vectors = []
    for s in streams:
        whole = jnp.zeros((half_m, rows, total), bf16)
        for t in range(nz):
            at = ((z - t) % nz * block - v * width) % total
            whole = lax.dynamic_update_slice_in_dim(whole, s, at, 2)
            if t < nz - 1:
                s = shift(s, "aux", na, 1, CORES)
        vectors.append(whole)

    def pair(chunk, vec):
        return jnp.einsum("qib,mjb->mqij", chunk, vec, preferred_element_type=f32).astype(bf16)

    def expand(p, chunk):
        return jnp.einsum("mqij,qja->mia", p, chunk, preferred_element_type=f32)

    sums = []
    for vec in vectors:
        one = expand(pair(chunks[-1], vec), chunks[-1])
        if len(chunks) > 1:
            early = jnp.concatenate(chunks[:-1], axis=0)
            one += expand(pair(early, vec), early)
        sums.append(one)
    s = jnp.stack(sums).reshape(nv, half_m, no, PIECES, 2, rows // (no * PIECES * 2), total)

    def over_vir(x):
        got = x[0]
        for r in range(1, nv):
            got += jnp.roll(shift(x[r].astype(bf16), "vir", nv, r).astype(f32), -r * width, axis=-1)
        return got

    def over_outer(x, axis):
        got = lax.dynamic_index_in_dim(x, o, axis, False)
        for r in range(1, no):
            sent = lax.dynamic_index_in_dim(x, (o + r) % no, axis, False).astype(bf16)
            got += shift(sent, "outer", no, r).astype(f32)
        return got

    out = []
    for p in range(PIECES):
        one = over_outer(over_vir(s[:, :, :, p, 0]), 1)
        two = over_vir(over_outer(s[:, :, :, p, 1], 2))
        u = jnp.concatenate([one, two], axis=1)

        def to(zz):
            return lax.dynamic_slice_in_dim(u, (zz * block - v * width) % total, block, 2)

        got = to(z)
        for t in range(1, nz):
            got += shift(to((z + t) % nz).astype(bf16), "aux", na, t, CORES).astype(f32)
        out.append(got)
    done = jnp.concatenate(out, axis=1)
    there = sibling(part(done, 1 - c, cols, 2), na)
    here = part(done, c, cols, 2)
    return jnp.where(
        c == 0, jnp.concatenate([here, there], axis=0), jnp.concatenate([there, here], axis=0)
    )


def solution(mesh):
    na, nv, no = (mesh.shape[name] for name in ("aux", "vir", "outer"))

    def step(factors, trials):
        nq, rows, width = factors.shape
        nm, _, cols = trials.shape
        fits = na % CORES == 0 and nm % CORES == 0 and nq % nv == 0
        fits = fits and width % (CORES * cols) == 0 and rows % (no * PIECES * 2 * 16) == 0
        if fits:
            return per_device(na, nv, no, factors, trials)
        return plain(factors, trials)

    placed = (P(("aux", "outer"), None, "vir"), P("vir", None, "aux"))
    return jax.shard_map(
        step, mesh=mesh, in_specs=placed, out_specs=P("vir", "outer", "aux"), check_vma=False
    )
```

```python
import functools

import jax
import jax.numpy as jnp
from jax import lax
from jax.experimental import pallas as pl
from jax.experimental.pallas import tpu as pltpu
from jax.sharding import PartitionSpec as P

CORES = 2
PIECES = 2
VMEM_LIMIT = 48 * 2**20
F32, BF16 = jnp.float32, jnp.bfloat16
VMEM = pl.BlockSpec(memory_space=pltpu.VMEM)
SMEM = pl.BlockSpec(memory_space=pltpu.SMEM)


def plain(factors, trials):
    trial_b = trials.astype(jnp.bfloat16)
    gathered = lax.all_gather(trial_b, "aux", axis=2, tiled=True)
    columns = lax.all_gather(factors, "vir", axis=2, tiled=True)
    pairs = jnp.einsum(
        "qib,mjb->mqij", columns, gathered, preferred_element_type=jnp.float32
    ).astype(jnp.bfloat16)
    stacked = jnp.einsum("mqij,qja->mia", pairs, columns, preferred_element_type=jnp.float32)
    slices = lax.psum_scatter(stacked, "aux", scatter_dimension=2, tiled=True)
    return lax.psum_scatter(slices, "outer", scatter_dimension=1, tiled=True)


def shift(array, axis, size, step, stride=1):
    count = size // stride
    pairs = [
        (i, (i // stride + step) % count * stride + i % stride) for i in range(size)
    ]
    return lax.ppermute(array, axis, pairs)


def sibling(array, size):
    return lax.ppermute(array, "aux", [(i, i ^ 1) for i in range(size)])


def part(array, index, size, axis):
    return lax.dynamic_slice_in_dim(array, index * size, size, axis)


def dot_nt(a, b):
    return lax.dot_general(a, b, (((1,), (1,)), ((), ())), preferred_element_type=F32)


def assemble(where, blocks, groups, rows, total):
    nt, ns = len(blocks), len(blocks[0])
    _, share, block = blocks[0][0].shape

    def body(at, *refs):
        out = refs[-1]
        for t in range(nt):
            col = pl.multiple_of(at[t], block)
            for s in range(ns):
                row = pl.multiple_of(at[nt + s], share)
                for g in range(groups):
                    out[g, pl.ds(row, share), pl.ds(col, block)] = refs[t * ns + s][g]

    flat = [b for row in blocks for b in row]
    moved = 2 * groups * rows * total * 2
    return pl.pallas_call(
        body,
        out_shape=jax.ShapeDtypeStruct((groups, rows, total), BF16),
        in_specs=[SMEM] + [VMEM] * len(flat),
        out_specs=VMEM,
        cost_estimate=pl.CostEstimate(flops=0, bytes_accessed=moved, transcendentals=0),
        compiler_params=pltpu.CompilerParams(vmem_limit_bytes=VMEM_LIMIT),
        name="assemble",
    )(where, *flat)


def early_sums(parts, vectors):
    groups, rows, total = vectors.shape
    flat = [p for side in parts for p in side]
    nr = len(parts[0])
    steps, _, width = flat[0].shape

    def body(*refs):
        vec, out = refs[len(flat)], refs[-1]

        @pl.when(pl.program_id(0) == 0)
        def _():
            out[...] = jnp.zeros_like(out)

        for g in range(groups):
            pairs = []
            for side in range(len(parts)):
                acc = None
                for r in range(nr):
                    term = dot_nt(refs[side * nr + r][0], vec[g, :, r * width : (r + 1) * width])
                    acc = term if acc is None else acc + term
                pairs.append(acc.astype(BF16))
            for r in range(nr):
                cols = slice(r * width, (r + 1) * width)
                acc = out[g, :, cols]
                for side, pair in enumerate(pairs):
                    acc = acc + jnp.dot(pair, refs[side * nr + r][0], preferred_element_type=F32)
                out[g, :, cols] = acc

    work = 4 * len(parts) * steps * groups * rows * rows * total
    moved = sum(2 * p.size for p in flat) + 2 * vectors.size + 4 * vectors.size
    return pl.pallas_call(
        body,
        grid=(steps,),
        out_shape=jax.ShapeDtypeStruct((groups, rows, total), F32),
        in_specs=[pl.BlockSpec((1, rows, width), lambda k: (k, 0, 0)) for _ in flat]
        + [pl.BlockSpec((groups, rows, total), lambda k: (0, 0, 0))],
        out_specs=pl.BlockSpec((groups, rows, total), lambda k: (0, 0, 0)),
        cost_estimate=pl.CostEstimate(flops=work, bytes_accessed=moved, transcendentals=0),
        compiler_params=pltpu.CompilerParams(vmem_limit_bytes=VMEM_LIMIT),
        name="early_sums",
    )(*flat, vectors)


def last_sums(piece, o, parts, vectors, early, no, nv):
    groups, rows, total = vectors.shape
    flat = [p for side in parts for p in side]
    nr = len(parts[0])
    width = total // nr
    per = groups // nv
    own = rows // no
    small = own // (PIECES * 2)
    more = [] if early is None else [early.reshape(groups, no, PIECES, 2, small, total)]

    def body(*refs):
        me = refs[0][0]
        ins = refs[1 : 1 + len(flat)]
        vec = refs[1 + len(flat)]
        before = refs[2 + len(flat)] if more else None
        send_x, keep_x, send_y, keep_y, acc = refs[-5:]

        def piece_rows(ref):
            found = []
            for oo in range(no):
                at = oo * own + piece * 2 * small
                found.append(ref[0, at : at + 2 * small, :])
            return jnp.concatenate(found, axis=0)

        left = [piece_rows(ref) for ref in ins]
        for g in range(groups):
            pairs = []
            for side in range(len(parts)):
                total_p = None
                for r in range(nr):
                    term = dot_nt(left[side * nr + r], vec[g, :, r * width : (r + 1) * width])
                    total_p = term if total_p is None else total_p + term
                pairs.append(total_p.astype(BF16))
            v = g // per
            for r in range(nr):
                got = None
                for side, pair in enumerate(pairs):
                    term = jnp.dot(pair, ins[side * nr + r][0], preferred_element_type=F32)
                    got = term if got is None else got + term
                got = got.reshape(no, 2, small, width)
                if before is not None:
                    got = got + before[g, :, 0, :, :, r * width : (r + 1) * width]
                to = (r - v) % nr * width
                cols = slice(to, to + width)
                if v == 0:
                    keep_x[g, :, :, cols] = got[:, 0]
                else:
                    send_x[g - per, :, :, cols] = got[:, 0].astype(BF16)
                acc[:, g, :, cols] = got[:, 1]
        keep_y[...] = acc[me]
        for s in range(1, no):
            send_y[s - 1] = acc[lax.rem(me + s, no)].astype(BF16)

    work = 4 * len(parts) * groups * rows * rows * total // PIECES
    moved = sum(2 * p.size for p in flat) + 2 * vectors.size + 2 * vectors.size
    early_spec = [
        pl.BlockSpec((groups, no, 1, 2, small, total), lambda k: (0, 0, piece, 0, 0, 0)) for _ in more
    ]

    def whole(*shape):
        return pl.BlockSpec(shape, lambda k: (0,) * len(shape))

    shapes = [
        ((groups - per, no, small, total), BF16),
        ((per, no, small, total), F32),
        ((no - 1, groups, small, total), BF16),
        ((groups, small, total), F32),
    ]
    return pl.pallas_call(
        body,
        grid=(1,),
        out_shape=[jax.ShapeDtypeStruct(s, d) for s, d in shapes],
        in_specs=[SMEM] + [whole(*p.shape) for p in flat] + [whole(*vectors.shape)] + early_spec,
        out_specs=[whole(*s) for s, _ in shapes],
        scratch_shapes=[pltpu.VMEM((no, groups, small, total), F32)],
        cost_estimate=pl.CostEstimate(flops=work, bytes_accessed=moved, transcendentals=0),
        compiler_params=pltpu.CompilerParams(vmem_limit_bytes=VMEM_LIMIT),
        name="last_sums",
    )(o.reshape(1), *flat, vectors, *more)


def per_device(na, nv, no, factors, trials):
    nq, rows, width = factors.shape
    nm, _, cols = trials.shape
    nz = na // CORES
    a, v, o = (lax.axis_index(name) for name in ("aux", "vir", "outer"))
    z, c = a // CORES, a % CORES
    half_m, take = nm // CORES, nq // nv
    block, total = CORES * cols, nv * width
    own = rows // no
    groups = nv * half_m

    mine = part(trials, o, own, 1).astype(BF16)
    both = jnp.concatenate([mine] + [shift(mine, "vir", nv, -r) for r in range(1, nv)], axis=0)
    both = both.reshape(nv, CORES, half_m, own, cols)
    given = sibling(lax.dynamic_index_in_dim(both, 1 - c, 1, False), na)
    kept = lax.dynamic_index_in_dim(both, c, 1, False)
    whole = jnp.where(
        c == 0,
        jnp.concatenate([kept, given], axis=-1),
        jnp.concatenate([given, kept], axis=-1),
    ).reshape(groups, own, block)

    sizes = [take - 1, 1] if take > 1 else [1]
    sides = []
    first = 0
    held, _ = lax.optimization_barrier((factors, both))
    for size in sizes:
        got = [lax.dynamic_slice_in_dim(held, v * take + first, size, 0)]
        for r in range(1, nv):
            sent = lax.dynamic_slice_in_dim(held, (v - r) % nv * take + first, size, 0)
            got.append(shift(sent, "vir", nv, -r))
        sides.append(got)
        first += size

    blocks = []
    for t in range(nz):
        got = whole if t == 0 else shift(whole, "aux", na, t, CORES)
        blocks.append([got] + [shift(got, "outer", no, -s) for s in range(1, no)])
    where = jnp.stack(
        [((z - t) % nz * block - v * width) % total for t in range(nz)]
        + [(o + s) % no * own for s in range(no)]
    ).astype(jnp.int32)
    vectors = assemble(where, blocks, groups, rows, total)

    early = None
    if take > 1:
        got, vectors = lax.optimization_barrier((sides[0], vectors))
        early = early_sums([got, [sibling(g, na) for g in got]], vectors)
    got, early = lax.optimization_barrier((sides[-1], early))
    last = [got, [sibling(g, na) for g in got]]

    out = []
    for p in range(PIECES):
        send_x, keep_x, send_y, keep_y = last_sums(p, o, last, vectors, early, no, nv)
        one = keep_x
        for r in range(1, nv):
            sent = send_x[(r - 1) * half_m : r * half_m]
            one += shift(sent, "vir", nv, r).astype(F32)
        u_one = lax.dynamic_index_in_dim(one, o, 1, False)
        for s in range(1, no):
            sent = lax.dynamic_index_in_dim(one, (o + s) % no, 1, False).astype(BF16)
            u_one += shift(sent, "outer", no, s).astype(F32)
        two = keep_y
        for s in range(1, no):
            two += shift(send_y[s - 1], "outer", no, s).astype(F32)
        u_two = two[:half_m]
        for r in range(1, nv):
            sent = two[r * half_m : (r + 1) * half_m].astype(BF16)
            u_two += shift(sent, "vir", nv, r).astype(F32)
        u = jnp.concatenate([u_one, u_two], axis=1)

        def to(zz):
            return lax.dynamic_slice_in_dim(u, (zz * block - v * width) % total, block, 2)

        got = to(z)
        for t in range(1, nz):
            got += shift(to((z + t) % nz).astype(BF16), "aux", na, t, CORES).astype(F32)
        out.append(got)
    done = jnp.concatenate(out, axis=1)
    there = sibling(part(done, 1 - c, cols, 2), na)
    here = part(done, c, cols, 2)
    return jnp.where(
        c == 0, jnp.concatenate([here, there], axis=0), jnp.concatenate([there, here], axis=0)
    )


def solution(mesh):
    na, nv, no = (mesh.shape[name] for name in ("aux", "vir", "outer"))

    def step(factors, trials):
        nq, rows, width = factors.shape
        nm, _, cols = trials.shape
        fits = na % CORES == 0 and nm % CORES == 0 and nq % nv == 0
        fits = fits and width % (CORES * cols) == 0 and cols % 128 == 0
        fits = fits and rows % (no * PIECES * 2 * 16) == 0
        if fits:
            return per_device(na, nv, no, factors, trials)
        return plain(factors, trials)

    placed = (P(("aux", "outer"), None, "vir"), P("vir", None, "aux"))
    return jax.shard_map(
        step, mesh=mesh, in_specs=placed, out_specs=P("vir", "outer", "aux"), check_vma=False
    )
```

```python
import jax
import jax.numpy as jnp
from jax import lax
from jax.experimental import pallas as pl
from jax.experimental.pallas import tpu as pltpu
from jax.sharding import PartitionSpec as P

CORES = 2
PIECES = 2
VMEM_LIMIT = 8 * 2**20
F32, BF16 = jnp.float32, jnp.bfloat16
VMEM = pl.BlockSpec(memory_space=pltpu.VMEM)
SMEM = pl.BlockSpec(memory_space=pltpu.SMEM)


def plain(factors, trials):
    trial_b = trials.astype(jnp.bfloat16)
    gathered = lax.all_gather(trial_b, "aux", axis=2, tiled=True)
    columns = lax.all_gather(factors, "vir", axis=2, tiled=True)
    pairs = jnp.einsum(
        "qib,mjb->mqij", columns, gathered, preferred_element_type=jnp.float32
    ).astype(jnp.bfloat16)
    stacked = jnp.einsum("mqij,qja->mia", pairs, columns, preferred_element_type=jnp.float32)
    slices = lax.psum_scatter(stacked, "aux", scatter_dimension=2, tiled=True)
    return lax.psum_scatter(slices, "outer", scatter_dimension=1, tiled=True)


def shift(array, axis, size, step, stride=1):
    count = size // stride
    pairs = [
        (i, (i // stride + step) % count * stride + i % stride) for i in range(size)
    ]
    return lax.ppermute(array, axis, pairs)


def sibling(array, size):
    return lax.ppermute(array, "aux", [(i, i ^ 1) for i in range(size)])


def part(array, index, size, axis):
    return lax.dynamic_slice_in_dim(array, index * size, size, axis)


def dot_nt(a, b):
    return lax.dot_general(a, b, (((1,), (1,)), ((), ())), preferred_element_type=F32)


def params():
    return pltpu.CompilerParams(vmem_limit_bytes=VMEM_LIMIT)


def cost(flops, *arrays):
    moved = sum(x.size * x.dtype.itemsize for x in arrays)
    return pl.CostEstimate(flops=flops, bytes_accessed=moved, transcendentals=0)


def assemble(where, blocks, groups, rows, total):
    shape = jax.ShapeDtypeStruct((groups, rows, total), BF16)

    def body(at, *refs):
        out = refs[-1]
        for ref, (_, first, row_slot, col_slot) in zip(refs, blocks):
            many, share, block = ref.shape
            row = pl.multiple_of(at[row_slot], share)
            col = pl.multiple_of(at[col_slot], block)
            for g in range(many):
                out[first + g, pl.ds(row, share), pl.ds(col, block)] = ref[g]

    return pl.pallas_call(
        body,
        out_shape=shape,
        in_specs=[SMEM] + [VMEM] * len(blocks),
        out_specs=VMEM,
        cost_estimate=cost(0, shape, shape),
        compiler_params=params(),
        name="assemble",
    )(where, *[b[0] for b in blocks])


def pairs_of(refs, firsts, count, vec, store):
    groups, rows, _ = vec.shape
    for g in range(groups):
        acc = None
        for r, (ref, first) in enumerate(zip(refs, firsts)):
            width = ref.shape[2]
            left = ref[first : first + count].reshape(count * rows, width)
            term = dot_nt(left, vec[g, :, r * width : (r + 1) * width])
            acc = term if acc is None else acc + term
        acc = acc.astype(BF16)
        for k in range(count):
            store(g, k, acc[k * rows : (k + 1) * rows])


def early_sums(sides, steps, vectors):
    groups, rows, total = vectors.shape
    nr = len(sides[0])
    width = total // nr
    flat = [p for side in sides for p in side]
    shape = jax.ShapeDtypeStruct((groups, rows, total), F32)
    tile = min(width, 512)

    def body(*refs):
        vec, out, held = refs[len(flat) :]
        for s in range(len(sides)):

            def store(g, k, pair, s=s):
                held[s, g * rows : (g + 1) * rows, k * rows : (k + 1) * rows] = pair

            pairs_of(refs[s * nr : (s + 1) * nr], [0] * nr, steps, vec, store)
        for r in range(nr):
            for at in range(0, width, tile):
                acc = None
                for s in range(len(sides)):
                    right = refs[s * nr + r][0:steps, :, at : at + tile]
                    term = jnp.dot(
                        held[s], right.reshape(steps * rows, tile), preferred_element_type=F32
                    )
                    acc = term if acc is None else acc + term
                col = r * width + at
                out[:, :, col : col + tile] = acc.reshape(groups, rows, tile)

    work = 4 * len(sides) * steps * groups * rows * rows * total
    return pl.pallas_call(
        body,
        out_shape=shape,
        in_specs=[VMEM] * (len(flat) + 1),
        out_specs=VMEM,
        scratch_shapes=[pltpu.VMEM((len(sides), groups * rows, steps * rows), BF16)],
        cost_estimate=cost(work, *flat, vectors, shape),
        compiler_params=params(),
        name="early_sums",
    )(*flat, vectors)


def own_pairs(side, firsts, vectors):
    groups, rows, total = vectors.shape
    shape = jax.ShapeDtypeStruct((groups, rows, rows), BF16)

    def body(*refs):
        vec, out = refs[-2:]

        def store(g, _, pair):
            out[g] = pair

        pairs_of(refs[:-2], firsts, 1, vec, store)

    return pl.pallas_call(
        body,
        out_shape=shape,
        in_specs=[VMEM] * (len(side) + 1),
        out_specs=VMEM,
        cost_estimate=cost(2 * groups * rows * rows * total, *side, vectors),
        compiler_params=params(),
        name="own_pairs",
    )(*side, vectors)


def last_sums(piece, o, sides, firsts, pairs, early, no, nv):
    groups, rows, _ = pairs[0].shape
    nr = len(sides[0])
    width = sides[0][0].shape[2]
    total = nr * width
    flat = [p for side in sides for p in side]
    per = groups // nv
    own = rows // no
    small = own // (PIECES * 2)
    more = [] if early is None else [early]
    tile = min(width, 512)

    def body(*refs):
        me = refs[0][0]
        ins = refs[1 : 1 + len(flat)]
        pair_refs = refs[1 + len(flat) : 1 + len(flat) + len(pairs)]
        before = refs[1 + len(flat) + len(pairs)]
        send_x, keep_x, send_y, keep_y, acc = refs[-5:]
        places = [oo * own + piece * 2 * small for oo in range(no)]
        left = [
            jnp.concatenate(
                [ref[g, at : at + 2 * small, :] for g in range(groups) for at in places], axis=0
            )
            for ref in pair_refs
        ]
        for r in range(nr):
            for at in range(0, width, tile):
                got = None
                for s in range(len(sides)):
                    right = ins[s * nr + r][firsts[r], :, at : at + tile]
                    term = jnp.dot(left[s], right, preferred_element_type=F32)
                    got = term if got is None else got + term
                got = got.reshape(groups, no, 2, small, tile)
                for g in range(groups):
                    v = g // per
                    to = (r - v) % nr * width + at
                    cols = slice(to, to + tile)
                    for oo in range(no):
                        half = [got[g, oo, 0], got[g, oo, 1]]
                        if more:
                            col = r * width + at
                            for h in range(2):
                                row = places[oo] + h * small
                                half[h] += before[g, row : row + small, col : col + tile]
                        if v == 0:
                            keep_x[g, oo, :, cols] = half[0]
                        else:
                            send_x[g - per, oo, :, cols] = half[0].astype(BF16)
                        acc[oo, g, :, cols] = half[1]
        keep_y[...] = acc[me]
        for s in range(1, no):
            send_y[s - 1] = acc[lax.rem(me + s, no)].astype(BF16)

    work = 2 * len(sides) * groups * rows * rows * total // PIECES
    shapes = [
        jax.ShapeDtypeStruct((groups - per, no, small, total), BF16),
        jax.ShapeDtypeStruct((per, no, small, total), F32),
        jax.ShapeDtypeStruct((no - 1, groups, small, total), BF16),
        jax.ShapeDtypeStruct((groups, small, total), F32),
    ]
    return pl.pallas_call(
        body,
        out_shape=shapes,
        in_specs=[SMEM] + [VMEM] * (len(flat) + len(pairs) + len(more)),
        out_specs=[VMEM] * len(shapes),
        scratch_shapes=[pltpu.VMEM((no, groups, small, total), F32)],
        cost_estimate=cost(work, *flat, *pairs, *shapes, *shapes),
        compiler_params=params(),
        name="last_sums",
    )(o.reshape(1), *flat, *pairs, *more)


def per_device(na, nv, no, factors, trials):
    nq, rows, width = factors.shape
    nm, _, cols = trials.shape
    nz = na // CORES
    a, v, o = (lax.axis_index(name) for name in ("aux", "vir", "outer"))
    z, c = a // CORES, a % CORES
    half_m, take = nm // CORES, nq // nv
    block, total = CORES * cols, nv * width
    own = rows // no
    groups = nv * half_m
    early_steps = take - 1

    trial_b = trials.astype(BF16)
    mine = part(trial_b, o, own, 1)
    others = [shift(mine, "vir", nv, -r) for r in range(1, nv)]

    def over_cores(x):
        x = x.reshape(x.shape[0] // nm, CORES, half_m, *x.shape[1:])
        given = sibling(lax.dynamic_index_in_dim(x, 1 - c, 1, False), na)
        kept = lax.dynamic_index_in_dim(x, c, 1, False)
        both = jnp.where(
            c == 0,
            jnp.concatenate([kept, given], axis=-1),
            jnp.concatenate([given, kept], axis=-1),
        )
        return both.reshape(-1, *both.shape[2:])

    own_whole = over_cores(trial_b)
    own_part = part(own_whole, o, own, 1)

    held, own_part = lax.optimization_barrier((factors, own_part))
    sizes = [early_steps, 1] if early_steps else [1]
    come, first = [], 0
    for size in sizes:
        got = []
        for r in range(1, nv):
            sent = lax.dynamic_slice_in_dim(held, (v - r) % nv * take + first, size, 0)
            got.append(shift(sent, "vir", nv, -r))
        come.append(got)
        first += size

    their = over_cores(jnp.concatenate(others, axis=0)) if others else None
    blocks = []
    for first, x in ((0, own_part), (half_m, their)):
        for t in range(nz):
            if x is None:
                continue
            if t == 0 and first == 0:
                for s in range(no):
                    blocks.append((part(own_whole, (o + s) % no, own, 1), 0, nz + s, 0))
                continue
            got = x if t == 0 else shift(x, "aux", na, t, CORES)
            blocks.append((got, first, nz, t))
            for s in range(1, no):
                blocks.append((shift(got, "outer", no, -s), first, nz + s, t))
    where = jnp.stack(
        [((z - t) % nz * block - v * width) % total for t in range(nz)]
        + [(o + s) % no * own for s in range(no)]
    ).astype(jnp.int32)
    vectors = assemble(where, blocks, groups, rows, total)

    later, _ = lax.optimization_barrier((factors, blocks[-no][0]))
    kept = lax.dynamic_slice_in_dim(later, v * take, take, 0)
    shown = sibling(kept, na)
    early = None
    if early_steps:
        got, vectors = lax.optimization_barrier((come[0], vectors))
        early = early_sums(
            [[kept] + got, [shown] + [sibling(g, na) for g in got]], early_steps, vectors
        )
    got, early = lax.optimization_barrier((come[-1], early))
    sides = [[kept] + got, [shown] + [sibling(g, na) for g in got]]
    firsts = [early_steps] + [0] * (nv - 1)
    pairs = [own_pairs(side, firsts, vectors) for side in sides]

    out = []
    for p in range(PIECES):
        send_x, keep_x, send_y, keep_y = last_sums(p, o, sides, firsts, pairs, early, no, nv)
        one = keep_x
        for r in range(1, nv):
            sent = send_x[(r - 1) * half_m : r * half_m]
            one += shift(sent, "vir", nv, r).astype(F32)
        u_one = lax.dynamic_index_in_dim(one, o, 1, False)
        for s in range(1, no):
            sent = lax.dynamic_index_in_dim(one, (o + s) % no, 1, False).astype(BF16)
            u_one += shift(sent, "outer", no, s).astype(F32)
        two = keep_y
        for s in range(1, no):
            two += shift(send_y[s - 1], "outer", no, s).astype(F32)
        u_two = two[:half_m]
        for r in range(1, nv):
            sent = two[r * half_m : (r + 1) * half_m].astype(BF16)
            u_two += shift(sent, "vir", nv, r).astype(F32)
        u = jnp.concatenate([u_one, u_two], axis=1)

        def to(zz):
            return lax.dynamic_slice_in_dim(u, (zz * block - v * width) % total, block, 2)

        got = to(z)
        for t in range(1, nz):
            got += shift(to((z + t) % nz).astype(BF16), "aux", na, t, CORES).astype(F32)
        out.append(got)
    done = jnp.concatenate(out, axis=1)
    there = sibling(part(done, 1 - c, cols, 2), na)
    here = part(done, c, cols, 2)
    return jnp.where(
        c == 0, jnp.concatenate([here, there], axis=0), jnp.concatenate([there, here], axis=0)
    )


def solution(mesh):
    na, nv, no = (mesh.shape[name] for name in ("aux", "vir", "outer"))

    def step(factors, trials):
        nq, rows, width = factors.shape
        nm, _, cols = trials.shape
        fits = na % CORES == 0 and nm % CORES == 0 and nq % nv == 0
        fits = fits and width % (CORES * cols) == 0 and cols % 128 == 0
        fits = fits and rows % (no * PIECES * 2 * 16) == 0
        if fits:
            return per_device(na, nv, no, factors, trials)
        return plain(factors, trials)

    placed = (P(("aux", "outer"), None, "vir"), P("vir", None, "aux"))
    return jax.shard_map(
        step, mesh=mesh, in_specs=placed, out_specs=P("vir", "outer", "aux"), check_vma=False
    )
```

```python
import jax
import jax.numpy as jnp
from jax import lax
from jax.experimental import pallas as pl
from jax.experimental.pallas import tpu as pltpu
from jax.sharding import PartitionSpec as P

CORES = 2
PIECES = 2
VMEM_LIMIT = 28 * 2**20
F32, BF16 = jnp.float32, jnp.bfloat16
VMEM = pl.BlockSpec(memory_space=pltpu.VMEM)
ANY = pl.BlockSpec(memory_space=pl.ANY)
SMEM = pl.BlockSpec(memory_space=pltpu.SMEM)


def plain(factors, trials):
    trial_b = trials.astype(jnp.bfloat16)
    gathered = lax.all_gather(trial_b, "aux", axis=2, tiled=True)
    columns = lax.all_gather(factors, "vir", axis=2, tiled=True)
    pairs = jnp.einsum(
        "qib,mjb->mqij", columns, gathered, preferred_element_type=jnp.float32
    ).astype(jnp.bfloat16)
    stacked = jnp.einsum("mqij,qja->mia", pairs, columns, preferred_element_type=jnp.float32)
    slices = lax.psum_scatter(stacked, "aux", scatter_dimension=2, tiled=True)
    return lax.psum_scatter(slices, "outer", scatter_dimension=1, tiled=True)


def shift(array, axis, size, step, stride=1):
    count = size // stride
    pairs = [
        (i, (i // stride + step) % count * stride + i % stride) for i in range(size)
    ]
    return lax.ppermute(array, axis, pairs)


def sibling(array, size):
    return lax.ppermute(array, "aux", [(i, i ^ 1) for i in range(size)])


def part(array, index, size, axis):
    return lax.dynamic_slice_in_dim(array, index * size, size, axis)


def dot_nt(a, b):
    return lax.dot_general(a, b, (((1,), (1,)), ((), ())), preferred_element_type=F32)


def params():
    return pltpu.CompilerParams(vmem_limit_bytes=VMEM_LIMIT)


def cost(flops, *arrays):
    moved = sum(x.size * x.dtype.itemsize for x in arrays)
    return pl.CostEstimate(flops=flops, bytes_accessed=moved, transcendentals=0)


def assemble(where, blocks, groups, rows, total):
    shape = jax.ShapeDtypeStruct((groups, rows, total), BF16)

    def body(at, *refs):
        out, sems = refs[-2:]
        copies = []
        for i, (_, first, row_slot, col_slot) in enumerate(blocks):
            many, share, block = refs[i].shape
            row = pl.multiple_of(at[row_slot], share)
            col = pl.multiple_of(at[col_slot], block)
            to = out.at[pl.ds(first, many), pl.ds(row, share), pl.ds(col, block)]
            copies.append(pltpu.make_async_copy(refs[i], to, sems.at[i]))
        for copy in copies:
            copy.start()
        for copy in copies:
            copy.wait()

    return pl.pallas_call(
        body,
        out_shape=shape,
        in_specs=[SMEM] + [ANY] * len(blocks),
        out_specs=ANY,
        scratch_shapes=[pltpu.SemaphoreType.DMA((len(blocks),))],
        cost_estimate=cost(0, shape),
        compiler_params=params(),
        name="assemble",
    )(where, *[b[0] for b in blocks])


def pairs_of(refs, vec, store):
    groups, rows, _ = vec.shape
    count, _, width = refs[0].shape
    for g in range(groups):
        acc = None
        for r, ref in enumerate(refs):
            left = ref[...].reshape(count * rows, width)
            term = dot_nt(left, vec[g, :, r * width : (r + 1) * width])
            acc = term if acc is None else acc + term
        acc = acc.astype(BF16)
        for k in range(count):
            store(g, k, acc[k * rows : (k + 1) * rows])


def early_sums(sides, steps, vectors):
    groups, rows, total = vectors.shape
    nr = len(sides[0])
    width = total // nr
    flat = [p for side in sides for p in side]
    n = len(flat)
    shape = jax.ShapeDtypeStruct((groups, rows, total), F32)
    tile = min(width, 512)
    tiles = total // tile

    def body(*refs):
        vec_in, out = refs[n : n + 2]
        vec, held, done, sems, out_sems = refs[-5:]
        ins = refs[n + 2 : 2 * n + 2]
        first = pltpu.make_async_copy(vec_in, vec, sems.at[n])
        first.start()
        copies = [
            pltpu.make_async_copy(refs[i].at[pl.ds(0, steps)], ins[i], sems.at[i]) for i in range(n)
        ]
        for copy in copies:
            copy.start()
        first.wait()
        for s in range(len(sides)):

            def store(g, k, pair, s=s):
                held[s, g * rows : (g + 1) * rows, k * rows : (k + 1) * rows] = pair

            for copy in copies[s * nr : (s + 1) * nr]:
                copy.wait()
            pairs_of(ins[s * nr : (s + 1) * nr], vec, store)
        sent = []
        for i in range(tiles):
            r, at = i * tile // width, i * tile % width
            acc = None
            for s in range(len(sides)):
                right = ins[s * nr + r][:, :, at : at + tile].reshape(steps * rows, tile)
                term = jnp.dot(held[s], right, preferred_element_type=F32)
                acc = term if acc is None else acc + term
            cols = pl.ds(i * tile, tile)
            done[:, :, cols] = acc.reshape(groups, rows, tile)
            sent.append(
                pltpu.make_async_copy(done.at[:, :, cols], out.at[:, :, cols], out_sems.at[i])
            )
            sent[-1].start()
        for copy in sent:
            copy.wait()

    return pl.pallas_call(
        body,
        out_shape=shape,
        in_specs=[ANY] * (n + 1),
        out_specs=ANY,
        scratch_shapes=[pltpu.VMEM((steps, rows, width), BF16)] * n
        + [
            pltpu.VMEM(vectors.shape, BF16),
            pltpu.VMEM((len(sides), groups * rows, steps * rows), BF16),
            pltpu.VMEM(shape.shape, F32),
            pltpu.SemaphoreType.DMA((n + 1,)),
            pltpu.SemaphoreType.DMA((tiles,)),
        ],
        cost_estimate=cost(0, vectors),
        compiler_params=params(),
        name="early_sums",
    )(*flat, vectors)


def step_pairs(side, firsts, vectors):
    groups, rows, total = vectors.shape
    shape = jax.ShapeDtypeStruct((groups, rows, rows), BF16)
    n = len(side)
    width = total // n

    def body(*refs):
        vec_in, out = refs[n : n + 2]
        ins = refs[n + 2 : 2 * n + 2]
        vec, sems = refs[-2:]
        copies = [pltpu.make_async_copy(vec_in, vec, sems.at[n])] + [
            pltpu.make_async_copy(refs[i].at[pl.ds(firsts[i], 1)], ins[i], sems.at[i])
            for i in range(n)
        ]
        for copy in copies:
            copy.start()
        for copy in copies:
            copy.wait()

        def store(g, _, pair):
            out[g] = pair

        pairs_of(ins, vec, store)

    return pl.pallas_call(
        body,
        out_shape=shape,
        in_specs=[ANY] * (n + 1),
        out_specs=VMEM,
        scratch_shapes=[pltpu.VMEM((1, rows, width), BF16)] * n
        + [pltpu.VMEM(vectors.shape, BF16), pltpu.SemaphoreType.DMA((n + 1,))],
        cost_estimate=cost(0, vectors),
        compiler_params=params(),
        name="step_pairs",
    )(*side, vectors)


def last_sums(o, sides, firsts, pair_own, vectors, early, no, nv):
    groups, rows, total = vectors.shape
    nr = len(sides[0])
    width = total // nr
    flat = [p for side in sides for p in side]
    n = len(flat)
    per = groups // nv
    own = rows // no
    small = own // (PIECES * 2)
    more = [] if early is None else [early]
    tile = min(width, 512)
    tiles = total // tile

    def body(*refs):
        me = refs[0][0]
        refs = refs[1:]
        pair_in, vec_in = refs[n : n + 2]
        results = refs[n + 2 + len(more) : n + 2 + len(more) + 4 * PIECES]
        outs = refs[n + 2 + len(more) + 4 * PIECES : n + 2 + len(more) + 8 * PIECES]
        ins = refs[-n - 7 : -7]
        vec, own_pair, their_pair, before, sems, early_sems, out_sems = refs[-7:]
        copies = [
            pltpu.make_async_copy(refs[i].at[pl.ds(firsts[i % nr], 1)], ins[i], sems.at[i])
            for i in range(n)
        ]
        vec_copy = pltpu.make_async_copy(vec_in, vec, sems.at[n])
        pair_copy = pltpu.make_async_copy(pair_in, own_pair, sems.at[n + 1])
        vec_copy.start()
        for copy in copies[nr:] + copies[:nr]:
            copy.start()
        pair_copy.start()
        early_copies = []
        for i in range(tiles if more else 0):
            cols = pl.ds(i * tile, tile)
            early_copies.append(
                pltpu.make_async_copy(
                    refs[n + 2].at[:, :, cols], before.at[:, :, cols], early_sems.at[i]
                )
            )
            early_copies[-1].start()
        vec_copy.wait()
        for copy in copies[nr:]:
            copy.wait()

        def store(g, _, pair):
            their_pair[g] = pair

        pairs_of(ins[nr:], vec, store)
        for copy in copies[:nr]:
            copy.wait()
        pair_copy.wait()
        left = [p[...].reshape(groups * rows, rows) for p in (own_pair, their_pair)]
        for i in range(tiles):
            r, at = i * tile // width, i * tile % width
            got = None
            for s in range(len(sides)):
                right = ins[s * nr + r][0, :, at : at + tile]
                term = jnp.dot(left[s], right, preferred_element_type=F32)
                got = term if got is None else got + term
            got = got.reshape(groups, rows, tile)
            if more:
                early_copies[i].wait()
                got = got + before[:, :, i * tile : (i + 1) * tile]
            got = got.reshape(groups, no, PIECES, 2, small, tile)
            for g in range(groups):
                v = g // per
                to = (r - v) % nr * width + at
                cols = slice(to, to + tile)
                for p in range(PIECES):
                    send_x, keep_x, send_y, keep_y = outs[4 * p : 4 * p + 4]
                    for oo in range(no):
                        if v == 0:
                            keep_x[g, oo, :, cols] = got[g, oo, p, 0]
                        else:
                            send_x[g - per, oo, :, cols] = got[g, oo, p, 0].astype(BF16)
            for s in range(no):
                for oo in range(no):

                    @pl.when(lax.rem(me + s, no) == oo)
                    def _(s=s, oo=oo, got=got, r=r, at=at):
                        for g in range(groups):
                            to = (r - g // per) % nr * width + at
                            cols = slice(to, to + tile)
                            for p in range(PIECES):
                                if s == 0:
                                    outs[4 * p + 3][g, :, cols] = got[g, oo, p, 1]
                                else:
                                    outs[4 * p + 2][s - 1, g, :, cols] = got[g, oo, p, 1].astype(BF16)
        sent = [
            pltpu.make_async_copy(out, result, out_sems.at[i])
            for i, (out, result) in enumerate(zip(outs, results))
        ]
        for copy in sent:
            copy.start()
        for copy in sent:
            copy.wait()

    shapes = [
        jax.ShapeDtypeStruct((groups - per, no, small, total), BF16),
        jax.ShapeDtypeStruct((per, no, small, total), F32),
        jax.ShapeDtypeStruct((no - 1, groups, small, total), BF16),
        jax.ShapeDtypeStruct((groups, small, total), F32),
    ] * PIECES
    outs = pl.pallas_call(
        body,
        out_shape=shapes,
        in_specs=[SMEM] + [ANY] * (n + 2 + len(more)),
        out_specs=[ANY] * len(shapes),
        scratch_shapes=[pltpu.VMEM(x.shape, x.dtype) for x in shapes]
        + [pltpu.VMEM((1, rows, width), BF16)] * n
        + [
            pltpu.VMEM(vectors.shape, BF16),
            pltpu.VMEM((groups, rows, rows), BF16),
            pltpu.VMEM((groups, rows, rows), BF16),
            pltpu.VMEM(vectors.shape if more else (8, 128), F32),
            pltpu.SemaphoreType.DMA((n + 2,)),
            pltpu.SemaphoreType.DMA((tiles,)),
            pltpu.SemaphoreType.DMA((len(shapes),)),
        ],
        cost_estimate=cost(0, *shapes),
        compiler_params=params(),
        name="last_sums",
    )(o.reshape(1), *flat, pair_own, vectors, *more)
    return [outs[4 * p : 4 * p + 4] for p in range(PIECES)]


def per_device(na, nv, no, factors, trials):
    nq, rows, width = factors.shape
    nm, _, cols = trials.shape
    nz = na // CORES
    a, v, o = (lax.axis_index(name) for name in ("aux", "vir", "outer"))
    z, c = a // CORES, a % CORES
    half_m, take = nm // CORES, nq // nv
    block, total = CORES * cols, nv * width
    own = rows // no
    groups = nv * half_m
    early_steps = take - 1

    trial_b = trials.astype(BF16)
    mine = part(trial_b, o, own, 1)
    others = [shift(mine, "vir", nv, -r) for r in range(1, nv)]

    def over_cores(x):
        x = x.reshape(x.shape[0] // nm, CORES, half_m, *x.shape[1:])
        given = sibling(lax.dynamic_index_in_dim(x, 1 - c, 1, False), na)
        kept = lax.dynamic_index_in_dim(x, c, 1, False)
        both = jnp.where(
            c == 0,
            jnp.concatenate([kept, given], axis=-1),
            jnp.concatenate([given, kept], axis=-1),
        )
        return both.reshape(-1, *both.shape[2:])

    own_whole = over_cores(trial_b)
    own_part = part(own_whole, o, own, 1)

    sizes = [early_steps, 1] if early_steps else [1]
    sends, first = [], 0
    for size in sizes:
        sends.append(
            [
                lax.dynamic_slice_in_dim(factors, (v - r) % nv * take + first, size, 0)
                for r in range(1, nv)
            ]
        )
        first += size
    sends, others = lax.optimization_barrier((sends, others))
    come = [[shift(x, "vir", nv, -r - 1) for r, x in enumerate(group)] for group in sends]

    their = over_cores(jnp.concatenate(others, axis=0)) if others else None
    blocks = []
    for first, x in ((0, own_part), (half_m, their)):
        for t in range(nz):
            if x is None:
                continue
            if t == 0 and first == 0:
                for s in range(no):
                    blocks.append((part(own_whole, (o + s) % no, own, 1), 0, nz + s, 0))
                continue
            got = x if t == 0 else shift(x, "aux", na, t, CORES)
            blocks.append((got, first, nz, t))
            for s in range(1, no):
                blocks.append((shift(got, "outer", no, -s), first, nz + s, t))
    where = jnp.stack(
        [((z - t) % nz * block - v * width) % total for t in range(nz)]
        + [(o + s) % no * own for s in range(no)]
    ).astype(jnp.int32)
    vectors = assemble(where, blocks, groups, rows, total)

    later, _ = lax.optimization_barrier((factors, blocks[-no][0]))
    kept = lax.dynamic_slice_in_dim(later, v * take, take, 0)
    shown = sibling(kept, na)
    early = None
    if early_steps:
        got, vectors = lax.optimization_barrier((come[0], vectors))
        early = early_sums(
            [[kept] + got, [shown] + [sibling(g, na) for g in got]], early_steps, vectors
        )
    got, early = lax.optimization_barrier((come[-1], early))
    sides = [[kept] + got, [shown] + [sibling(g, na) for g in got]]
    firsts = [early_steps] + [0] * (nv - 1)
    pair_own = step_pairs(sides[0], firsts, vectors)

    out = []
    for p in last_sums(o, sides, firsts, pair_own, vectors, early, no, nv):
        send_x, keep_x, send_y, keep_y = p
        one = keep_x
        for r in range(1, nv):
            sent = send_x[(r - 1) * half_m : r * half_m]
            one += shift(sent, "vir", nv, r).astype(F32)
        u_one = lax.dynamic_index_in_dim(one, o, 1, False)
        for s in range(1, no):
            sent = lax.dynamic_index_in_dim(one, (o + s) % no, 1, False).astype(BF16)
            u_one += shift(sent, "outer", no, s).astype(F32)
        two = keep_y
        for s in range(1, no):
            two += shift(send_y[s - 1], "outer", no, s).astype(F32)
        u_two = two[:half_m]
        for r in range(1, nv):
            sent = two[r * half_m : (r + 1) * half_m].astype(BF16)
            u_two += shift(sent, "vir", nv, r).astype(F32)
        u = jnp.concatenate([u_one, u_two], axis=1)

        def to(zz):
            return lax.dynamic_slice_in_dim(u, (zz * block - v * width) % total, block, 2)

        got = to(z)
        for t in range(1, nz):
            got += shift(to((z + t) % nz).astype(BF16), "aux", na, t, CORES).astype(F32)
        out.append(got)
    done = jnp.concatenate(out, axis=1)
    there = sibling(part(done, 1 - c, cols, 2), na)
    here = part(done, c, cols, 2)
    return jnp.where(
        c == 0, jnp.concatenate([here, there], axis=0), jnp.concatenate([there, here], axis=0)
    )


def solution(mesh):
    na, nv, no = (mesh.shape[name] for name in ("aux", "vir", "outer"))

    def step(factors, trials):
        nq, rows, width = factors.shape
        nm, _, cols = trials.shape
        fits = na % CORES == 0 and nm % CORES == 0 and nq % nv == 0
        fits = fits and width % (CORES * cols) == 0 and cols % 128 == 0
        fits = fits and rows % (no * PIECES * 2 * 16) == 0
        if fits:
            return per_device(na, nv, no, factors, trials)
        return plain(factors, trials)

    placed = (P(("aux", "outer"), None, "vir"), P("vir", None, "aux"))
    return jax.shard_map(
        step, mesh=mesh, in_specs=placed, out_specs=P("vir", "outer", "aux"), check_vma=False
    )
```

```python
import jax
import jax.numpy as jnp
from jax import lax
from jax.experimental import pallas as pl
from jax.experimental.pallas import tpu as pltpu
from jax.sharding import PartitionSpec as P

CORES = 2
PIECES = 2
VMEM_LIMIT = 28 * 2**20
F32, BF16 = jnp.float32, jnp.bfloat16
VMEM = pl.BlockSpec(memory_space=pltpu.VMEM)
ANY = pl.BlockSpec(memory_space=pl.ANY)
HBM = pl.BlockSpec(memory_space=pltpu.HBM)
SMEM = pl.BlockSpec(memory_space=pltpu.SMEM)


def plain(factors, trials):
    trial_b = trials.astype(jnp.bfloat16)
    gathered = lax.all_gather(trial_b, "aux", axis=2, tiled=True)
    columns = lax.all_gather(factors, "vir", axis=2, tiled=True)
    pairs = jnp.einsum(
        "qib,mjb->mqij", columns, gathered, preferred_element_type=jnp.float32
    ).astype(jnp.bfloat16)
    stacked = jnp.einsum("mqij,qja->mia", pairs, columns, preferred_element_type=jnp.float32)
    slices = lax.psum_scatter(stacked, "aux", scatter_dimension=2, tiled=True)
    return lax.psum_scatter(slices, "outer", scatter_dimension=1, tiled=True)


def shift(array, axis, size, step, stride=1):
    count = size // stride
    pairs = [
        (i, (i // stride + step) % count * stride + i % stride) for i in range(size)
    ]
    return lax.ppermute(array, axis, pairs)


def sibling(array, size):
    return lax.ppermute(array, "aux", [(i, i ^ 1) for i in range(size)])


def part(array, index, size, axis):
    return lax.dynamic_slice_in_dim(array, index * size, size, axis)


def dot_nt(a, b):
    return lax.dot_general(a, b, (((1,), (1,)), ((), ())), preferred_element_type=F32)


def params():
    return pltpu.CompilerParams(vmem_limit_bytes=VMEM_LIMIT)


def cost(flops, *arrays):
    moved = sum(x.size * x.dtype.itemsize for x in arrays)
    return pl.CostEstimate(flops=flops, bytes_accessed=moved, transcendentals=0)


def assemble(where, blocks, groups, rows, total):
    shape = jax.ShapeDtypeStruct((groups, rows, total), BF16)

    def body(at, *refs):
        out, sems = refs[-2:]
        copies = []
        for i, (_, first, row_slot, col_slot) in enumerate(blocks):
            many, share, block = refs[i].shape
            row = pl.multiple_of(at[row_slot], share)
            col = pl.multiple_of(at[col_slot], block)
            to = out.at[pl.ds(first, many), pl.ds(row, share), pl.ds(col, block)]
            copies.append(pltpu.make_async_copy(refs[i], to, sems.at[i]))
        for copy in copies:
            copy.start()
        for copy in copies:
            copy.wait()

    return pl.pallas_call(
        body,
        out_shape=shape,
        in_specs=[SMEM] + [ANY] * len(blocks),
        out_specs=ANY,
        scratch_shapes=[pltpu.SemaphoreType.DMA((len(blocks),))],
        cost_estimate=cost(0, shape),
        compiler_params=params(),
        name="assemble",
    )(where, *[b[0] for b in blocks])


def pairs_of(refs, vec, store):
    groups, rows, _ = vec.shape
    count, _, width = refs[0].shape
    for g in range(groups):
        acc = None
        for r, ref in enumerate(refs):
            left = ref[...].reshape(count * rows, width)
            term = dot_nt(left, vec[g, :, r * width : (r + 1) * width])
            acc = term if acc is None else acc + term
        acc = acc.astype(BF16)
        for k in range(count):
            store(g, k, acc[k * rows : (k + 1) * rows])


def early_sums(sides, steps, vectors):
    groups, rows, total = vectors.shape
    nr = len(sides[0])
    width = total // nr
    slots = [pieces for side in sides for pieces in side]
    flat = [p for pieces in slots for p in pieces]
    n, ns = len(flat), len(slots)
    shape = jax.ShapeDtypeStruct((groups, rows, total), F32)
    tile = min(width, 512)
    tiles = total // tile

    def body(*refs):
        vec_in, out = refs[n : n + 2]
        vec, held, done, sems, out_sems = refs[-5:]
        ins = refs[n + 2 : n + 2 + ns]
        first = pltpu.make_async_copy(vec_in, vec, sems.at[n])
        first.start()
        copies, i = [], 0
        for slot, pieces in zip(ins, slots):
            group, at = [], 0
            for piece in pieces:
                size = min(piece.shape[0], steps)
                to = slot.at[pl.ds(at, size)]
                group.append(pltpu.make_async_copy(refs[i].at[pl.ds(0, size)], to, sems.at[i]))
                group[-1].start()
                i, at = i + 1, at + size
            copies.append(group)
        first.wait()
        for s in range(len(sides)):

            def store(g, k, pair, s=s):
                held[s, g * rows : (g + 1) * rows, k * rows : (k + 1) * rows] = pair

            for group in copies[s * nr : (s + 1) * nr]:
                for copy in group:
                    copy.wait()
            pairs_of(ins[s * nr : (s + 1) * nr], vec, store)
        sent = []
        for i in range(tiles):
            r, at = i * tile // width, i * tile % width
            acc = None
            for s in range(len(sides)):
                right = ins[s * nr + r][:, :, at : at + tile].reshape(steps * rows, tile)
                term = jnp.dot(held[s], right, preferred_element_type=F32)
                acc = term if acc is None else acc + term
            cols = pl.ds(i * tile, tile)
            done[:, :, cols] = acc.reshape(groups, rows, tile)
            sent.append(
                pltpu.make_async_copy(done.at[:, :, cols], out.at[:, :, cols], out_sems.at[i])
            )
            sent[-1].start()
        for copy in sent:
            copy.wait()

    return pl.pallas_call(
        body,
        out_shape=shape,
        in_specs=[ANY] * (n + 1),
        out_specs=ANY,
        scratch_shapes=[pltpu.VMEM((steps, rows, width), BF16)] * ns
        + [
            pltpu.VMEM(vectors.shape, BF16),
            pltpu.VMEM((len(sides), groups * rows, steps * rows), BF16),
            pltpu.VMEM(shape.shape, F32),
            pltpu.SemaphoreType.DMA((n + 1,)),
            pltpu.SemaphoreType.DMA((tiles,)),
        ],
        cost_estimate=cost(0, vectors),
        compiler_params=params(),
        name="early_sums",
    )(*flat, vectors)


def step_pairs(side, firsts, vectors):
    groups, rows, total = vectors.shape
    shape = jax.ShapeDtypeStruct((groups, rows, rows), BF16)
    n = len(side)
    width = total // n

    def body(*refs):
        vec_in, out = refs[n : n + 2]
        ins = refs[n + 2 : 2 * n + 2]
        vec, sems = refs[-2:]
        copies = [pltpu.make_async_copy(vec_in, vec, sems.at[n])] + [
            pltpu.make_async_copy(refs[i].at[pl.ds(firsts[i], 1)], ins[i], sems.at[i])
            for i in range(n)
        ]
        for copy in copies:
            copy.start()
        for copy in copies:
            copy.wait()

        def store(g, _, pair):
            out[g] = pair

        pairs_of(ins, vec, store)

    return pl.pallas_call(
        body,
        out_shape=shape,
        in_specs=[ANY] * (n + 1),
        out_specs=VMEM,
        scratch_shapes=[pltpu.VMEM((1, rows, width), BF16)] * n
        + [pltpu.VMEM(vectors.shape, BF16), pltpu.SemaphoreType.DMA((n + 1,))],
        cost_estimate=cost(0, vectors),
        compiler_params=params(),
        name="step_pairs",
    )(*side, vectors)


def last_sums(o, sides, firsts, pair_own, vectors, early, no, nv):
    groups, rows, total = vectors.shape
    nr = len(sides[0])
    width = total // nr
    flat = [p for side in sides for p in side]
    n = len(flat)
    per = groups // nv
    own = rows // no
    small = own // (PIECES * 2)
    more = [] if early is None else [early]
    tile = min(width, 512)
    tiles = total // tile

    def body(*refs):
        me = refs[0][0]
        refs = refs[1:]
        pair_in, vec_in = refs[n : n + 2]
        results = refs[n + 2 + len(more) : n + 2 + len(more) + 4 * PIECES]
        outs = refs[n + 2 + len(more) + 4 * PIECES : n + 2 + len(more) + 8 * PIECES]
        ins = refs[-n - 7 : -7]
        vec, own_pair, their_pair, before, sems, early_sems, out_sems = refs[-7:]
        copies = [
            pltpu.make_async_copy(refs[i].at[pl.ds(firsts[i % nr], 1)], ins[i], sems.at[i])
            for i in range(n)
        ]
        vec_copy = pltpu.make_async_copy(vec_in, vec, sems.at[n])
        pair_copy = pltpu.make_async_copy(pair_in, own_pair, sems.at[n + 1])
        vec_copy.start()
        for copy in copies[nr:] + copies[:nr]:
            copy.start()
        pair_copy.start()
        early_copies = []
        for i in range(tiles if more else 0):
            cols = pl.ds(i * tile, tile)
            early_copies.append(
                pltpu.make_async_copy(
                    refs[n + 2].at[:, :, cols], before.at[:, :, cols], early_sems.at[i]
                )
            )
            early_copies[-1].start()
        vec_copy.wait()
        for copy in copies[nr:]:
            copy.wait()

        def store(g, _, pair):
            their_pair[g] = pair

        pairs_of(ins[nr:], vec, store)
        for copy in copies[:nr]:
            copy.wait()
        pair_copy.wait()
        left = [p[...].reshape(groups * rows, rows) for p in (own_pair, their_pair)]
        sent = []
        for i in range(tiles):
            r, at = i * tile // width, i * tile % width
            got = None
            for s in range(len(sides)):
                right = ins[s * nr + r][0, :, at : at + tile]
                term = jnp.dot(left[s], right, preferred_element_type=F32)
                got = term if got is None else got + term
            got = got.reshape(groups, rows, tile)
            if more:
                early_copies[i].wait()
                got = got + before[:, :, i * tile : (i + 1) * tile]
            got = got.reshape(groups, no, PIECES, 2, small, tile)
            for g in range(groups):
                v = g // per
                to = (r - v) % nr * width + at
                cols = slice(to, to + tile)
                for p in range(PIECES):
                    send_x, keep_x, send_y, keep_y = outs[4 * p : 4 * p + 4]
                    for oo in range(no):
                        if v == 0:
                            keep_x[g, oo, :, cols] = got[g, oo, p, 0]
                        else:
                            send_x[g - per, oo, :, cols] = got[g, oo, p, 0].astype(BF16)
            for s in range(no):
                for oo in range(no):

                    @pl.when(lax.rem(me + s, no) == oo)
                    def _(s=s, oo=oo, got=got, r=r, at=at):
                        for g in range(groups):
                            to = (r - g // per) % nr * width + at
                            cols = slice(to, to + tile)
                            for p in range(PIECES):
                                if s == 0:
                                    outs[4 * p + 3][g, :, cols] = got[g, oo, p, 1]
                                else:
                                    outs[4 * p + 2][s - 1, g, :, cols] = got[g, oo, p, 1].astype(BF16)
            for v in range(nv):
                cols = pl.ds((r - v) % nr * width + at, tile)
                for p in range(PIECES):
                    at_x = (pl.ds(0, per) if v == 0 else pl.ds((v - 1) * per, per), slice(None), slice(None), cols)
                    at_y = (pl.ds(v * per, per), slice(None), cols)
                    for k, where in (
                        (1 if v == 0 else 0, at_x),
                        (2, (slice(None), *at_y)),
                        (3, at_y),
                    ):
                        out, result = outs[4 * p + k], results[4 * p + k]
                        sent.append(
                            pltpu.make_async_copy(
                                out.at[where], result.at[where], out_sems.at[len(sent)]
                            )
                        )
                        sent[-1].start()
        for copy in sent:
            copy.wait()

    shapes = [
        jax.ShapeDtypeStruct((groups - per, no, small, total), BF16),
        jax.ShapeDtypeStruct((per, no, small, total), F32),
        jax.ShapeDtypeStruct((no - 1, groups, small, total), BF16),
        jax.ShapeDtypeStruct((groups, small, total), F32),
    ] * PIECES
    outs = pl.pallas_call(
        body,
        out_shape=shapes,
        in_specs=[SMEM] + [ANY] * (n + 2 + len(more)),
        out_specs=[HBM] * len(shapes),
        scratch_shapes=[pltpu.VMEM(x.shape, x.dtype) for x in shapes]
        + [pltpu.VMEM((1, rows, width), BF16)] * n
        + [
            pltpu.VMEM(vectors.shape, BF16),
            pltpu.VMEM((groups, rows, rows), BF16),
            pltpu.VMEM((groups, rows, rows), BF16),
            pltpu.VMEM(vectors.shape if more else (8, 128), F32),
            pltpu.SemaphoreType.DMA((n + 2,)),
            pltpu.SemaphoreType.DMA((tiles,)),
            pltpu.SemaphoreType.DMA((tiles * nv * PIECES * 3,)),
        ],
        cost_estimate=cost(0, *shapes),
        compiler_params=params(),
        name="last_sums",
    )(o.reshape(1), *flat, pair_own, vectors, *more)
    return [outs[4 * p : 4 * p + 4] for p in range(PIECES)]


def per_device(na, nv, no, factors, trials):
    nq, rows, width = factors.shape
    nm, _, cols = trials.shape
    nz = na // CORES
    a, v, o = (lax.axis_index(name) for name in ("aux", "vir", "outer"))
    z, c = a // CORES, a % CORES
    half_m, take = nm // CORES, nq // nv
    block, total = CORES * cols, nv * width
    own = rows // no
    groups = nv * half_m
    early_steps = take - 1

    mine = part(trials, o, own, 1).astype(BF16)
    others = [shift(mine, "vir", nv, -r) for r in range(1, nv)]

    def sends(source, first, size):
        return [
            lax.dynamic_slice_in_dim(source, (v - r) % nv * take + first, size, 0)
            for r in range(1, nv)
        ]

    def along_vir(group):
        return [shift(x, "vir", nv, -r - 1) for r, x in enumerate(group)]

    come = None
    if early_steps:
        group, others = lax.optimization_barrier((sends(factors, 0, early_steps), others))
        come = along_vir(group)

    both = jnp.concatenate([mine] + others, axis=0).reshape(nv, CORES, half_m, own, cols)
    given = sibling(lax.dynamic_index_in_dim(both, 1 - c, 1, False), na)
    kept = lax.dynamic_index_in_dim(both, c, 1, False)
    whole = jnp.where(
        c == 0,
        jnp.concatenate([kept, given], axis=-1),
        jnp.concatenate([given, kept], axis=-1),
    ).reshape(groups, own, block)
    later, whole = lax.optimization_barrier((factors, whole))
    come_last = along_vir(sends(later, early_steps, 1))

    blocks = []
    for t in range(nz):
        got = whole if t == 0 else shift(whole, "aux", na, t, CORES)
        blocks.append((got, 0, nz, t))
        for s in range(1, no):
            blocks.append((shift(got, "outer", no, -s), 0, nz + s, t))
    where = jnp.stack(
        [((z - t) % nz * block - v * width) % total for t in range(nz)]
        + [(o + s) % no * own for s in range(no)]
    ).astype(jnp.int32)
    vectors = assemble(where, blocks, groups, rows, total)

    later, _ = lax.optimization_barrier((factors, blocks[no][0]))
    kept = lax.dynamic_slice_in_dim(later, v * take, take, 0)
    shown = sibling(kept, na)
    early = None
    if early_steps:
        got, vectors = lax.optimization_barrier((come, vectors))
        their = [[sibling(g[k : k + 1], na) for k in range(early_steps)] for g in got]
        early = early_sums(
            [[[kept]] + [[g] for g in got], [[shown]] + their], early_steps, vectors
        )
    got, early = lax.optimization_barrier((come_last, early))
    sides = [[kept] + got, [shown] + [sibling(g, na) for g in got]]
    firsts = [early_steps] + [0] * (nv - 1)
    pair_own = step_pairs(sides[0], firsts, vectors)

    out = []
    for p in last_sums(o, sides, firsts, pair_own, vectors, early, no, nv):
        send_x, keep_x, send_y, keep_y = p
        one = keep_x
        for r in range(1, nv):
            sent = send_x[(r - 1) * half_m : r * half_m]
            one += shift(sent, "vir", nv, r).astype(F32)
        u_one = lax.dynamic_index_in_dim(one, o, 1, False)
        for s in range(1, no):
            sent = lax.dynamic_index_in_dim(one, (o + s) % no, 1, False).astype(BF16)
            u_one += shift(sent, "outer", no, s).astype(F32)
        two = keep_y
        for s in range(1, no):
            two += shift(send_y[s - 1], "outer", no, s).astype(F32)
        u_two = two[:half_m]
        for r in range(1, nv):
            sent = two[r * half_m : (r + 1) * half_m].astype(BF16)
            u_two += shift(sent, "vir", nv, r).astype(F32)
        u = jnp.concatenate([u_one, u_two], axis=1)

        def to(zz):
            return lax.dynamic_slice_in_dim(u, (zz * block - v * width) % total, block, 2)

        got = to(z)
        for t in range(1, nz):
            got += shift(to((z + t) % nz).astype(BF16), "aux", na, t, CORES).astype(F32)
        out.append(got)
    done = jnp.concatenate(out, axis=1)
    there = sibling(part(done, 1 - c, cols, 2), na)
    here = part(done, c, cols, 2)
    return jnp.where(
        c == 0, jnp.concatenate([here, there], axis=0), jnp.concatenate([there, here], axis=0)
    )


def solution(mesh):
    na, nv, no = (mesh.shape[name] for name in ("aux", "vir", "outer"))

    def step(factors, trials):
        nq, rows, width = factors.shape
        nm, _, cols = trials.shape
        fits = na % CORES == 0 and nm % CORES == 0 and nq % nv == 0
        fits = fits and width % (CORES * cols) == 0 and cols % 128 == 0
        fits = fits and rows % (no * PIECES * 2 * 16) == 0
        if fits:
            return per_device(na, nv, no, factors, trials)
        return plain(factors, trials)

    placed = (P(("aux", "outer"), None, "vir"), P("vir", None, "aux"))
    return jax.shard_map(
        step, mesh=mesh, in_specs=placed, out_specs=P("vir", "outer", "aux"), check_vma=False
    )
```

```python
import jax
import jax.numpy as jnp
from jax import lax
from jax.experimental import pallas as pl
from jax.experimental.pallas import tpu as pltpu
from jax.sharding import PartitionSpec as P

CORES = 2
PIECES = 2
VMEM_LIMIT = 28 * 2**20
F32, BF16 = jnp.float32, jnp.bfloat16
VMEM = pl.BlockSpec(memory_space=pltpu.VMEM)
ANY = pl.BlockSpec(memory_space=pl.ANY)
HBM = pl.BlockSpec(memory_space=pltpu.HBM)
SMEM = pl.BlockSpec(memory_space=pltpu.SMEM)


def plain(factors, trials):
    trial_b = trials.astype(jnp.bfloat16)
    gathered = lax.all_gather(trial_b, "aux", axis=2, tiled=True)
    columns = lax.all_gather(factors, "vir", axis=2, tiled=True)
    pairs = jnp.einsum(
        "qib,mjb->mqij", columns, gathered, preferred_element_type=jnp.float32
    ).astype(jnp.bfloat16)
    stacked = jnp.einsum("mqij,qja->mia", pairs, columns, preferred_element_type=jnp.float32)
    slices = lax.psum_scatter(stacked, "aux", scatter_dimension=2, tiled=True)
    return lax.psum_scatter(slices, "outer", scatter_dimension=1, tiled=True)


def shift(array, axis, size, step, stride=1):
    count = size // stride
    pairs = [
        (i, (i // stride + step) % count * stride + i % stride) for i in range(size)
    ]
    return lax.ppermute(array, axis, pairs)


def sibling(array, size):
    return lax.ppermute(array, "aux", [(i, i ^ 1) for i in range(size)])


def part(array, index, size, axis):
    return lax.dynamic_slice_in_dim(array, index * size, size, axis)


def dot_nt(a, b):
    return lax.dot_general(a, b, (((1,), (1,)), ((), ())), preferred_element_type=F32)


def params():
    return pltpu.CompilerParams(vmem_limit_bytes=VMEM_LIMIT)


def in_hbm(x):
    return pltpu.with_memory_space_constraint(x, pltpu.HBM)


def cost(flops, *arrays):
    moved = sum(x.size * x.dtype.itemsize for x in arrays)
    return pl.CostEstimate(flops=flops, bytes_accessed=moved, transcendentals=0)


def assemble(where, blocks, groups, rows, total):
    shape = jax.ShapeDtypeStruct((groups, rows, total), BF16)

    def body(at, *refs):
        out, sems = refs[-2:]
        copies = []
        for i, (_, first, row_slot, col_slot) in enumerate(blocks):
            many, share, block = refs[i].shape
            row = pl.multiple_of(at[row_slot], share)
            col = pl.multiple_of(at[col_slot], block)
            to = out.at[pl.ds(first, many), pl.ds(row, share), pl.ds(col, block)]
            copies.append(pltpu.make_async_copy(refs[i], to, sems.at[i]))
        for copy in copies:
            copy.start()
        for copy in copies:
            copy.wait()

    return pl.pallas_call(
        body,
        out_shape=shape,
        in_specs=[SMEM] + [ANY] * len(blocks),
        out_specs=ANY,
        scratch_shapes=[pltpu.SemaphoreType.DMA((len(blocks),))],
        cost_estimate=cost(0, shape),
        compiler_params=params(),
        name="assemble",
    )(where, *[in_hbm(b[0]) for b in blocks])


def pairs_of(refs, vec, store):
    groups, rows, _ = vec.shape
    count, _, width = refs[0].shape
    for g in range(groups):
        acc = None
        for r, ref in enumerate(refs):
            left = ref[...].reshape(count * rows, width)
            term = dot_nt(left, vec[g, :, r * width : (r + 1) * width])
            acc = term if acc is None else acc + term
        acc = acc.astype(BF16)
        for k in range(count):
            store(g, k, acc[k * rows : (k + 1) * rows])


def early_sums(sides, steps, vectors):
    groups, rows, total = vectors.shape
    nr = len(sides[0])
    width = total // nr
    slots = [pieces for side in sides for pieces in side]
    flat = [p for pieces in slots for p in pieces]
    n, ns = len(flat), len(slots)
    shape = jax.ShapeDtypeStruct((groups, rows, total), F32)
    tile = min(width, 512)
    tiles = total // tile

    def body(*refs):
        vec_in, out = refs[n : n + 2]
        vec, held, done, sems, out_sems = refs[-5:]
        ins = refs[n + 2 : n + 2 + ns]
        first = pltpu.make_async_copy(vec_in, vec, sems.at[n])
        first.start()
        copies, i = [], 0
        for slot, pieces in zip(ins, slots):
            group, at = [], 0
            for piece in pieces:
                size = min(piece.shape[0], steps)
                to = slot.at[pl.ds(at, size)]
                group.append(pltpu.make_async_copy(refs[i].at[pl.ds(0, size)], to, sems.at[i]))
                group[-1].start()
                i, at = i + 1, at + size
            copies.append(group)
        first.wait()
        for s in range(len(sides)):

            def store(g, k, pair, s=s):
                held[s, g * rows : (g + 1) * rows, k * rows : (k + 1) * rows] = pair

            for group in copies[s * nr : (s + 1) * nr]:
                for copy in group:
                    copy.wait()
            pairs_of(ins[s * nr : (s + 1) * nr], vec, store)
        sent = []
        for i in range(tiles):
            r, at = i * tile // width, i * tile % width
            acc = None
            for s in range(len(sides)):
                right = ins[s * nr + r][:, :, at : at + tile].reshape(steps * rows, tile)
                term = jnp.dot(held[s], right, preferred_element_type=F32)
                acc = term if acc is None else acc + term
            cols = pl.ds(i * tile, tile)
            done[:, :, cols] = acc.reshape(groups, rows, tile)
            sent.append(
                pltpu.make_async_copy(done.at[:, :, cols], out.at[:, :, cols], out_sems.at[i])
            )
            sent[-1].start()
        for copy in sent:
            copy.wait()

    return pl.pallas_call(
        body,
        out_shape=shape,
        in_specs=[ANY] * (n + 1),
        out_specs=ANY,
        scratch_shapes=[pltpu.VMEM((steps, rows, width), BF16)] * ns
        + [
            pltpu.VMEM(vectors.shape, BF16),
            pltpu.VMEM((len(sides), groups * rows, steps * rows), BF16),
            pltpu.VMEM(shape.shape, F32),
            pltpu.SemaphoreType.DMA((n + 1,)),
            pltpu.SemaphoreType.DMA((tiles,)),
        ],
        cost_estimate=cost(0, vectors),
        compiler_params=params(),
        name="early_sums",
    )(*flat, vectors)


def step_pairs(side, firsts, vectors):
    groups, rows, total = vectors.shape
    shape = jax.ShapeDtypeStruct((groups, rows, rows), BF16)
    n = len(side)
    width = total // n

    def body(*refs):
        vec_in, out = refs[n : n + 2]
        ins = refs[n + 2 : 2 * n + 2]
        vec, sems = refs[-2:]
        copies = [pltpu.make_async_copy(vec_in, vec, sems.at[n])] + [
            pltpu.make_async_copy(refs[i].at[pl.ds(firsts[i], 1)], ins[i], sems.at[i])
            for i in range(n)
        ]
        for copy in copies:
            copy.start()
        for copy in copies:
            copy.wait()

        def store(g, _, pair):
            out[g] = pair

        pairs_of(ins, vec, store)

    return pl.pallas_call(
        body,
        out_shape=shape,
        in_specs=[ANY] * (n + 1),
        out_specs=VMEM,
        scratch_shapes=[pltpu.VMEM((1, rows, width), BF16)] * n
        + [pltpu.VMEM(vectors.shape, BF16), pltpu.SemaphoreType.DMA((n + 1,))],
        cost_estimate=cost(0, vectors),
        compiler_params=params(),
        name="step_pairs",
    )(*side, vectors)


def last_sums(o, sides, firsts, pair_own, vectors, early, no, nv):
    groups, rows, total = vectors.shape
    nr = len(sides[0])
    width = total // nr
    flat = [p for side in sides for p in side]
    n = len(flat)
    per = groups // nv
    own = rows // no
    small = own // (PIECES * 2)
    more = [] if early is None else [early]
    tile = min(width, 512)
    tiles = total // tile

    def body(*refs):
        me = refs[0][0]
        refs = refs[1:]
        pair_in, vec_in = refs[n : n + 2]
        results = refs[n + 2 + len(more) : n + 2 + len(more) + 4 * PIECES]
        outs = refs[n + 2 + len(more) + 4 * PIECES : n + 2 + len(more) + 8 * PIECES]
        ins = refs[-n - 7 : -7]
        vec, own_pair, their_pair, before, sems, early_sems, out_sems = refs[-7:]
        copies = [
            pltpu.make_async_copy(refs[i].at[pl.ds(firsts[i % nr], 1)], ins[i], sems.at[i])
            for i in range(n)
        ]
        vec_copy = pltpu.make_async_copy(vec_in, vec, sems.at[n])
        pair_copy = pltpu.make_async_copy(pair_in, own_pair, sems.at[n + 1])
        vec_copy.start()
        for copy in copies[nr:] + copies[:nr]:
            copy.start()
        pair_copy.start()
        early_copies = []
        for i in range(tiles if more else 0):
            cols = pl.ds(i * tile, tile)
            early_copies.append(
                pltpu.make_async_copy(
                    refs[n + 2].at[:, :, cols], before.at[:, :, cols], early_sems.at[i]
                )
            )
            early_copies[-1].start()
        vec_copy.wait()
        for copy in copies[nr:]:
            copy.wait()

        def store(g, _, pair):
            their_pair[g] = pair

        pairs_of(ins[nr:], vec, store)
        for copy in copies[:nr]:
            copy.wait()
        pair_copy.wait()
        left = [p[...].reshape(groups * rows, rows) for p in (own_pair, their_pair)]
        sent = []
        for i in range(tiles):
            r, at = i * tile // width, i * tile % width
            got = None
            for s in range(len(sides)):
                right = ins[s * nr + r][0, :, at : at + tile]
                term = jnp.dot(left[s], right, preferred_element_type=F32)
                got = term if got is None else got + term
            got = got.reshape(groups, rows, tile)
            if more:
                early_copies[i].wait()
                got = got + before[:, :, i * tile : (i + 1) * tile]
            got = got.reshape(groups, no, PIECES, 2, small, tile)
            for g in range(groups):
                v = g // per
                to = (r - v) % nr * width + at
                cols = slice(to, to + tile)
                for p in range(PIECES):
                    send_x, keep_x, send_y, keep_y = outs[4 * p : 4 * p + 4]
                    for oo in range(no):
                        if v == 0:
                            keep_x[g, oo, :, cols] = got[g, oo, p, 0]
                        else:
                            send_x[g - per, oo, :, cols] = got[g, oo, p, 0].astype(BF16)
            for s in range(no):
                for oo in range(no):

                    @pl.when(lax.rem(me + s, no) == oo)
                    def _(s=s, oo=oo, got=got, r=r, at=at):
                        for g in range(groups):
                            to = (r - g // per) % nr * width + at
                            cols = slice(to, to + tile)
                            for p in range(PIECES):
                                if s == 0:
                                    outs[4 * p + 3][g, :, cols] = got[g, oo, p, 1]
                                else:
                                    outs[4 * p + 2][s - 1, g, :, cols] = got[g, oo, p, 1].astype(BF16)
            for v in range(nv):
                cols = pl.ds((r - v) % nr * width + at, tile)
                for p in range(PIECES):
                    at_x = (pl.ds(0, per) if v == 0 else pl.ds((v - 1) * per, per), slice(None), slice(None), cols)
                    at_y = (pl.ds(v * per, per), slice(None), cols)
                    for k, where in (
                        (1 if v == 0 else 0, at_x),
                        (2, (slice(None), *at_y)),
                        (3, at_y),
                    ):
                        out, result = outs[4 * p + k], results[4 * p + k]
                        sent.append(
                            pltpu.make_async_copy(
                                out.at[where], result.at[where], out_sems.at[len(sent)]
                            )
                        )
                        sent[-1].start()
        for copy in sent:
            copy.wait()

    shapes = [
        jax.ShapeDtypeStruct((groups - per, no, small, total), BF16),
        jax.ShapeDtypeStruct((per, no, small, total), F32),
        jax.ShapeDtypeStruct((no - 1, groups, small, total), BF16),
        jax.ShapeDtypeStruct((groups, small, total), F32),
    ] * PIECES
    outs = pl.pallas_call(
        body,
        out_shape=[pltpu.HBM(x.shape, x.dtype) for x in shapes],
        in_specs=[SMEM] + [ANY] * (n + 2 + len(more)),
        out_specs=[HBM] * len(shapes),
        scratch_shapes=[pltpu.VMEM(x.shape, x.dtype) for x in shapes]
        + [pltpu.VMEM((1, rows, width), BF16)] * n
        + [
            pltpu.VMEM(vectors.shape, BF16),
            pltpu.VMEM((groups, rows, rows), BF16),
            pltpu.VMEM((groups, rows, rows), BF16),
            pltpu.VMEM(vectors.shape if more else (8, 128), F32),
            pltpu.SemaphoreType.DMA((n + 2,)),
            pltpu.SemaphoreType.DMA((tiles,)),
            pltpu.SemaphoreType.DMA((tiles * nv * PIECES * 3,)),
        ],
        cost_estimate=cost(0, *shapes),
        compiler_params=params(),
        name="last_sums",
    )(o.reshape(1), *flat, pair_own, vectors, *more)
    return [outs[4 * p : 4 * p + 4] for p in range(PIECES)]


def per_device(na, nv, no, factors, trials):
    nq, rows, width = factors.shape
    nm, _, cols = trials.shape
    nz = na // CORES
    a, v, o = (lax.axis_index(name) for name in ("aux", "vir", "outer"))
    z, c = a // CORES, a % CORES
    half_m, take = nm // CORES, nq // nv
    block, total = CORES * cols, nv * width
    own = rows // no
    groups = nv * half_m
    early_steps = take - 1
    last_steps = take - early_steps

    mine = part(trials, o, own, 1).astype(BF16)
    others = [shift(mine, "vir", nv, -r) for r in range(1, nv)]

    def sends(source, first, size):
        return [
            lax.dynamic_slice_in_dim(source, (v - r) % nv * take + first, size, 0)
            for r in range(1, nv)
        ]

    def along_vir(group):
        return [shift(x, "vir", nv, -r - 1) for r, x in enumerate(group)]

    come = None
    if early_steps:
        group, others = lax.optimization_barrier((sends(factors, 0, early_steps), others))
        come = along_vir(group)

    both = jnp.concatenate([mine] + others, axis=0).reshape(nv, CORES, half_m, own, cols)
    given = sibling(lax.dynamic_index_in_dim(both, 1 - c, 1, False), na)
    kept = lax.dynamic_index_in_dim(both, c, 1, False)
    whole = jnp.where(
        c == 0,
        jnp.concatenate([kept, given], axis=-1),
        jnp.concatenate([given, kept], axis=-1),
    ).reshape(groups, own, block)
    later, whole = lax.optimization_barrier((factors, whole))

    steps = [whole] + [shift(whole, "aux", na, t, CORES) for t in range(1, nz)]
    blocks = []
    for t, got in enumerate(steps):
        blocks.append((got, 0, nz, t))
        for s in range(1, no):
            blocks.append((shift(got, "outer", no, -s), 0, nz + s, t))
    where = jnp.stack(
        [((z - t) % nz * block - v * width) % total for t in range(nz)]
        + [(o + s) % no * own for s in range(no)]
    ).astype(jnp.int32)
    later, _ = lax.optimization_barrier((factors, blocks[no - 1][0]))
    held = (come, sends(later, early_steps, last_steps), [b[0] for b in blocks])
    come, group, arrays = lax.optimization_barrier(held)
    come_last = along_vir(group)
    blocks = [(x, *b[1:]) for x, b in zip(arrays, blocks)]
    vectors = assemble(where, blocks, groups, rows, total)

    kept = lax.dynamic_slice_in_dim(later, v * take, take, 0)
    shown = sibling(kept, na)
    early = None
    if early_steps:
        got = come
        their = [[sibling(g, na)] for g in got]
        early = early_sums(
            [[[kept]] + [[g] for g in got], [[shown]] + their], early_steps, vectors
        )
    got, early = lax.optimization_barrier((come_last, early))
    sides = [[kept] + got, [shown] + [sibling(g, na) for g in got]]
    firsts = [early_steps] + [0] * (nv - 1)
    pair_own = step_pairs(sides[0], firsts, vectors)

    out = []
    for p in last_sums(o, sides, firsts, pair_own, vectors, early, no, nv):
        send_x, keep_x, send_y, keep_y = p
        one = keep_x
        for r in range(1, nv):
            sent = send_x[(r - 1) * half_m : r * half_m]
            one += shift(sent, "vir", nv, r).astype(F32)
        u_one = lax.dynamic_index_in_dim(one, o, 1, False)
        for s in range(1, no):
            sent = lax.dynamic_index_in_dim(one, (o + s) % no, 1, False).astype(BF16)
            u_one += shift(sent, "outer", no, s).astype(F32)
        two = keep_y
        for s in range(1, no):
            two += shift(send_y[s - 1], "outer", no, s).astype(F32)
        u_two = two[:half_m]
        for r in range(1, nv):
            sent = two[r * half_m : (r + 1) * half_m].astype(BF16)
            u_two += shift(sent, "vir", nv, r).astype(F32)
        u = jnp.concatenate([u_one, u_two], axis=1)

        def to(zz):
            return lax.dynamic_slice_in_dim(u, (zz * block - v * width) % total, block, 2)

        got = to(z)
        for t in range(1, nz):
            got += shift(to((z + t) % nz).astype(BF16), "aux", na, t, CORES).astype(F32)
        out.append(got)
    done = jnp.concatenate(out, axis=1)
    there = sibling(part(done, 1 - c, cols, 2), na)
    here = part(done, c, cols, 2)
    return jnp.where(
        c == 0, jnp.concatenate([here, there], axis=0), jnp.concatenate([there, here], axis=0)
    )


def solution(mesh):
    na, nv, no = (mesh.shape[name] for name in ("aux", "vir", "outer"))

    def step(factors, trials):
        nq, rows, width = factors.shape
        nm, _, cols = trials.shape
        fits = na % CORES == 0 and nm % CORES == 0 and nq % nv == 0
        fits = fits and width % (CORES * cols) == 0 and cols % 128 == 0
        fits = fits and rows % (no * PIECES * 2 * 16) == 0
        if fits:
            return per_device(na, nv, no, factors, trials)
        return plain(factors, trials)

    placed = (P(("aux", "outer"), None, "vir"), P("vir", None, "aux"))
    return jax.shard_map(
        step, mesh=mesh, in_specs=placed, out_specs=P("vir", "outer", "aux"), check_vma=False
    )
```

```python
import jax
import jax.numpy as jnp
from jax import lax
from jax.experimental import pallas as pl
from jax.experimental.pallas import tpu as pltpu
from jax.sharding import PartitionSpec as P

CORES = 2
PIECES = 2
VMEM_LIMIT = 20 * 2**20
F32, BF16 = jnp.float32, jnp.bfloat16
VMEM = pl.BlockSpec(memory_space=pltpu.VMEM)
ANY = pl.BlockSpec(memory_space=pl.ANY)
HBM = pl.BlockSpec(memory_space=pltpu.HBM)
SMEM = pl.BlockSpec(memory_space=pltpu.SMEM)


def plain(factors, trials):
    trial_b = trials.astype(jnp.bfloat16)
    gathered = lax.all_gather(trial_b, "aux", axis=2, tiled=True)
    columns = lax.all_gather(factors, "vir", axis=2, tiled=True)
    pairs = jnp.einsum(
        "qib,mjb->mqij", columns, gathered, preferred_element_type=jnp.float32
    ).astype(jnp.bfloat16)
    stacked = jnp.einsum("mqij,qja->mia", pairs, columns, preferred_element_type=jnp.float32)
    slices = lax.psum_scatter(stacked, "aux", scatter_dimension=2, tiled=True)
    return lax.psum_scatter(slices, "outer", scatter_dimension=1, tiled=True)


def shift(array, axis, size, step, stride=1):
    count = size // stride
    pairs = [
        (i, (i // stride + step) % count * stride + i % stride) for i in range(size)
    ]
    return lax.ppermute(array, axis, pairs)


def sibling(array, size):
    return lax.ppermute(array, "aux", [(i, i ^ 1) for i in range(size)])


def part(array, index, size, axis):
    return lax.dynamic_slice_in_dim(array, index * size, size, axis)


def dot_nt(a, b):
    return lax.dot_general(a, b, (((1,), (1,)), ((), ())), preferred_element_type=F32)


def params():
    return pltpu.CompilerParams(vmem_limit_bytes=VMEM_LIMIT)


def in_hbm(x):
    return pltpu.with_memory_space_constraint(x, pltpu.HBM)


def cost(flops, *arrays):
    moved = sum(x.size * x.dtype.itemsize for x in arrays)
    return pl.CostEstimate(flops=flops, bytes_accessed=moved, transcendentals=0)


def assemble(where, blocks, groups, rows, total):
    shape = jax.ShapeDtypeStruct((groups, rows, total), BF16)

    def body(at, *refs):
        out, sems = refs[-2:]
        copies = []
        for i, (_, first, row_slot, col_slot) in enumerate(blocks):
            many, share, block = refs[i].shape
            row = pl.multiple_of(at[row_slot], share)
            col = pl.multiple_of(at[col_slot], block)
            to = out.at[pl.ds(first, many), pl.ds(row, share), pl.ds(col, block)]
            copies.append(pltpu.make_async_copy(refs[i], to, sems.at[i]))
        for copy in copies:
            copy.start()
        for copy in copies:
            copy.wait()

    return pl.pallas_call(
        body,
        out_shape=shape,
        in_specs=[SMEM] + [ANY] * len(blocks),
        out_specs=ANY,
        scratch_shapes=[pltpu.SemaphoreType.DMA((len(blocks),))],
        cost_estimate=cost(0, shape),
        compiler_params=params(),
        name="assemble",
    )(where, *[in_hbm(b[0]) for b in blocks])


def pairs_of(refs, vec, store):
    groups, rows, _ = vec.shape
    count, _, width = refs[0].shape
    for g in range(groups):
        acc = None
        for r, ref in enumerate(refs):
            left = ref[...].reshape(count * rows, width)
            term = dot_nt(left, vec[g, :, r * width : (r + 1) * width])
            acc = term if acc is None else acc + term
        acc = acc.astype(BF16)
        for k in range(count):
            store(g, k, acc[k * rows : (k + 1) * rows])


def early_sums(sides, steps, vectors):
    groups, rows, total = vectors.shape
    nr = len(sides[0])
    width = total // nr
    slots = [pieces for side in sides for pieces in side]
    flat = [p for pieces in slots for p in pieces]
    n, ns = len(flat), len(slots)
    shape = jax.ShapeDtypeStruct((groups, rows, total), F32)
    tile = min(width, 512)
    tiles = total // tile

    def body(*refs):
        vec, out = refs[n : n + 2]
        held, sems = refs[-2:]
        ins = refs[n + 2 : n + 2 + ns]
        copies, i = [], 0
        for slot, pieces in zip(ins, slots):
            group, at = [], 0
            for piece in pieces:
                size = min(piece.shape[0], steps)
                to = slot.at[pl.ds(at, size)]
                group.append(pltpu.make_async_copy(refs[i].at[pl.ds(0, size)], to, sems.at[i]))
                group[-1].start()
                i, at = i + 1, at + size
            copies.append(group)
        for s in range(len(sides)):

            def store(g, k, pair, s=s):
                held[s, g * rows : (g + 1) * rows, k * rows : (k + 1) * rows] = pair

            for group in copies[s * nr : (s + 1) * nr]:
                for copy in group:
                    copy.wait()
            pairs_of(ins[s * nr : (s + 1) * nr], vec, store)
        for i in range(tiles):
            r, at = i * tile // width, i * tile % width
            acc = None
            for s in range(len(sides)):
                right = ins[s * nr + r][:, :, at : at + tile].reshape(steps * rows, tile)
                term = jnp.dot(held[s], right, preferred_element_type=F32)
                acc = term if acc is None else acc + term
            out[:, :, i * tile : (i + 1) * tile] = acc.reshape(groups, rows, tile)

    return pl.pallas_call(
        body,
        out_shape=shape,
        in_specs=[ANY] * n + [VMEM],
        out_specs=VMEM,
        scratch_shapes=[pltpu.VMEM((steps, rows, width), BF16)] * ns
        + [
            pltpu.VMEM((len(sides), groups * rows, steps * rows), BF16),
            pltpu.SemaphoreType.DMA((n,)),
        ],
        cost_estimate=cost(0, vectors),
        compiler_params=params(),
        name="early_sums",
    )(*flat, vectors)


def step_pairs(side, firsts, vectors):
    groups, rows, total = vectors.shape
    shape = jax.ShapeDtypeStruct((groups, rows, rows), BF16)
    n = len(side)
    width = total // n

    def body(*refs):
        vec, out = refs[n : n + 2]
        ins = refs[n + 2 : 2 * n + 2]
        sems = refs[-1]
        copies = [
            pltpu.make_async_copy(refs[i].at[pl.ds(firsts[i], 1)], ins[i], sems.at[i])
            for i in range(n)
        ]
        for copy in copies:
            copy.start()
        for copy in copies:
            copy.wait()

        def store(g, _, pair):
            out[g] = pair

        pairs_of(ins, vec, store)

    return pl.pallas_call(
        body,
        out_shape=shape,
        in_specs=[ANY] * n + [VMEM],
        out_specs=VMEM,
        scratch_shapes=[pltpu.VMEM((1, rows, width), BF16)] * n
        + [pltpu.SemaphoreType.DMA((n,))],
        cost_estimate=cost(0, vectors),
        compiler_params=params(),
        name="step_pairs",
    )(*side, vectors)


def last_sums(o, sides, firsts, pair_own, vectors, early, no, nv):
    groups, rows, total = vectors.shape
    nr = len(sides[0])
    width = total // nr
    flat = [p for side in sides for p in side]
    n = len(flat)
    per = groups // nv
    own = rows // no
    small = own // (PIECES * 2)
    more = [] if early is None else [early]
    tile = min(width, 512)
    tiles = total // tile

    def body(*refs):
        me = refs[0][0]
        refs = refs[1:]
        own_pair, vec = refs[n : n + 2]
        before = refs[n + 2] if more else None
        results = refs[n + 2 + len(more) : n + 2 + len(more) + 4 * PIECES]
        outs = refs[n + 2 + len(more) + 4 * PIECES : n + 2 + len(more) + 8 * PIECES]
        ins = refs[-n - 3 : -3]
        their_pair, sems, out_sems = refs[-3:]
        copies = [
            pltpu.make_async_copy(refs[i].at[pl.ds(firsts[i % nr], 1)], ins[i], sems.at[i])
            for i in range(n)
        ]
        for copy in copies[nr:] + copies[:nr]:
            copy.start()
        for copy in copies[nr:]:
            copy.wait()

        def store(g, _, pair):
            their_pair[g] = pair

        pairs_of(ins[nr:], vec, store)
        for copy in copies[:nr]:
            copy.wait()
        left = [p[...].reshape(groups * rows, rows) for p in (own_pair, their_pair)]
        sent = []
        for i in range(tiles):
            r, at = i * tile // width, i * tile % width
            got = None
            for s in range(len(sides)):
                right = ins[s * nr + r][0, :, at : at + tile]
                term = jnp.dot(left[s], right, preferred_element_type=F32)
                got = term if got is None else got + term
            got = got.reshape(groups, rows, tile)
            if more:
                got = got + before[:, :, i * tile : (i + 1) * tile]
            got = got.reshape(groups, no, PIECES, 2, small, tile)
            for g in range(groups):
                v = g // per
                to = (r - v) % nr * width + at
                cols = slice(to, to + tile)
                for p in range(PIECES):
                    send_x, keep_x, send_y, keep_y = outs[4 * p : 4 * p + 4]
                    for oo in range(no):
                        if v == 0:
                            keep_x[g, oo, :, cols] = got[g, oo, p, 0]
                        else:
                            send_x[g - per, oo, :, cols] = got[g, oo, p, 0].astype(BF16)
            for s in range(no):
                for oo in range(no):

                    @pl.when(lax.rem(me + s, no) == oo)
                    def _(s=s, oo=oo, got=got, r=r, at=at):
                        for g in range(groups):
                            to = (r - g // per) % nr * width + at
                            cols = slice(to, to + tile)
                            for p in range(PIECES):
                                if s == 0:
                                    outs[4 * p + 3][g, :, cols] = got[g, oo, p, 1]
                                else:
                                    outs[4 * p + 2][s - 1, g, :, cols] = got[g, oo, p, 1].astype(BF16)
            for v in range(nv):
                cols = pl.ds((r - v) % nr * width + at, tile)
                for p in range(PIECES):
                    at_x = (pl.ds(0, per) if v == 0 else pl.ds((v - 1) * per, per), slice(None), slice(None), cols)
                    at_y = (pl.ds(v * per, per), slice(None), cols)
                    for k, where in (
                        (1 if v == 0 else 0, at_x),
                        (2, (slice(None), *at_y)),
                        (3, at_y),
                    ):
                        out, result = outs[4 * p + k], results[4 * p + k]
                        sent.append(
                            pltpu.make_async_copy(
                                out.at[where], result.at[where], out_sems.at[len(sent)]
                            )
                        )
                        sent[-1].start()
        for copy in sent:
            copy.wait()

    shapes = [
        jax.ShapeDtypeStruct((groups - per, no, small, total), BF16),
        jax.ShapeDtypeStruct((per, no, small, total), F32),
        jax.ShapeDtypeStruct((no - 1, groups, small, total), BF16),
        jax.ShapeDtypeStruct((groups, small, total), F32),
    ] * PIECES
    outs = pl.pallas_call(
        body,
        out_shape=[pltpu.HBM(x.shape, x.dtype) for x in shapes],
        in_specs=[SMEM] + [ANY] * n + [VMEM] * (2 + len(more)),
        out_specs=[HBM] * len(shapes),
        scratch_shapes=[pltpu.VMEM(x.shape, x.dtype) for x in shapes]
        + [pltpu.VMEM((1, rows, width), BF16)] * n
        + [
            pltpu.VMEM((groups, rows, rows), BF16),
            pltpu.SemaphoreType.DMA((n,)),
            pltpu.SemaphoreType.DMA((tiles * nv * PIECES * 3,)),
        ],
        cost_estimate=cost(0, *shapes),
        compiler_params=params(),
        name="last_sums",
    )(o.reshape(1), *flat, pair_own, vectors, *more)
    return [outs[4 * p : 4 * p + 4] for p in range(PIECES)]


def per_device(na, nv, no, factors, trials):
    nq, rows, width = factors.shape
    nm, _, cols = trials.shape
    nz = na // CORES
    a, v, o = (lax.axis_index(name) for name in ("aux", "vir", "outer"))
    z, c = a // CORES, a % CORES
    half_m, take = nm // CORES, nq // nv
    block, total = CORES * cols, nv * width
    own = rows // no
    groups = nv * half_m
    early_steps = take - 1
    last_steps = take - early_steps

    mine = part(trials, o, own, 1).astype(BF16)
    others = [shift(mine, "vir", nv, -r) for r in range(1, nv)]

    def sends(source, first, size):
        return [
            lax.dynamic_slice_in_dim(source, (v - r) % nv * take + first, size, 0)
            for r in range(1, nv)
        ]

    def along_vir(group):
        return [shift(x, "vir", nv, -r - 1) for r, x in enumerate(group)]

    come = None
    if early_steps:
        group, others = lax.optimization_barrier((sends(factors, 0, early_steps), others))
        come = along_vir(group)

    both = jnp.concatenate([mine] + others, axis=0).reshape(nv, CORES, half_m, own, cols)
    given = sibling(lax.dynamic_index_in_dim(both, 1 - c, 1, False), na)
    kept = lax.dynamic_index_in_dim(both, c, 1, False)
    whole = jnp.where(
        c == 0,
        jnp.concatenate([kept, given], axis=-1),
        jnp.concatenate([given, kept], axis=-1),
    ).reshape(groups, own, block)
    later, whole = lax.optimization_barrier((factors, whole))

    blocks = []
    for t in sorted(range(nz), key=lambda t: min(t, nz - t)):
        got = whole if t == 0 else shift(whole, "aux", na, t, CORES)
        blocks.append((got, 0, nz, t))
        for s in range(1, no):
            blocks.append((shift(got, "outer", no, -s), 0, nz + s, t))
    where = jnp.stack(
        [((z - t) % nz * block - v * width) % total for t in range(nz)]
        + [(o + s) % no * own for s in range(no)]
    ).astype(jnp.int32)
    later, _ = lax.optimization_barrier((factors, blocks[no - 1][0]))
    held = (come, sends(later, early_steps, last_steps), [b[0] for b in blocks])
    come, group, _ = lax.optimization_barrier(held)
    come_last = along_vir(group)
    vectors = assemble(where, blocks, groups, rows, total)

    kept = lax.dynamic_slice_in_dim(later, v * take, take, 0)
    shown = sibling(kept, na)
    early = None
    if early_steps:
        got = come
        their = [[sibling(g, na)] for g in got]
        early = early_sums(
            [[[kept]] + [[g] for g in got], [[shown]] + their], early_steps, vectors
        )
    got, early = lax.optimization_barrier((come_last, early))
    sides = [[kept] + got, [shown] + [sibling(g, na) for g in got]]
    firsts = [early_steps] + [0] * (nv - 1)
    pair_own = step_pairs(sides[0], firsts, vectors)

    out = []
    for p in last_sums(o, sides, firsts, pair_own, vectors, early, no, nv):
        send_x, keep_x, send_y, keep_y = p
        one = keep_x
        for r in range(1, nv):
            sent = send_x[(r - 1) * half_m : r * half_m]
            one += shift(sent, "vir", nv, r).astype(F32)
        u_one = lax.dynamic_index_in_dim(one, o, 1, False)
        for s in range(1, no):
            sent = lax.dynamic_index_in_dim(one, (o + s) % no, 1, False).astype(BF16)
            u_one += shift(sent, "outer", no, s).astype(F32)
        two = keep_y
        for s in range(1, no):
            two += shift(send_y[s - 1], "outer", no, s).astype(F32)
        u_two = two[:half_m]
        for r in range(1, nv):
            sent = two[r * half_m : (r + 1) * half_m].astype(BF16)
            u_two += shift(sent, "vir", nv, r).astype(F32)
        u = jnp.concatenate([u_one, u_two], axis=1)

        def to(zz):
            return lax.dynamic_slice_in_dim(u, (zz * block - v * width) % total, block, 2)

        got = to(z)
        for t in range(1, nz):
            got += shift(to((z + t) % nz).astype(BF16), "aux", na, t, CORES).astype(F32)
        out.append(got)
    done = jnp.concatenate(out, axis=1)
    there = sibling(part(done, 1 - c, cols, 2), na)
    here = part(done, c, cols, 2)
    return jnp.where(
        c == 0, jnp.concatenate([here, there], axis=0), jnp.concatenate([there, here], axis=0)
    )


def solution(mesh):
    na, nv, no = (mesh.shape[name] for name in ("aux", "vir", "outer"))

    def step(factors, trials):
        nq, rows, width = factors.shape
        nm, _, cols = trials.shape
        fits = na % CORES == 0 and nm % CORES == 0 and nq % nv == 0
        fits = fits and width % (CORES * cols) == 0 and cols % 128 == 0
        fits = fits and rows % (no * PIECES * 2 * 16) == 0
        if fits:
            return per_device(na, nv, no, factors, trials)
        return plain(factors, trials)

    placed = (P(("aux", "outer"), None, "vir"), P("vir", None, "aux"))
    return jax.shard_map(
        step, mesh=mesh, in_specs=placed, out_specs=P("vir", "outer", "aux"), check_vma=False
    )
```

```python
import jax
import jax.numpy as jnp
from jax import lax
from jax.experimental import pallas as pl
from jax.experimental.pallas import tpu as pltpu
from jax.sharding import PartitionSpec as P

CORES = 2
PIECES = 2
VMEM_LIMIT = 30 * 2**20
F32, BF16 = jnp.float32, jnp.bfloat16
VMEM = pl.BlockSpec(memory_space=pltpu.VMEM)
ANY = pl.BlockSpec(memory_space=pl.ANY)
HBM = pl.BlockSpec(memory_space=pltpu.HBM)
SMEM = pl.BlockSpec(memory_space=pltpu.SMEM)


def plain(factors, trials):
    trial_b = trials.astype(jnp.bfloat16)
    gathered = lax.all_gather(trial_b, "aux", axis=2, tiled=True)
    columns = lax.all_gather(factors, "vir", axis=2, tiled=True)
    pairs = jnp.einsum(
        "qib,mjb->mqij", columns, gathered, preferred_element_type=jnp.float32
    ).astype(jnp.bfloat16)
    stacked = jnp.einsum("mqij,qja->mia", pairs, columns, preferred_element_type=jnp.float32)
    slices = lax.psum_scatter(stacked, "aux", scatter_dimension=2, tiled=True)
    return lax.psum_scatter(slices, "outer", scatter_dimension=1, tiled=True)


def shift(array, axis, size, step, stride=1):
    count = size // stride
    pairs = [
        (i, (i // stride + step) % count * stride + i % stride) for i in range(size)
    ]
    return lax.ppermute(array, axis, pairs)


def sibling(array, size):
    return lax.ppermute(array, "aux", [(i, i ^ 1) for i in range(size)])


def part(array, index, size, axis):
    return lax.dynamic_slice_in_dim(array, index * size, size, axis)


def dot_nt(a, b):
    return lax.dot_general(a, b, (((1,), (1,)), ((), ())), preferred_element_type=F32)


def params():
    return pltpu.CompilerParams(vmem_limit_bytes=VMEM_LIMIT)


def in_hbm(x):
    return pltpu.with_memory_space_constraint(x, pltpu.HBM)


def cost(flops, *arrays):
    moved = sum(x.size * x.dtype.itemsize for x in arrays)
    return pl.CostEstimate(flops=flops, bytes_accessed=moved, transcendentals=0)


def assemble(where, blocks, groups, rows, total):
    shape = jax.ShapeDtypeStruct((groups, rows, total), BF16)

    def body(at, *refs):
        out, sems = refs[-2:]
        copies = []
        for i, (_, first, row_slot, col_slot) in enumerate(blocks):
            many, share, block = refs[i].shape
            row = pl.multiple_of(at[row_slot], share)
            col = pl.multiple_of(at[col_slot], block)
            to = out.at[pl.ds(first, many), pl.ds(row, share), pl.ds(col, block)]
            copies.append(pltpu.make_async_copy(refs[i], to, sems.at[i]))
        for copy in copies:
            copy.start()
        for copy in copies:
            copy.wait()

    return pl.pallas_call(
        body,
        out_shape=shape,
        in_specs=[SMEM] + [ANY] * len(blocks),
        out_specs=ANY,
        scratch_shapes=[pltpu.SemaphoreType.DMA((len(blocks),))],
        cost_estimate=cost(0, shape),
        compiler_params=params(),
        name="assemble",
    )(where, *[in_hbm(b[0]) for b in blocks])


def pairs_of(refs, vec, store):
    groups, rows, _ = vec.shape
    count, _, width = refs[0].shape
    for g in range(groups):
        acc = None
        for r, ref in enumerate(refs):
            left = ref[...].reshape(count * rows, width)
            term = dot_nt(left, vec[g, :, r * width : (r + 1) * width])
            acc = term if acc is None else acc + term
        acc = acc.astype(BF16)
        for k in range(count):
            store(g, k, acc[k * rows : (k + 1) * rows])


def early_sums(sides, steps, vectors):
    groups, rows, total = vectors.shape
    nr = len(sides[0])
    width = total // nr
    slots = [pieces for side in sides for pieces in side]
    flat = [p for pieces in slots for p in pieces]
    n, ns = len(flat), len(slots)
    shape = jax.ShapeDtypeStruct((groups, rows, total), F32)
    tile = min(width, 512)
    tiles = total // tile

    def body(*refs):
        vec, out = refs[n : n + 2]
        held, sems = refs[-2:]
        ins = refs[n + 2 : n + 2 + ns]
        copies, i = [], 0
        for slot, pieces in zip(ins, slots):
            group, at = [], 0
            for piece in pieces:
                size = min(piece.shape[0], steps)
                to = slot.at[pl.ds(at, size)]
                group.append(pltpu.make_async_copy(refs[i].at[pl.ds(0, size)], to, sems.at[i]))
                group[-1].start()
                i, at = i + 1, at + size
            copies.append(group)
        for s in range(len(sides)):

            def store(g, k, pair, s=s):
                held[s, g * rows : (g + 1) * rows, k * rows : (k + 1) * rows] = pair

            for group in copies[s * nr : (s + 1) * nr]:
                for copy in group:
                    copy.wait()
            pairs_of(ins[s * nr : (s + 1) * nr], vec, store)
        for i in range(tiles):
            r, at = i * tile // width, i * tile % width
            acc = None
            for s in range(len(sides)):
                right = ins[s * nr + r][:, :, at : at + tile].reshape(steps * rows, tile)
                term = jnp.dot(held[s], right, preferred_element_type=F32)
                acc = term if acc is None else acc + term
            out[:, :, i * tile : (i + 1) * tile] = acc.reshape(groups, rows, tile)

    return pl.pallas_call(
        body,
        out_shape=shape,
        in_specs=[ANY] * n + [VMEM],
        out_specs=VMEM,
        scratch_shapes=[pltpu.VMEM((steps, rows, width), BF16)] * ns
        + [
            pltpu.VMEM((len(sides), groups * rows, steps * rows), BF16),
            pltpu.SemaphoreType.DMA((n,)),
        ],
        cost_estimate=cost(0, vectors),
        compiler_params=params(),
        name="early_sums",
    )(*flat, vectors)


def step_pairs(side, firsts, vectors):
    groups, rows, total = vectors.shape
    shape = jax.ShapeDtypeStruct((groups, rows, rows), BF16)
    n = len(side)
    width = total // n

    def body(*refs):
        vec, out = refs[n : n + 2]
        ins = refs[n + 2 : 2 * n + 2]
        sems = refs[-1]
        copies = [
            pltpu.make_async_copy(refs[i].at[pl.ds(firsts[i], 1)], ins[i], sems.at[i])
            for i in range(n)
        ]
        for copy in copies:
            copy.start()
        for copy in copies:
            copy.wait()

        def store(g, _, pair):
            out[g] = pair

        pairs_of(ins, vec, store)

    return pl.pallas_call(
        body,
        out_shape=shape,
        in_specs=[ANY] * n + [VMEM],
        out_specs=VMEM,
        scratch_shapes=[pltpu.VMEM((1, rows, width), BF16)] * n
        + [pltpu.SemaphoreType.DMA((n,))],
        cost_estimate=cost(0, vectors),
        compiler_params=params(),
        name="step_pairs",
    )(*side, vectors)


def last_sums(o, sides, firsts, pair_own, vectors, early, no, nv):
    groups, rows, total = vectors.shape
    nr = len(sides[0])
    width = total // nr
    flat = [p for side in sides for p in side]
    n = len(flat)
    per = groups // nv
    own = rows // no
    small = own // (PIECES * 2)
    more = [] if early is None else [early]
    tile = min(width, 1024)
    tiles = total // tile

    def body(*refs):
        me = refs[0][0]
        refs = refs[1:]
        own_pair, vec = refs[n : n + 2]
        before = refs[n + 2] if more else None
        results = refs[n + 2 + len(more) : n + 2 + len(more) + 4 * PIECES]
        outs = refs[n + 2 + len(more) + 4 * PIECES : n + 2 + len(more) + 8 * PIECES]
        ins = refs[-n - 3 : -3]
        their_pair, sems, out_sems = refs[-3:]
        copies = [
            pltpu.make_async_copy(refs[i].at[pl.ds(firsts[i % nr], 1)], ins[i], sems.at[i])
            for i in range(n)
        ]
        for copy in copies[nr:] + copies[:nr]:
            copy.start()
        for copy in copies[nr:]:
            copy.wait()

        def store(g, _, pair):
            their_pair[g] = pair

        pairs_of(ins[nr:], vec, store)
        for copy in copies[:nr]:
            copy.wait()
        left = [p[...].reshape(groups * rows, rows) for p in (own_pair, their_pair)]
        sent = []
        for i in range(tiles):
            r, at = i * tile // width, i * tile % width
            got = None
            for s in range(len(sides)):
                right = ins[s * nr + r][0, :, at : at + tile]
                term = jnp.dot(left[s], right, preferred_element_type=F32)
                got = term if got is None else got + term
            got = got.reshape(groups, rows, tile)
            if more:
                got = got + before[:, :, i * tile : (i + 1) * tile]
            got = got.reshape(groups, no, PIECES, 2, small, tile)
            for g in range(groups):
                v = g // per
                to = (r - v) % nr * width + at
                cols = slice(to, to + tile)
                for p in range(PIECES):
                    send_x, keep_x, send_y, keep_y = outs[4 * p : 4 * p + 4]
                    for oo in range(no):
                        if v == 0:
                            keep_x[g, oo, :, cols] = got[g, oo, p, 0]
                        else:
                            send_x[g - per, oo, :, cols] = got[g, oo, p, 0].astype(BF16)
            for oo in range(no):
                slot = lax.rem(oo - me + no, no)
                for g in range(groups):
                    to = (r - g // per) % nr * width + at
                    cols = slice(to, to + tile)
                    for p in range(PIECES):
                        outs[4 * p + 2][slot, g, :, cols] = got[g, oo, p, 1].astype(BF16)
                        outs[4 * p + 3][slot, g, :, cols] = got[g, oo, p, 1]
            for v in range(nv):
                cols = pl.ds((r - v) % nr * width + at, tile)
                for p in range(PIECES):
                    at_x = (pl.ds(0, per) if v == 0 else pl.ds((v - 1) * per, per), slice(None), slice(None), cols)
                    at_y = (pl.ds(v * per, per), slice(None), cols)
                    for k, source, where in (
                        (1 if v == 0 else 0, at_x, at_x),
                        (2, (pl.ds(1, no - 1), *at_y), (slice(None), *at_y)),
                        (3, (0, *at_y), at_y),
                    ):
                        out, result = outs[4 * p + k], results[4 * p + k]
                        sent.append(
                            pltpu.make_async_copy(
                                out.at[source], result.at[where], out_sems.at[len(sent)]
                            )
                        )
                        sent[-1].start()
        for copy in sent:
            copy.wait()

    shapes = [
        jax.ShapeDtypeStruct((groups - per, no, small, total), BF16),
        jax.ShapeDtypeStruct((per, no, small, total), F32),
        jax.ShapeDtypeStruct((no - 1, groups, small, total), BF16),
        jax.ShapeDtypeStruct((groups, small, total), F32),
    ] * PIECES
    every = (no, groups, small, total)
    held = [(shapes[0].shape, BF16), (shapes[1].shape, F32), (every, BF16), (every, F32)] * PIECES
    outs = pl.pallas_call(
        body,
        out_shape=[pltpu.HBM(x.shape, x.dtype) for x in shapes],
        in_specs=[SMEM] + [ANY] * n + [VMEM] * (2 + len(more)),
        out_specs=[HBM] * len(shapes),
        scratch_shapes=[pltpu.VMEM(x, d) for x, d in held]
        + [pltpu.VMEM((1, rows, width), BF16)] * n
        + [
            pltpu.VMEM((groups, rows, rows), BF16),
            pltpu.SemaphoreType.DMA((n,)),
            pltpu.SemaphoreType.DMA((tiles * nv * PIECES * 3,)),
        ],
        cost_estimate=cost(0, *shapes),
        compiler_params=params(),
        name="last_sums",
    )(o.reshape(1), *flat, pair_own, vectors, *more)
    return [outs[4 * p : 4 * p + 4] for p in range(PIECES)]


def per_device(na, nv, no, factors, trials):
    nq, rows, width = factors.shape
    nm, _, cols = trials.shape
    nz = na // CORES
    a, v, o = (lax.axis_index(name) for name in ("aux", "vir", "outer"))
    z, c = a // CORES, a % CORES
    half_m, take = nm // CORES, nq // nv
    block, total = CORES * cols, nv * width
    own = rows // no
    groups = nv * half_m
    early_steps = take - 1
    last_steps = take - early_steps

    mine = part(trials, o, own, 1).astype(BF16)
    others = [shift(mine, "vir", nv, -r) for r in range(1, nv)]

    def sends(source, first, size):
        return [
            lax.dynamic_slice_in_dim(source, (v - r) % nv * take + first, size, 0)
            for r in range(1, nv)
        ]

    def along_vir(group):
        return [shift(x, "vir", nv, -r - 1) for r, x in enumerate(group)]

    come = None
    if early_steps:
        group, others = lax.optimization_barrier((sends(factors, 0, early_steps), others))
        come = along_vir(group)

    both = jnp.concatenate([mine] + others, axis=0).reshape(nv, CORES, half_m, own, cols)
    given = sibling(lax.dynamic_index_in_dim(both, 1 - c, 1, False), na)
    kept = lax.dynamic_index_in_dim(both, c, 1, False)
    whole = jnp.where(
        c == 0,
        jnp.concatenate([kept, given], axis=-1),
        jnp.concatenate([given, kept], axis=-1),
    ).reshape(groups, own, block)
    later, whole = lax.optimization_barrier((factors, whole))

    blocks = []
    for t in sorted(range(nz), key=lambda t: min(t, nz - t)):
        got = whole if t == 0 else shift(whole, "aux", na, t, CORES)
        blocks.append((got, 0, nz, t))
        for s in range(1, no):
            blocks.append((shift(got, "outer", no, -s), 0, nz + s, t))
    where = jnp.stack(
        [((z - t) % nz * block - v * width) % total for t in range(nz)]
        + [(o + s) % no * own for s in range(no)]
    ).astype(jnp.int32)
    later, _ = lax.optimization_barrier((factors, blocks[no - 1][0]))
    group = sends(later, early_steps, last_steps)
    come_last = along_vir(group)
    come, _ = lax.optimization_barrier((come, (group, [b[0] for b in blocks])))
    vectors = assemble(where, blocks, groups, rows, total)

    kept = lax.dynamic_slice_in_dim(later, v * take, take, 0)
    shown = sibling(kept, na)
    early = None
    if early_steps:
        got = come
        their = [[sibling(g, na)] for g in got]
        early = early_sums(
            [[[kept]] + [[g] for g in got], [[shown]] + their], early_steps, vectors
        )
    got, early = lax.optimization_barrier((come_last, early))
    sides = [[kept] + got, [shown] + [sibling(g, na) for g in got]]
    firsts = [early_steps] + [0] * (nv - 1)
    pair_own = step_pairs(sides[0], firsts, vectors)

    out = []
    for p in last_sums(o, sides, firsts, pair_own, vectors, early, no, nv):
        send_x, keep_x, send_y, keep_y = p
        one = keep_x
        for r in range(1, nv):
            sent = send_x[(r - 1) * half_m : r * half_m]
            one += shift(sent, "vir", nv, r).astype(F32)
        u_one = lax.dynamic_index_in_dim(one, o, 1, False)
        for s in range(1, no):
            sent = lax.dynamic_index_in_dim(one, (o + s) % no, 1, False).astype(BF16)
            u_one += shift(sent, "outer", no, s).astype(F32)
        two = keep_y
        for s in range(1, no):
            two += shift(send_y[s - 1], "outer", no, s).astype(F32)
        u_two = two[:half_m]
        for r in range(1, nv):
            sent = two[r * half_m : (r + 1) * half_m].astype(BF16)
            u_two += shift(sent, "vir", nv, r).astype(F32)
        u = jnp.concatenate([u_one, u_two], axis=1)

        def to(zz):
            return lax.dynamic_slice_in_dim(u, (zz * block - v * width) % total, block, 2)

        got = to(z)
        for t in range(1, nz):
            got += shift(to((z + t) % nz).astype(BF16), "aux", na, t, CORES).astype(F32)
        out.append(got)
    done = jnp.concatenate(out, axis=1)
    there = sibling(part(done, 1 - c, cols, 2), na)
    here = part(done, c, cols, 2)
    return jnp.where(
        c == 0, jnp.concatenate([here, there], axis=0), jnp.concatenate([there, here], axis=0)
    )


def solution(mesh):
    na, nv, no = (mesh.shape[name] for name in ("aux", "vir", "outer"))

    def step(factors, trials):
        nq, rows, width = factors.shape
        nm, _, cols = trials.shape
        fits = na % CORES == 0 and nm % CORES == 0 and nq % nv == 0
        fits = fits and width % (CORES * cols) == 0 and cols % 128 == 0
        fits = fits and rows % (no * PIECES * 2 * 16) == 0
        if fits:
            return per_device(na, nv, no, factors, trials)
        return plain(factors, trials)

    placed = (P(("aux", "outer"), None, "vir"), P("vir", None, "aux"))
    return jax.shard_map(
        step, mesh=mesh, in_specs=placed, out_specs=P("vir", "outer", "aux"), check_vma=False
    )
```

```python
import jax
import jax.numpy as jnp
from jax import lax
from jax.experimental import pallas as pl
from jax.experimental.pallas import tpu as pltpu
from jax.sharding import PartitionSpec as P

CORES = 2
PIECES = 2
VMEM_LIMIT = 30 * 2**20
F32, BF16 = jnp.float32, jnp.bfloat16
VMEM = pl.BlockSpec(memory_space=pltpu.VMEM)
ANY = pl.BlockSpec(memory_space=pl.ANY)
HBM = pl.BlockSpec(memory_space=pltpu.HBM)
SMEM = pl.BlockSpec(memory_space=pltpu.SMEM)


def plain(factors, trials):
    trial_b = trials.astype(jnp.bfloat16)
    gathered = lax.all_gather(trial_b, "aux", axis=2, tiled=True)
    columns = lax.all_gather(factors, "vir", axis=2, tiled=True)
    pairs = jnp.einsum(
        "qib,mjb->mqij", columns, gathered, preferred_element_type=jnp.float32
    ).astype(jnp.bfloat16)
    stacked = jnp.einsum("mqij,qja->mia", pairs, columns, preferred_element_type=jnp.float32)
    slices = lax.psum_scatter(stacked, "aux", scatter_dimension=2, tiled=True)
    return lax.psum_scatter(slices, "outer", scatter_dimension=1, tiled=True)


def shift(array, axis, size, step, stride=1):
    count = size // stride
    pairs = [
        (i, (i // stride + step) % count * stride + i % stride) for i in range(size)
    ]
    return lax.ppermute(array, axis, pairs)


def sibling(array, size):
    return lax.ppermute(array, "aux", [(i, i ^ 1) for i in range(size)])


def part(array, index, size, axis):
    return lax.dynamic_slice_in_dim(array, index * size, size, axis)


def dot_nt(a, b):
    return lax.dot_general(a, b, (((1,), (1,)), ((), ())), preferred_element_type=F32)


def params():
    return pltpu.CompilerParams(vmem_limit_bytes=VMEM_LIMIT)


def in_hbm(x):
    return pltpu.with_memory_space_constraint(x, pltpu.HBM)


def cost(flops, *arrays):
    moved = sum(x.size * x.dtype.itemsize for x in arrays)
    return pl.CostEstimate(flops=flops, bytes_accessed=moved, transcendentals=0)


def assemble(where, blocks, groups, rows, total):
    shape = jax.ShapeDtypeStruct((groups, rows, total), BF16)

    def body(at, *refs):
        out, sems = refs[-2:]
        copies = []
        for i, (_, first, row_slot, col_slot) in enumerate(blocks):
            many, share, block = refs[i].shape
            row = pl.multiple_of(at[row_slot], share)
            col = pl.multiple_of(at[col_slot], block)
            to = out.at[pl.ds(first, many), pl.ds(row, share), pl.ds(col, block)]
            copies.append(pltpu.make_async_copy(refs[i], to, sems.at[i]))
        for copy in copies:
            copy.start()
        for copy in copies:
            copy.wait()

    return pl.pallas_call(
        body,
        out_shape=shape,
        in_specs=[SMEM] + [ANY] * len(blocks),
        out_specs=ANY,
        scratch_shapes=[pltpu.SemaphoreType.DMA((len(blocks),))],
        cost_estimate=cost(0, shape),
        compiler_params=params(),
        name="assemble",
    )(where, *[in_hbm(b[0]) for b in blocks])


def pairs_of(refs, vec, store):
    groups, rows, _ = vec.shape
    count, _, width = refs[0].shape
    for g in range(groups):
        acc = None
        for r, ref in enumerate(refs):
            left = ref[...].reshape(count * rows, width)
            term = dot_nt(left, vec[g, :, r * width : (r + 1) * width])
            acc = term if acc is None else acc + term
        acc = acc.astype(BF16)
        for k in range(count):
            store(g, k, acc[k * rows : (k + 1) * rows])


def early_sums(sides, steps, vectors):
    groups, rows, total = vectors.shape
    nr = len(sides[0])
    width = total // nr
    slots = [pieces for side in sides for pieces in side]
    flat = [p for pieces in slots for p in pieces]
    n, ns = len(flat), len(slots)
    shape = jax.ShapeDtypeStruct((groups, rows, total), F32)
    tile = min(width, 512)
    tiles = total // tile

    def body(*refs):
        vec, out = refs[n : n + 2]
        held, sems = refs[-2:]
        ins = refs[n + 2 : n + 2 + ns]
        copies, i = [], 0
        for slot, pieces in zip(ins, slots):
            group, at = [], 0
            for piece in pieces:
                size = min(piece.shape[0], steps)
                to = slot.at[pl.ds(at, size)]
                group.append(pltpu.make_async_copy(refs[i].at[pl.ds(0, size)], to, sems.at[i]))
                group[-1].start()
                i, at = i + 1, at + size
            copies.append(group)
        for s in range(len(sides)):

            def store(g, k, pair, s=s):
                held[s, g * rows : (g + 1) * rows, k * rows : (k + 1) * rows] = pair

            for group in copies[s * nr : (s + 1) * nr]:
                for copy in group:
                    copy.wait()
            pairs_of(ins[s * nr : (s + 1) * nr], vec, store)
        for i in range(tiles):
            r, at = i * tile // width, i * tile % width
            acc = None
            for s in range(len(sides)):
                right = ins[s * nr + r][:, :, at : at + tile].reshape(steps * rows, tile)
                term = jnp.dot(held[s], right, preferred_element_type=F32)
                acc = term if acc is None else acc + term
            out[:, :, i * tile : (i + 1) * tile] = acc.reshape(groups, rows, tile)

    return pl.pallas_call(
        body,
        out_shape=shape,
        in_specs=[ANY] * n + [VMEM],
        out_specs=VMEM,
        scratch_shapes=[pltpu.VMEM((steps, rows, width), BF16)] * ns
        + [
            pltpu.VMEM((len(sides), groups * rows, steps * rows), BF16),
            pltpu.SemaphoreType.DMA((n,)),
        ],
        cost_estimate=cost(0, vectors),
        compiler_params=params(),
        name="early_sums",
    )(*flat, vectors)


def step_pairs(side, firsts, vectors):
    groups, rows, total = vectors.shape
    shape = jax.ShapeDtypeStruct((groups, rows, rows), BF16)
    n = len(side)
    width = total // n

    def body(*refs):
        vec, out = refs[n : n + 2]
        ins = refs[n + 2 : 2 * n + 2]
        sems = refs[-1]
        copies = [
            pltpu.make_async_copy(refs[i].at[pl.ds(firsts[i], 1)], ins[i], sems.at[i])
            for i in range(n)
        ]
        for copy in copies:
            copy.start()
        for copy in copies:
            copy.wait()

        def store(g, _, pair):
            out[g] = pair

        pairs_of(ins, vec, store)

    return pl.pallas_call(
        body,
        out_shape=shape,
        in_specs=[ANY] * n + [VMEM],
        out_specs=VMEM,
        scratch_shapes=[pltpu.VMEM((1, rows, width), BF16)] * n
        + [pltpu.SemaphoreType.DMA((n,))],
        cost_estimate=cost(0, vectors),
        compiler_params=params(),
        name="step_pairs",
    )(*side, vectors)


def last_sums(o, sides, firsts, pair_own, vectors, early, no, nv):
    groups, rows, total = vectors.shape
    nr = len(sides[0])
    width = total // nr
    flat = [p for side in sides for p in side]
    n = len(flat)
    per = groups // nv
    own = rows // no
    small = own // (PIECES * 2)
    more = [] if early is None else [early]
    tile = min(width, 1024)
    tiles = total // tile

    def body(*refs):
        me = refs[0][0]
        refs = refs[1:]
        own_pair, vec = refs[n : n + 2]
        before = refs[n + 2] if more else None
        results = refs[n + 2 + len(more) : n + 2 + len(more) + 4 * PIECES]
        outs = refs[n + 2 + len(more) + 4 * PIECES : n + 2 + len(more) + 8 * PIECES]
        ins = refs[-n - 3 : -3]
        their_pair, sems, out_sems = refs[-3:]
        copies = [
            pltpu.make_async_copy(refs[i].at[pl.ds(firsts[i % nr], 1)], ins[i], sems.at[i])
            for i in range(n)
        ]
        for copy in copies[nr:] + copies[:nr]:
            copy.start()
        for copy in copies[nr:]:
            copy.wait()

        def store(g, _, pair):
            their_pair[g] = pair

        pairs_of(ins[nr:], vec, store)
        for copy in copies[:nr]:
            copy.wait()
        left = [p[...].reshape(groups * rows, rows) for p in (own_pair, their_pair)]
        sent = []
        for i in range(tiles):
            r, at = i * tile // width, i * tile % width
            got = None
            for s in range(len(sides)):
                right = ins[s * nr + r][0, :, at : at + tile]
                term = jnp.dot(left[s], right, preferred_element_type=F32)
                got = term if got is None else got + term
            got = got.reshape(groups, rows, tile)
            if more:
                got = got + before[:, :, i * tile : (i + 1) * tile]
            got = got.reshape(groups, no, PIECES, 2, small, tile)
            for g in range(groups):
                v = g // per
                to = (r - v) % nr * width + at
                cols = slice(to, to + tile)
                for p in range(PIECES):
                    send_x, keep_x, send_y, keep_y = outs[4 * p : 4 * p + 4]
                    for oo in range(no):
                        if v == 0:
                            keep_x[g, oo, :, cols] = got[g, oo, p, 0]
                        else:
                            send_x[g - per, oo, :, cols] = got[g, oo, p, 0].astype(BF16)
            for oo in range(no):
                slot = lax.rem(oo - me + no, no)
                for g in range(groups):
                    to = (r - g // per) % nr * width + at
                    cols = slice(to, to + tile)
                    for p in range(PIECES):
                        outs[4 * p + 2][slot, g, :, cols] = got[g, oo, p, 1].astype(BF16)
                        outs[4 * p + 3][slot, g, :, cols] = got[g, oo, p, 1]
            for v in range(nv):
                cols = pl.ds((r - v) % nr * width + at, tile)
                for p in range(PIECES):
                    at_x = (pl.ds(0, per) if v == 0 else pl.ds((v - 1) * per, per), slice(None), slice(None), cols)
                    at_y = (pl.ds(v * per, per), slice(None), cols)
                    for k, source, where in (
                        (1 if v == 0 else 0, at_x, at_x),
                        (2, (pl.ds(1, no - 1), *at_y), (slice(None), *at_y)),
                        (3, (0, *at_y), at_y),
                    ):
                        out, result = outs[4 * p + k], results[4 * p + k]
                        sent.append(
                            pltpu.make_async_copy(
                                out.at[source], result.at[where], out_sems.at[len(sent)]
                            )
                        )
                        sent[-1].start()
        for copy in sent:
            copy.wait()

    shapes = [
        jax.ShapeDtypeStruct((groups - per, no, small, total), BF16),
        jax.ShapeDtypeStruct((per, no, small, total), F32),
        jax.ShapeDtypeStruct((no - 1, groups, small, total), BF16),
        jax.ShapeDtypeStruct((groups, small, total), F32),
    ] * PIECES
    every = (no, groups, small, total)
    held = [(shapes[0].shape, BF16), (shapes[1].shape, F32), (every, BF16), (every, F32)] * PIECES
    outs = pl.pallas_call(
        body,
        out_shape=[pltpu.HBM(x.shape, x.dtype) for x in shapes],
        in_specs=[SMEM] + [ANY] * n + [VMEM] * (2 + len(more)),
        out_specs=[HBM] * len(shapes),
        scratch_shapes=[pltpu.VMEM(x, d) for x, d in held]
        + [pltpu.VMEM((1, rows, width), BF16)] * n
        + [
            pltpu.VMEM((groups, rows, rows), BF16),
            pltpu.SemaphoreType.DMA((n,)),
            pltpu.SemaphoreType.DMA((tiles * nv * PIECES * 3,)),
        ],
        cost_estimate=cost(0, *shapes),
        compiler_params=params(),
        name="last_sums",
    )(o.reshape(1), *flat, pair_own, vectors, *more)
    return [outs[4 * p : 4 * p + 4] for p in range(PIECES)]


def per_device(na, nv, no, factors, trials):
    nq, rows, width = factors.shape
    nm, _, cols = trials.shape
    nz = na // CORES
    a, v, o = (lax.axis_index(name) for name in ("aux", "vir", "outer"))
    z, c = a // CORES, a % CORES
    half_m, take = nm // CORES, nq // nv
    block, total = CORES * cols, nv * width
    own = rows // no
    groups = nv * half_m
    early_steps = take - 1
    last_steps = take - early_steps

    mine = part(trials, o, own, 1).astype(BF16)
    others = [shift(mine, "vir", nv, -r) for r in range(1, nv)]

    def sends(source, first, size):
        return [
            lax.dynamic_slice_in_dim(source, (v - r) % nv * take + first, size, 0)
            for r in range(1, nv)
        ]

    def along_vir(group):
        return [shift(x, "vir", nv, -r - 1) for r, x in enumerate(group)]

    come = None
    if early_steps:
        group, others = lax.optimization_barrier((sends(factors, 0, early_steps), others))
        come = along_vir(group)

    both = jnp.concatenate([mine] + others, axis=0).reshape(nv, CORES, half_m, own, cols)
    given = sibling(lax.dynamic_index_in_dim(both, 1 - c, 1, False), na)
    kept = lax.dynamic_index_in_dim(both, c, 1, False)
    whole = jnp.where(
        c == 0,
        jnp.concatenate([kept, given], axis=-1),
        jnp.concatenate([given, kept], axis=-1),
    ).reshape(groups, own, block)
    later, whole = lax.optimization_barrier((factors, whole))

    blocks = []
    for t in sorted(range(nz), key=lambda t: min(t, nz - t)):
        got = whole if t == 0 else shift(whole, "aux", na, t, CORES)
        blocks.append((got, 0, nz, t))
        for s in range(1, no):
            blocks.append((shift(got, "outer", no, -s), 0, nz + s, t))
    where = jnp.stack(
        [((z - t) % nz * block - v * width) % total for t in range(nz)]
        + [(o + s) % no * own for s in range(no)]
    ).astype(jnp.int32)
    later, _ = lax.optimization_barrier((factors, blocks[no - 1][0]))
    held = (come, sends(later, early_steps, last_steps), [b[0] for b in blocks])
    come, group, _ = lax.optimization_barrier(held)
    come_last = along_vir(group)
    vectors = assemble(where, blocks, groups, rows, total)

    kept = lax.dynamic_slice_in_dim(later, v * take, take, 0)
    shown = sibling(kept, na)
    early = None
    if early_steps:
        got = come
        their = [[sibling(g, na)] for g in got]
        early = early_sums(
            [[[kept]] + [[g] for g in got], [[shown]] + their], early_steps, vectors
        )
    got, early = lax.optimization_barrier((come_last, early))
    sides = [[kept] + got, [shown] + [sibling(g, na) for g in got]]
    firsts = [early_steps] + [0] * (nv - 1)
    pair_own = step_pairs(sides[0], firsts, vectors)

    out = []
    for p in last_sums(o, sides, firsts, pair_own, vectors, early, no, nv):
        send_x, keep_x, send_y, keep_y = p
        one = keep_x
        for r in range(1, nv):
            sent = send_x[(r - 1) * half_m : r * half_m]
            one += shift(sent, "vir", nv, r).astype(F32)
        u_one = lax.dynamic_index_in_dim(one, o, 1, False)
        for s in range(1, no):
            sent = lax.dynamic_index_in_dim(one, (o + s) % no, 1, False).astype(BF16)
            u_one += shift(sent, "outer", no, s).astype(F32)
        two = keep_y
        for s in range(1, no):
            two += shift(send_y[s - 1], "outer", no, s).astype(F32)
        u_two = two[:half_m]
        for r in range(1, nv):
            sent = two[r * half_m : (r + 1) * half_m].astype(BF16)
            u_two += shift(sent, "vir", nv, r).astype(F32)
        u = jnp.concatenate([u_one, u_two], axis=1)

        def to(zz):
            return lax.dynamic_slice_in_dim(u, (zz * block - v * width) % total, block, 2)

        got = to(z)
        for t in range(1, nz):
            got += shift(to((z + t) % nz).astype(BF16), "aux", na, t, CORES).astype(F32)
        out.append(got)
    done = jnp.concatenate(out, axis=1)
    there = sibling(part(done, 1 - c, cols, 2), na)
    here = part(done, c, cols, 2)
    return jnp.where(
        c == 0, jnp.concatenate([here, there], axis=0), jnp.concatenate([there, here], axis=0)
    )


def solution(mesh):
    na, nv, no = (mesh.shape[name] for name in ("aux", "vir", "outer"))

    def step(factors, trials):
        nq, rows, width = factors.shape
        nm, _, cols = trials.shape
        fits = na % CORES == 0 and nm % CORES == 0 and nq % nv == 0
        fits = fits and width % (CORES * cols) == 0 and cols % 128 == 0
        fits = fits and rows % (no * PIECES * 2 * 16) == 0
        if fits:
            return per_device(na, nv, no, factors, trials)
        return plain(factors, trials)

    placed = (P(("aux", "outer"), None, "vir"), P("vir", None, "aux"))
    return jax.shard_map(
        step, mesh=mesh, in_specs=placed, out_specs=P("vir", "outer", "aux"), check_vma=False
    )
```

```python
import jax
import jax.numpy as jnp
from jax import lax
from jax.experimental import pallas as pl
from jax.experimental.pallas import tpu as pltpu
from jax.sharding import PartitionSpec as P

CORES = 2
PIECES = 2
VMEM_LIMIT = 30 * 2**20
F32, BF16 = jnp.float32, jnp.bfloat16
VMEM = pl.BlockSpec(memory_space=pltpu.VMEM)
ANY = pl.BlockSpec(memory_space=pl.ANY)
HBM = pl.BlockSpec(memory_space=pltpu.HBM)
SMEM = pl.BlockSpec(memory_space=pltpu.SMEM)


def plain(factors, trials):
    trial_b = trials.astype(jnp.bfloat16)
    gathered = lax.all_gather(trial_b, "aux", axis=2, tiled=True)
    columns = lax.all_gather(factors, "vir", axis=2, tiled=True)
    pairs = jnp.einsum(
        "qib,mjb->mqij", columns, gathered, preferred_element_type=jnp.float32
    ).astype(jnp.bfloat16)
    stacked = jnp.einsum("mqij,qja->mia", pairs, columns, preferred_element_type=jnp.float32)
    slices = lax.psum_scatter(stacked, "aux", scatter_dimension=2, tiled=True)
    return lax.psum_scatter(slices, "outer", scatter_dimension=1, tiled=True)


def shift(array, axis, size, step, stride=1):
    count = size // stride
    pairs = [
        (i, (i // stride + step) % count * stride + i % stride) for i in range(size)
    ]
    return lax.ppermute(array, axis, pairs)


def sibling(array, size):
    return lax.ppermute(array, "aux", [(i, i ^ 1) for i in range(size)])


def part(array, index, size, axis):
    return lax.dynamic_slice_in_dim(array, index * size, size, axis)


def dot_nt(a, b):
    return lax.dot_general(a, b, (((1,), (1,)), ((), ())), preferred_element_type=F32)


def params():
    return pltpu.CompilerParams(vmem_limit_bytes=VMEM_LIMIT)


def in_hbm(x):
    return pltpu.with_memory_space_constraint(x, pltpu.HBM)


def cost(flops, *arrays):
    moved = sum(x.size * x.dtype.itemsize for x in arrays)
    return pl.CostEstimate(flops=flops, bytes_accessed=moved, transcendentals=0)


def assemble(where, blocks, groups, rows, total):
    shape = jax.ShapeDtypeStruct((groups, rows, total), BF16)

    def body(at, *refs):
        out, sems = refs[-2:]
        copies = []
        for i, (_, first, row_slot, col_slot) in enumerate(blocks):
            many, share, block = refs[i].shape
            row = pl.multiple_of(at[row_slot], share)
            col = pl.multiple_of(at[col_slot], block)
            to = out.at[pl.ds(first, many), pl.ds(row, share), pl.ds(col, block)]
            copies.append(pltpu.make_async_copy(refs[i], to, sems.at[i]))
        for copy in copies:
            copy.start()
        for copy in copies:
            copy.wait()

    return pl.pallas_call(
        body,
        out_shape=shape,
        in_specs=[SMEM] + [ANY] * len(blocks),
        out_specs=ANY,
        scratch_shapes=[pltpu.SemaphoreType.DMA((len(blocks),))],
        cost_estimate=cost(0, shape),
        compiler_params=params(),
        name="assemble",
    )(where, *[in_hbm(b[0]) for b in blocks[:-1]], blocks[-1][0])


def pairs_of(refs, vec, store):
    groups, rows, _ = vec.shape
    count, _, width = refs[0].shape
    for g in range(groups):
        acc = None
        for r, ref in enumerate(refs):
            left = ref[...].reshape(count * rows, width)
            term = dot_nt(left, vec[g, :, r * width : (r + 1) * width])
            acc = term if acc is None else acc + term
        acc = acc.astype(BF16)
        for k in range(count):
            store(g, k, acc[k * rows : (k + 1) * rows])


def early_sums(sides, steps, vectors):
    groups, rows, total = vectors.shape
    nr = len(sides[0])
    width = total // nr
    slots = [pieces for side in sides for pieces in side]
    flat = [p for pieces in slots for p in pieces]
    n, ns = len(flat), len(slots)
    shape = jax.ShapeDtypeStruct((groups, rows, total), F32)
    tile = min(width, 512)
    tiles = total // tile

    def body(*refs):
        vec, out = refs[n : n + 2]
        held, sems = refs[-2:]
        ins = refs[n + 2 : n + 2 + ns]
        copies, i = [], 0
        for slot, pieces in zip(ins, slots):
            group, at = [], 0
            for piece in pieces:
                size = min(piece.shape[0], steps)
                to = slot.at[pl.ds(at, size)]
                group.append(pltpu.make_async_copy(refs[i].at[pl.ds(0, size)], to, sems.at[i]))
                group[-1].start()
                i, at = i + 1, at + size
            copies.append(group)
        for s in range(len(sides)):

            def store(g, k, pair, s=s):
                held[s, g * rows : (g + 1) * rows, k * rows : (k + 1) * rows] = pair

            for group in copies[s * nr : (s + 1) * nr]:
                for copy in group:
                    copy.wait()
            pairs_of(ins[s * nr : (s + 1) * nr], vec, store)
        for i in range(tiles):
            r, at = i * tile // width, i * tile % width
            acc = None
            for s in range(len(sides)):
                right = ins[s * nr + r][:, :, at : at + tile].reshape(steps * rows, tile)
                term = jnp.dot(held[s], right, preferred_element_type=F32)
                acc = term if acc is None else acc + term
            out[:, :, i * tile : (i + 1) * tile] = acc.reshape(groups, rows, tile)

    return pl.pallas_call(
        body,
        out_shape=shape,
        in_specs=[ANY] * n + [VMEM],
        out_specs=VMEM,
        scratch_shapes=[pltpu.VMEM((steps, rows, width), BF16)] * ns
        + [
            pltpu.VMEM((len(sides), groups * rows, steps * rows), BF16),
            pltpu.SemaphoreType.DMA((n,)),
        ],
        cost_estimate=cost(0, vectors),
        compiler_params=params(),
        name="early_sums",
    )(*flat, vectors)


def step_pairs(side, firsts, vectors):
    groups, rows, total = vectors.shape
    shape = jax.ShapeDtypeStruct((groups, rows, rows), BF16)
    n = len(side)
    width = total // n

    def body(*refs):
        vec, out = refs[n : n + 2]
        ins = refs[n + 2 : 2 * n + 2]
        sems = refs[-1]
        copies = [
            pltpu.make_async_copy(refs[i].at[pl.ds(firsts[i], 1)], ins[i], sems.at[i])
            for i in range(n)
        ]
        for copy in copies:
            copy.start()
        for copy in copies:
            copy.wait()

        def store(g, _, pair):
            out[g] = pair

        pairs_of(ins, vec, store)

    return pl.pallas_call(
        body,
        out_shape=shape,
        in_specs=[ANY] * n + [VMEM],
        out_specs=VMEM,
        scratch_shapes=[pltpu.VMEM((1, rows, width), BF16)] * n
        + [pltpu.SemaphoreType.DMA((n,))],
        cost_estimate=cost(0, vectors),
        compiler_params=params(),
        name="step_pairs",
    )(*side, vectors)


def last_sums(o, sides, firsts, pair_own, vectors, early, no, nv):
    groups, rows, total = vectors.shape
    nr = len(sides[0])
    width = total // nr
    flat = [p for side in sides for p in side]
    n = len(flat)
    per = groups // nv
    own = rows // no
    small = own // (PIECES * 2)
    more = [] if early is None else [early]
    tile = min(width, 1024)
    tiles = total // tile

    def body(*refs):
        me = refs[0][0]
        refs = refs[1:]
        own_pair, vec = refs[n : n + 2]
        before = refs[n + 2] if more else None
        results = refs[n + 2 + len(more) : n + 2 + len(more) + 4 * PIECES]
        outs = refs[n + 2 + len(more) + 4 * PIECES : n + 2 + len(more) + 8 * PIECES]
        ins = refs[-n - 3 : -3]
        their_pair, sems, out_sems = refs[-3:]
        copies = [
            pltpu.make_async_copy(refs[i].at[pl.ds(firsts[i % nr], 1)], ins[i], sems.at[i])
            for i in range(n)
        ]
        for copy in copies[nr:] + copies[:nr]:
            copy.start()
        for copy in copies[nr:]:
            copy.wait()

        def store(g, _, pair):
            their_pair[g] = pair

        pairs_of(ins[nr:], vec, store)
        for copy in copies[:nr]:
            copy.wait()
        left = [p[...].reshape(groups * rows, rows) for p in (own_pair, their_pair)]
        sent = []
        for i in range(tiles):
            r, at = i * tile // width, i * tile % width
            got = None
            for s in range(len(sides)):
                right = ins[s * nr + r][0, :, at : at + tile]
                term = jnp.dot(left[s], right, preferred_element_type=F32)
                got = term if got is None else got + term
            got = got.reshape(groups, rows, tile)
            if more:
                got = got + before[:, :, i * tile : (i + 1) * tile]
            got = got.reshape(groups, no, PIECES, 2, small, tile)
            for g in range(groups):
                v = g // per
                to = (r - v) % nr * width + at
                cols = slice(to, to + tile)
                for p in range(PIECES):
                    send_x, keep_x, send_y, keep_y = outs[4 * p : 4 * p + 4]
                    for oo in range(no):
                        if v == 0:
                            keep_x[g, oo, :, cols] = got[g, oo, p, 0]
                        else:
                            send_x[g - per, oo, :, cols] = got[g, oo, p, 0].astype(BF16)
            for oo in range(no):
                slot = lax.rem(oo - me + no, no)
                for g in range(groups):
                    to = (r - g // per) % nr * width + at
                    cols = slice(to, to + tile)
                    for p in range(PIECES):
                        outs[4 * p + 2][slot, g, :, cols] = got[g, oo, p, 1].astype(BF16)
                        outs[4 * p + 3][slot, g, :, cols] = got[g, oo, p, 1]
            for v in range(nv):
                cols = pl.ds((r - v) % nr * width + at, tile)
                for p in range(PIECES):
                    at_x = (pl.ds(0, per) if v == 0 else pl.ds((v - 1) * per, per), slice(None), slice(None), cols)
                    at_y = (pl.ds(v * per, per), slice(None), cols)
                    for k, source, where in (
                        (1 if v == 0 else 0, at_x, at_x),
                        (2, (pl.ds(1, no - 1), *at_y), (slice(None), *at_y)),
                        (3, (0, *at_y), at_y),
                    ):
                        out, result = outs[4 * p + k], results[4 * p + k]
                        sent.append(
                            pltpu.make_async_copy(
                                out.at[source], result.at[where], out_sems.at[len(sent)]
                            )
                        )
                        sent[-1].start()
        for copy in sent:
            copy.wait()

    shapes = [
        jax.ShapeDtypeStruct((groups - per, no, small, total), BF16),
        jax.ShapeDtypeStruct((per, no, small, total), F32),
        jax.ShapeDtypeStruct((no - 1, groups, small, total), BF16),
        jax.ShapeDtypeStruct((groups, small, total), F32),
    ] * PIECES
    every = (no, groups, small, total)
    held = [(shapes[0].shape, BF16), (shapes[1].shape, F32), (every, BF16), (every, F32)] * PIECES
    outs = pl.pallas_call(
        body,
        out_shape=[pltpu.HBM(x.shape, x.dtype) for x in shapes],
        in_specs=[SMEM] + [ANY] * n + [VMEM] * (2 + len(more)),
        out_specs=[HBM] * len(shapes),
        scratch_shapes=[pltpu.VMEM(x, d) for x, d in held]
        + [pltpu.VMEM((1, rows, width), BF16)] * n
        + [
            pltpu.VMEM((groups, rows, rows), BF16),
            pltpu.SemaphoreType.DMA((n,)),
            pltpu.SemaphoreType.DMA((tiles * nv * PIECES * 3,)),
        ],
        cost_estimate=cost(0, *shapes),
        compiler_params=params(),
        name="last_sums",
    )(o.reshape(1), *flat, pair_own, vectors, *more)
    return [outs[4 * p : 4 * p + 4] for p in range(PIECES)]


def per_device(na, nv, no, factors, trials):
    nq, rows, width = factors.shape
    nm, _, cols = trials.shape
    nz = na // CORES
    a, v, o = (lax.axis_index(name) for name in ("aux", "vir", "outer"))
    z, c = a // CORES, a % CORES
    half_m, take = nm // CORES, nq // nv
    block, total = CORES * cols, nv * width
    own = rows // no
    groups = nv * half_m
    early_steps = take - 1
    last_steps = take - early_steps

    mine = part(trials, o, own, 1).astype(BF16)
    others = [shift(mine, "vir", nv, -r) for r in range(1, nv)]

    def sends(source, first, size):
        return [
            lax.dynamic_slice_in_dim(source, (v - r) % nv * take + first, size, 0)
            for r in range(1, nv)
        ]

    def along_vir(group):
        return [shift(x, "vir", nv, -r - 1) for r, x in enumerate(group)]

    come = None
    if early_steps:
        group, others = lax.optimization_barrier((sends(factors, 0, early_steps), others))
        come = along_vir(group)

    both = jnp.concatenate([mine] + others, axis=0).reshape(nv, CORES, half_m, own, cols)
    given = sibling(lax.dynamic_index_in_dim(both, 1 - c, 1, False), na)
    kept = lax.dynamic_index_in_dim(both, c, 1, False)
    whole = jnp.where(
        c == 0,
        jnp.concatenate([kept, given], axis=-1),
        jnp.concatenate([given, kept], axis=-1),
    ).reshape(groups, own, block)
    later, whole = lax.optimization_barrier((factors, whole))

    blocks = []
    for t in sorted(range(nz), key=lambda t: min(t, nz - t)):
        got = whole if t == 0 else shift(whole, "aux", na, t, CORES)
        blocks.append((got, 0, nz, t))
        for s in range(1, no):
            blocks.append((shift(got, "outer", no, -s), 0, nz + s, t))
    where = jnp.stack(
        [((z - t) % nz * block - v * width) % total for t in range(nz)]
        + [(o + s) % no * own for s in range(no)]
    ).astype(jnp.int32)
    later, _ = lax.optimization_barrier((factors, blocks[no - 1][0]))
    held = (come, sends(later, early_steps, last_steps), [b[0] for b in blocks])
    come, group, _ = lax.optimization_barrier(held)
    come_last = along_vir(group)
    vectors = assemble(where, blocks, groups, rows, total)

    kept = lax.dynamic_slice_in_dim(later, v * take, take, 0)
    shown = sibling(kept, na)
    early = None
    if early_steps:
        got = come
        their = [[sibling(g, na)] for g in got]
        early = early_sums(
            [[[kept]] + [[g] for g in got], [[shown]] + their], early_steps, vectors
        )
    got, early = lax.optimization_barrier((come_last, early))
    sides = [[kept] + got, [shown] + [sibling(g, na) for g in got]]
    firsts = [early_steps] + [0] * (nv - 1)
    pair_own = step_pairs(sides[0], firsts, vectors)

    out = []
    for p in last_sums(o, sides, firsts, pair_own, vectors, early, no, nv):
        send_x, keep_x, send_y, keep_y = p
        come_x = [
            shift(send_x[(r - 1) * half_m : r * half_m], "vir", nv, r) for r in range(1, nv)
        ]

        def one(oo):
            got = lax.dynamic_index_in_dim(keep_x, oo, 1, False)
            for x in come_x:
                got += lax.dynamic_index_in_dim(x, oo, 1, False).astype(F32)
            return got

        come_x2 = [shift(one((o + s) % no).astype(BF16), "outer", no, s) for s in range(1, no)]
        u_one = one(o)
        for x in come_x2:
            u_one += x.astype(F32)

        come_y = [shift(send_y[s - 1], "outer", no, s) for s in range(1, no)]

        def two(r):
            rows_r = slice(r * half_m, (r + 1) * half_m)
            got = keep_y[rows_r]
            for x in come_y:
                got += x[rows_r].astype(F32)
            return got

        come_y2 = [shift(two(r).astype(BF16), "vir", nv, r) for r in range(1, nv)]
        u_two = two(0)
        for x in come_y2:
            u_two += x.astype(F32)
        u = jnp.concatenate([u_one, u_two], axis=1)

        def to(zz):
            return lax.dynamic_slice_in_dim(u, (zz * block - v * width) % total, block, 2)

        got = to(z)
        for t in range(1, nz):
            got += shift(to((z + t) % nz).astype(BF16), "aux", na, t, CORES).astype(F32)
        out.append(got)
    done = jnp.concatenate(out, axis=1)
    there = sibling(part(done, 1 - c, cols, 2), na)
    here = part(done, c, cols, 2)
    return jnp.where(
        c == 0, jnp.concatenate([here, there], axis=0), jnp.concatenate([there, here], axis=0)
    )


def solution(mesh):
    na, nv, no = (mesh.shape[name] for name in ("aux", "vir", "outer"))

    def step(factors, trials):
        nq, rows, width = factors.shape
        nm, _, cols = trials.shape
        fits = na % CORES == 0 and nm % CORES == 0 and nq % nv == 0
        fits = fits and width % (CORES * cols) == 0 and cols % 128 == 0
        fits = fits and rows % (no * PIECES * 2 * 16) == 0
        if fits:
            return per_device(na, nv, no, factors, trials)
        return plain(factors, trials)

    placed = (P(("aux", "outer"), None, "vir"), P("vir", None, "aux"))
    return jax.shard_map(
        step, mesh=mesh, in_specs=placed, out_specs=P("vir", "outer", "aux"), check_vma=False
    )
```

```python
import jax
import jax.numpy as jnp
from jax import lax
from jax.experimental import pallas as pl
from jax.experimental.pallas import tpu as pltpu
from jax.sharding import PartitionSpec as P

CORES = 2
PIECES = 2
VMEM_LIMIT = 30 * 2**20
F32, BF16 = jnp.float32, jnp.bfloat16
VMEM = pl.BlockSpec(memory_space=pltpu.VMEM)
ANY = pl.BlockSpec(memory_space=pl.ANY)
HBM = pl.BlockSpec(memory_space=pltpu.HBM)
SMEM = pl.BlockSpec(memory_space=pltpu.SMEM)


def plain(factors, trials):
    trial_b = trials.astype(jnp.bfloat16)
    gathered = lax.all_gather(trial_b, "aux", axis=2, tiled=True)
    columns = lax.all_gather(factors, "vir", axis=2, tiled=True)
    pairs = jnp.einsum(
        "qib,mjb->mqij", columns, gathered, preferred_element_type=jnp.float32
    ).astype(jnp.bfloat16)
    stacked = jnp.einsum("mqij,qja->mia", pairs, columns, preferred_element_type=jnp.float32)
    slices = lax.psum_scatter(stacked, "aux", scatter_dimension=2, tiled=True)
    return lax.psum_scatter(slices, "outer", scatter_dimension=1, tiled=True)


def shift(array, axis, size, step, stride=1):
    count = size // stride
    pairs = [
        (i, (i // stride + step) % count * stride + i % stride) for i in range(size)
    ]
    return lax.ppermute(array, axis, pairs)


def sibling(array, size):
    return lax.ppermute(array, "aux", [(i, i ^ 1) for i in range(size)])


def part(array, index, size, axis):
    return lax.dynamic_slice_in_dim(array, index * size, size, axis)


def dot_nt(a, b):
    return lax.dot_general(a, b, (((1,), (1,)), ((), ())), preferred_element_type=F32)


def params():
    return pltpu.CompilerParams(vmem_limit_bytes=VMEM_LIMIT)


def in_hbm(x):
    return pltpu.with_memory_space_constraint(x, pltpu.HBM)


def cost(flops, *arrays):
    moved = sum(x.size * x.dtype.itemsize for x in arrays)
    return pl.CostEstimate(flops=flops, bytes_accessed=moved, transcendentals=0)


def assemble(where, blocks, groups, rows, total):
    shape = jax.ShapeDtypeStruct((groups, rows, total), BF16)

    def body(at, *refs):
        out, sems = refs[-2:]
        copies = []
        for i, (_, first, row_slot, col_slot) in enumerate(blocks):
            many, share, block = refs[i].shape
            row = pl.multiple_of(at[row_slot], share)
            col = pl.multiple_of(at[col_slot], block)
            to = out.at[pl.ds(first, many), pl.ds(row, share), pl.ds(col, block)]
            copies.append(pltpu.make_async_copy(refs[i], to, sems.at[i]))
        for copy in copies:
            copy.start()
        for copy in copies:
            copy.wait()

    return pl.pallas_call(
        body,
        out_shape=shape,
        in_specs=[SMEM] + [ANY] * len(blocks),
        out_specs=ANY,
        scratch_shapes=[pltpu.SemaphoreType.DMA((len(blocks),))],
        cost_estimate=cost(0, shape),
        compiler_params=params(),
        name="assemble",
    )(where, *[in_hbm(b[0]) for b in blocks[:-1]], blocks[-1][0])


def pairs_of(refs, vec, store):
    groups, rows, _ = vec.shape
    count, _, width = refs[0].shape
    for g in range(groups):
        acc = None
        for r, ref in enumerate(refs):
            left = ref[...].reshape(count * rows, width)
            term = dot_nt(left, vec[g, :, r * width : (r + 1) * width])
            acc = term if acc is None else acc + term
        acc = acc.astype(BF16)
        for k in range(count):
            store(g, k, acc[k * rows : (k + 1) * rows])


def early_sums(sides, steps, vectors):
    groups, rows, total = vectors.shape
    nr = len(sides[0])
    width = total // nr
    slots = [pieces for side in sides for pieces in side]
    flat = [p for pieces in slots for p in pieces]
    n, ns = len(flat), len(slots)
    shape = jax.ShapeDtypeStruct((groups, rows, total), F32)
    tile = min(width, 512)
    tiles = total // tile

    def body(*refs):
        vec, out = refs[n : n + 2]
        held, sems = refs[-2:]
        ins = refs[n + 2 : n + 2 + ns]
        copies, i = [], 0
        for slot, pieces in zip(ins, slots):
            group, at = [], 0
            for piece in pieces:
                size = min(piece.shape[0], steps)
                to = slot.at[pl.ds(at, size)]
                group.append(pltpu.make_async_copy(refs[i].at[pl.ds(0, size)], to, sems.at[i]))
                group[-1].start()
                i, at = i + 1, at + size
            copies.append(group)
        for s in range(len(sides)):

            def store(g, k, pair, s=s):
                held[s, g * rows : (g + 1) * rows, k * rows : (k + 1) * rows] = pair

            for group in copies[s * nr : (s + 1) * nr]:
                for copy in group:
                    copy.wait()
            pairs_of(ins[s * nr : (s + 1) * nr], vec, store)
        for i in range(tiles):
            r, at = i * tile // width, i * tile % width
            acc = None
            for s in range(len(sides)):
                right = ins[s * nr + r][:, :, at : at + tile].reshape(steps * rows, tile)
                term = jnp.dot(held[s], right, preferred_element_type=F32)
                acc = term if acc is None else acc + term
            out[:, :, i * tile : (i + 1) * tile] = acc.reshape(groups, rows, tile)

    return pl.pallas_call(
        body,
        out_shape=shape,
        in_specs=[ANY] * n + [VMEM],
        out_specs=VMEM,
        scratch_shapes=[pltpu.VMEM((steps, rows, width), BF16)] * ns
        + [
            pltpu.VMEM((len(sides), groups * rows, steps * rows), BF16),
            pltpu.SemaphoreType.DMA((n,)),
        ],
        cost_estimate=cost(0, vectors),
        compiler_params=params(),
        name="early_sums",
    )(*flat, vectors)


def step_pairs(side, firsts, vectors):
    groups, rows, total = vectors.shape
    shape = jax.ShapeDtypeStruct((groups, rows, rows), BF16)
    n = len(side)
    width = total // n

    def body(*refs):
        vec, out = refs[n : n + 2]
        ins = refs[n + 2 : 2 * n + 2]
        sems = refs[-1]
        copies = [
            pltpu.make_async_copy(refs[i].at[pl.ds(firsts[i], 1)], ins[i], sems.at[i])
            for i in range(n)
        ]
        for copy in copies:
            copy.start()
        for copy in copies:
            copy.wait()

        def store(g, _, pair):
            out[g] = pair

        pairs_of(ins, vec, store)

    return pl.pallas_call(
        body,
        out_shape=shape,
        in_specs=[ANY] * n + [VMEM],
        out_specs=VMEM,
        scratch_shapes=[pltpu.VMEM((1, rows, width), BF16)] * n
        + [pltpu.SemaphoreType.DMA((n,))],
        cost_estimate=cost(0, vectors),
        compiler_params=params(),
        name="step_pairs",
    )(*side, vectors)


def last_sums(o, sides, firsts, pair_own, vectors, early, no, nv):
    groups, rows, total = vectors.shape
    nr = len(sides[0])
    width = total // nr
    flat = [p for side in sides for p in side]
    n = len(flat)
    per = groups // nv
    own = rows // no
    small = own // (PIECES * 2)
    more = [] if early is None else [early]
    tile = min(width, 1024)
    tiles = total // tile

    def body(*refs):
        me = refs[0][0]
        refs = refs[1:]
        own_pair, vec = refs[n : n + 2]
        before = refs[n + 2] if more else None
        results = refs[n + 2 + len(more) : n + 2 + len(more) + 4 * PIECES]
        outs = refs[n + 2 + len(more) + 4 * PIECES : n + 2 + len(more) + 8 * PIECES]
        ins = refs[-n - 3 : -3]
        their_pair, sems, out_sems = refs[-3:]
        copies = [
            pltpu.make_async_copy(refs[i].at[pl.ds(firsts[i % nr], 1)], ins[i], sems.at[i])
            for i in range(n)
        ]
        for copy in copies[nr:] + copies[:nr]:
            copy.start()
        for copy in copies[nr:]:
            copy.wait()

        def store(g, _, pair):
            their_pair[g] = pair

        pairs_of(ins[nr:], vec, store)
        for copy in copies[:nr]:
            copy.wait()
        left = [p[...].reshape(groups * rows, rows) for p in (own_pair, their_pair)]
        sent = []
        for i in range(tiles):
            r, at = i * tile // width, i * tile % width
            got = None
            for s in range(len(sides)):
                right = ins[s * nr + r][0, :, at : at + tile]
                term = jnp.dot(left[s], right, preferred_element_type=F32)
                got = term if got is None else got + term
            got = got.reshape(groups, rows, tile)
            if more:
                got = got + before[:, :, i * tile : (i + 1) * tile]
            got = got.reshape(groups, no, PIECES, 2, small, tile)
            for g in range(groups):
                v = g // per
                to = (r - v) % nr * width + at
                cols = slice(to, to + tile)
                for p in range(PIECES):
                    send_x, keep_x, send_y, keep_y = outs[4 * p : 4 * p + 4]
                    for oo in range(no):
                        if v == 0:
                            keep_x[g, oo, :, cols] = got[g, oo, p, 0]
                        else:
                            send_x[g - per, oo, :, cols] = got[g, oo, p, 0].astype(BF16)
            for oo in range(no):
                slot = lax.rem(oo - me + no, no)
                for g in range(groups):
                    to = (r - g // per) % nr * width + at
                    cols = slice(to, to + tile)
                    for p in range(PIECES):
                        outs[4 * p + 2][slot, g, :, cols] = got[g, oo, p, 1].astype(BF16)
                        outs[4 * p + 3][slot, g, :, cols] = got[g, oo, p, 1]
            for v in range(nv):
                cols = pl.ds((r - v) % nr * width + at, tile)
                for p in range(PIECES):
                    at_x = (pl.ds(0, per) if v == 0 else pl.ds((v - 1) * per, per), slice(None), slice(None), cols)
                    at_y = (pl.ds(v * per, per), slice(None), cols)
                    for k, source, where in (
                        (1 if v == 0 else 0, at_x, at_x),
                        (2, (pl.ds(1, no - 1), *at_y), (slice(None), *at_y)),
                        (3, (0, *at_y), at_y),
                    ):
                        out, result = outs[4 * p + k], results[4 * p + k]
                        sent.append(
                            pltpu.make_async_copy(
                                out.at[source], result.at[where], out_sems.at[len(sent)]
                            )
                        )
                        sent[-1].start()
        for copy in sent:
            copy.wait()

    shapes = [
        jax.ShapeDtypeStruct((groups - per, no, small, total), BF16),
        jax.ShapeDtypeStruct((per, no, small, total), F32),
        jax.ShapeDtypeStruct((no - 1, groups, small, total), BF16),
        jax.ShapeDtypeStruct((groups, small, total), F32),
    ] * PIECES
    every = (no, groups, small, total)
    held = [(shapes[0].shape, BF16), (shapes[1].shape, F32), (every, BF16), (every, F32)] * PIECES
    outs = pl.pallas_call(
        body,
        out_shape=[pltpu.HBM(x.shape, x.dtype) for x in shapes],
        in_specs=[SMEM] + [ANY] * n + [VMEM] * (2 + len(more)),
        out_specs=[HBM] * len(shapes),
        scratch_shapes=[pltpu.VMEM(x, d) for x, d in held]
        + [pltpu.VMEM((1, rows, width), BF16)] * n
        + [
            pltpu.VMEM((groups, rows, rows), BF16),
            pltpu.SemaphoreType.DMA((n,)),
            pltpu.SemaphoreType.DMA((tiles * nv * PIECES * 3,)),
        ],
        cost_estimate=cost(0, *shapes),
        compiler_params=params(),
        name="last_sums",
    )(o.reshape(1), *flat, pair_own, vectors, *more)
    return [outs[4 * p : 4 * p + 4] for p in range(PIECES)]


def per_device(na, nv, no, factors, trials):
    nq, rows, width = factors.shape
    nm, _, cols = trials.shape
    nz = na // CORES
    a, v, o = (lax.axis_index(name) for name in ("aux", "vir", "outer"))
    z, c = a // CORES, a % CORES
    half_m, take = nm // CORES, nq // nv
    block, total = CORES * cols, nv * width
    own = rows // no
    groups = nv * half_m
    early_steps = take - 1
    last_steps = take - early_steps

    mine = part(trials, o, own, 1).astype(BF16)
    others = [shift(mine, "vir", nv, -r) for r in range(1, nv)]

    def sends(source, first, size):
        return [
            lax.dynamic_slice_in_dim(source, (v - r) % nv * take + first, size, 0)
            for r in range(1, nv)
        ]

    def along_vir(group):
        return [shift(x, "vir", nv, -r - 1) for r, x in enumerate(group)]

    come = None
    if early_steps:
        group, others = lax.optimization_barrier((sends(factors, 0, early_steps), others))
        come = along_vir(group)

    both = jnp.concatenate([mine] + others, axis=0).reshape(nv, CORES, half_m, own, cols)
    given = sibling(lax.dynamic_index_in_dim(both, 1 - c, 1, False), na)
    kept = lax.dynamic_index_in_dim(both, c, 1, False)
    whole = jnp.where(
        c == 0,
        jnp.concatenate([kept, given], axis=-1),
        jnp.concatenate([given, kept], axis=-1),
    ).reshape(groups, own, block)
    later, whole = lax.optimization_barrier((factors, whole))

    blocks = []
    for t in sorted(range(nz), key=lambda t: min(t, nz - t)):
        got = whole if t == 0 else shift(whole, "aux", na, t, CORES)
        blocks.append((got, 0, nz, t))
        for s in range(1, no):
            blocks.append((shift(got, "outer", no, -s), 0, nz + s, t))
    where = jnp.stack(
        [((z - t) % nz * block - v * width) % total for t in range(nz)]
        + [(o + s) % no * own for s in range(no)]
    ).astype(jnp.int32)
    later, _ = lax.optimization_barrier((factors, blocks[no - 1][0]))
    held = (come, sends(later, early_steps, last_steps), [b[0] for b in blocks])
    come, group, _ = lax.optimization_barrier(held)
    come_last = along_vir(group)
    vectors = assemble(where, blocks, groups, rows, total)

    kept = lax.dynamic_slice_in_dim(later, v * take, take, 0)
    shown = sibling(kept, na)
    early = None
    if early_steps:
        got = come
        their = [[sibling(g, na)] for g in got]
        early = early_sums(
            [[[kept]] + [[g] for g in got], [[shown]] + their], early_steps, vectors
        )
    got, early = lax.optimization_barrier((come_last, early))
    sides = [[kept] + got, [shown] + [sibling(g, na) for g in got]]
    firsts = [early_steps] + [0] * (nv - 1)
    pair_own = step_pairs(sides[0], firsts, vectors)

    out = []
    for p in last_sums(o, sides, firsts, pair_own, vectors, early, no, nv):
        send_x, keep_x, send_y, keep_y = p
        one = keep_x
        for r in range(1, nv):
            sent = send_x[(r - 1) * half_m : r * half_m]
            one += shift(sent, "vir", nv, r).astype(F32)
        u_one = lax.dynamic_index_in_dim(one, o, 1, False)
        for s in range(1, no):
            sent = lax.dynamic_index_in_dim(one, (o + s) % no, 1, False).astype(BF16)
            u_one += shift(sent, "outer", no, s).astype(F32)
        two = keep_y
        for s in range(1, no):
            two += shift(send_y[s - 1], "outer", no, s).astype(F32)
        u_two = two[:half_m]
        for r in range(1, nv):
            sent = two[r * half_m : (r + 1) * half_m].astype(BF16)
            u_two += shift(sent, "vir", nv, r).astype(F32)
        u = jnp.concatenate([u_one, u_two], axis=1)

        def to(zz):
            return lax.dynamic_slice_in_dim(u, (zz * block - v * width) % total, block, 2)

        got = to(z)
        for t in range(1, nz):
            got += shift(to((z + t) % nz).astype(BF16), "aux", na, t, CORES).astype(F32)
        out.append(got)
    done = jnp.concatenate(out, axis=1)
    there = sibling(part(done, 1 - c, cols, 2), na)
    here = part(done, c, cols, 2)
    return jnp.where(
        c == 0, jnp.concatenate([here, there], axis=0), jnp.concatenate([there, here], axis=0)
    )


def solution(mesh):
    na, nv, no = (mesh.shape[name] for name in ("aux", "vir", "outer"))

    def step(factors, trials):
        nq, rows, width = factors.shape
        nm, _, cols = trials.shape
        fits = na % CORES == 0 and nm % CORES == 0 and nq % nv == 0
        fits = fits and width % (CORES * cols) == 0 and cols % 128 == 0
        fits = fits and rows % (no * PIECES * 2 * 16) == 0
        if fits:
            return per_device(na, nv, no, factors, trials)
        return plain(factors, trials)

    placed = (P(("aux", "outer"), None, "vir"), P("vir", None, "aux"))
    return jax.shard_map(
        step, mesh=mesh, in_specs=placed, out_specs=P("vir", "outer", "aux"), check_vma=False
    )
```

```python
import jax
import jax.numpy as jnp
from jax import lax
from jax.experimental import pallas as pl
from jax.experimental.pallas import tpu as pltpu
from jax.sharding import PartitionSpec as P

CORES = 2
PIECES = 2
VMEM_LIMIT = 30 * 2**20
VMEM_LARGE = 44 * 2**20
F32, BF16 = jnp.float32, jnp.bfloat16
VMEM = pl.BlockSpec(memory_space=pltpu.VMEM)
ANY = pl.BlockSpec(memory_space=pl.ANY)
HBM = pl.BlockSpec(memory_space=pltpu.HBM)
SMEM = pl.BlockSpec(memory_space=pltpu.SMEM)


def plain(factors, trials):
    trial_b = trials.astype(jnp.bfloat16)
    gathered = lax.all_gather(trial_b, "aux", axis=2, tiled=True)
    columns = lax.all_gather(factors, "vir", axis=2, tiled=True)
    pairs = jnp.einsum(
        "qib,mjb->mqij", columns, gathered, preferred_element_type=jnp.float32
    ).astype(jnp.bfloat16)
    stacked = jnp.einsum("mqij,qja->mia", pairs, columns, preferred_element_type=jnp.float32)
    slices = lax.psum_scatter(stacked, "aux", scatter_dimension=2, tiled=True)
    return lax.psum_scatter(slices, "outer", scatter_dimension=1, tiled=True)


def shift(array, axis, size, step, stride=1):
    count = size // stride
    pairs = [
        (i, (i // stride + step) % count * stride + i % stride) for i in range(size)
    ]
    return lax.ppermute(array, axis, pairs)


def sibling(array, size):
    return lax.ppermute(array, "aux", [(i, i ^ 1) for i in range(size)])


def part(array, index, size, axis):
    return lax.dynamic_slice_in_dim(array, index * size, size, axis)


def dot_nt(a, b):
    return lax.dot_general(a, b, (((1,), (1,)), ((), ())), preferred_element_type=F32)


def params(sums=0):
    large = 4 * sums > 8 * 2**20
    return pltpu.CompilerParams(vmem_limit_bytes=VMEM_LARGE if large else VMEM_LIMIT)


def in_hbm(x):
    return pltpu.with_memory_space_constraint(x, pltpu.HBM)


def cost(flops, *arrays):
    moved = sum(x.size * x.dtype.itemsize for x in arrays)
    return pl.CostEstimate(flops=flops, bytes_accessed=moved, transcendentals=0)


def assemble(where, blocks, groups, rows, total):
    shape = jax.ShapeDtypeStruct((groups, rows, total), BF16)

    def body(at, *refs):
        out, sems = refs[-2:]
        copies = []
        for i, (_, first, row_slot, col_slot) in enumerate(blocks):
            many, share, block = refs[i].shape
            row = pl.multiple_of(at[row_slot], share)
            col = pl.multiple_of(at[col_slot], block)
            to = out.at[pl.ds(first, many), pl.ds(row, share), pl.ds(col, block)]
            copies.append(pltpu.make_async_copy(refs[i], to, sems.at[i]))
        for copy in copies:
            copy.start()
        for copy in copies:
            copy.wait()

    return pl.pallas_call(
        body,
        out_shape=shape,
        in_specs=[SMEM] + [ANY] * len(blocks),
        out_specs=ANY,
        scratch_shapes=[pltpu.SemaphoreType.DMA((len(blocks),))],
        cost_estimate=cost(0, shape),
        compiler_params=params(),
        name="assemble",
    )(where, *[in_hbm(b[0]) for b in blocks[:-1]], blocks[-1][0])


def pairs_of(refs, vec, store):
    groups, rows, _ = vec.shape
    count, _, width = refs[0].shape
    for g in range(groups):
        acc = None
        for r, ref in enumerate(refs):
            left = ref[...].reshape(count * rows, width)
            term = dot_nt(left, vec[g, :, r * width : (r + 1) * width])
            acc = term if acc is None else acc + term
        acc = acc.astype(BF16)
        for k in range(count):
            store(g, k, acc[k * rows : (k + 1) * rows])


def early_sums(sides, steps, vectors):
    groups, rows, total = vectors.shape
    nr = len(sides[0])
    width = total // nr
    slots = [pieces for side in sides for pieces in side]
    flat = [p for pieces in slots for p in pieces]
    n, ns = len(flat), len(slots)
    shape = jax.ShapeDtypeStruct((groups, rows, total), F32)
    tile = min(width, 512)
    tiles = total // tile

    def body(*refs):
        vec, out = refs[n : n + 2]
        held, sems = refs[-2:]
        ins = refs[n + 2 : n + 2 + ns]
        copies, i = [], 0
        for slot, pieces in zip(ins, slots):
            group, at = [], 0
            for piece in pieces:
                size = min(piece.shape[0], steps)
                to = slot.at[pl.ds(at, size)]
                group.append(pltpu.make_async_copy(refs[i].at[pl.ds(0, size)], to, sems.at[i]))
                group[-1].start()
                i, at = i + 1, at + size
            copies.append(group)
        for s in range(len(sides)):

            def store(g, k, pair, s=s):
                held[s, g * rows : (g + 1) * rows, k * rows : (k + 1) * rows] = pair

            for group in copies[s * nr : (s + 1) * nr]:
                for copy in group:
                    copy.wait()
            pairs_of(ins[s * nr : (s + 1) * nr], vec, store)
        for i in range(tiles):
            r, at = i * tile // width, i * tile % width
            acc = None
            for s in range(len(sides)):
                right = ins[s * nr + r][:, :, at : at + tile].reshape(steps * rows, tile)
                term = jnp.dot(held[s], right, preferred_element_type=F32)
                acc = term if acc is None else acc + term
            out[:, :, i * tile : (i + 1) * tile] = acc.reshape(groups, rows, tile)

    return pl.pallas_call(
        body,
        out_shape=shape,
        in_specs=[ANY] * n + [VMEM],
        out_specs=VMEM,
        scratch_shapes=[pltpu.VMEM((steps, rows, width), BF16)] * ns
        + [
            pltpu.VMEM((len(sides), groups * rows, steps * rows), BF16),
            pltpu.SemaphoreType.DMA((n,)),
        ],
        cost_estimate=cost(0, vectors),
        compiler_params=params(),
        name="early_sums",
    )(*flat, vectors)


def own_sums(side, firsts, vectors, early):
    groups, rows, total = vectors.shape
    n = len(side)
    width = total // n
    tile = min(width, 1024)
    more = [] if early is None else [early]
    shape = jax.ShapeDtypeStruct((groups, rows, total), F32)

    def body(*refs):
        vec = refs[n]
        out = refs[n + 1 + len(more)]
        before = refs[n + 1] if more else None
        ins = refs[n + 2 + len(more) : 2 * n + 2 + len(more)]
        pairs, sems = refs[-2:]
        copies = [
            pltpu.make_async_copy(refs[i].at[pl.ds(firsts[i], 1)], ins[i], sems.at[i])
            for i in range(n)
        ]
        for copy in copies:
            copy.start()
        for copy in copies:
            copy.wait()

        def store(g, _, pair):
            pairs[g * rows : (g + 1) * rows] = pair

        pairs_of(ins, vec, store)
        for i in range(total // tile):
            r, at = i * tile // width, i * tile % width
            cols = slice(i * tile, (i + 1) * tile)
            got = jnp.dot(pairs[...], ins[r][0, :, at : at + tile], preferred_element_type=F32)
            got = got.reshape(groups, rows, tile)
            out[:, :, cols] = got if before is None else got + before[:, :, cols]

    return pl.pallas_call(
        body,
        out_shape=shape,
        in_specs=[ANY] * n + [VMEM] * (1 + len(more)),
        out_specs=VMEM,
        scratch_shapes=[pltpu.VMEM((1, rows, width), BF16)] * n
        + [pltpu.VMEM((groups * rows, rows), BF16), pltpu.SemaphoreType.DMA((n,))],
        input_output_aliases={n + 1: 0} if more else {},
        cost_estimate=cost(0, vectors),
        compiler_params=params(vectors.size),
        name="own_sums",
    )(*side, vectors, *more)


def last_sums(o, side, firsts, vectors, sums, no, nv):
    groups, rows, total = vectors.shape
    nr = n = len(side)
    width = total // nr
    per = groups // nv
    own = rows // no
    small = own // (PIECES * 2)
    tile = min(width, 1024)
    tiles = total // tile

    def body(*refs):
        me = refs[0][0]
        refs = refs[1:]
        vec, before = refs[n : n + 2]
        results = refs[n + 2 : n + 2 + 4 * PIECES]
        outs = refs[n + 2 + 4 * PIECES : n + 2 + 8 * PIECES]
        ins = refs[-n - 3 : -3]
        their_pair, sems, out_sems = refs[-3:]
        copies = [
            pltpu.make_async_copy(refs[i].at[pl.ds(firsts[i], 1)], ins[i], sems.at[i])
            for i in range(n)
        ]
        for copy in copies:
            copy.start()
        for copy in copies:
            copy.wait()

        def store(g, _, pair):
            their_pair[g] = pair

        pairs_of(ins, vec, store)
        left = their_pair[...].reshape(groups * rows, rows)
        sent = []
        for i in range(tiles):
            r, at = i * tile // width, i * tile % width
            got = jnp.dot(left, ins[r][0, :, at : at + tile], preferred_element_type=F32)
            got = got.reshape(groups, rows, tile) + before[:, :, i * tile : (i + 1) * tile]
            got = got.reshape(groups, no, PIECES, 2, small, tile)
            for g in range(groups):
                v = g // per
                to = (r - v) % nr * width + at
                cols = slice(to, to + tile)
                for p in range(PIECES):
                    send_x, keep_x, send_y, keep_y = outs[4 * p : 4 * p + 4]
                    for oo in range(no):
                        if v == 0:
                            keep_x[g, oo, :, cols] = got[g, oo, p, 0]
                        else:
                            send_x[g - per, oo, :, cols] = got[g, oo, p, 0].astype(BF16)
            for oo in range(no):
                slot = lax.rem(oo - me + no, no)
                for g in range(groups):
                    to = (r - g // per) % nr * width + at
                    cols = slice(to, to + tile)
                    for p in range(PIECES):
                        outs[4 * p + 2][slot, g, :, cols] = got[g, oo, p, 1].astype(BF16)
                        outs[4 * p + 3][slot, g, :, cols] = got[g, oo, p, 1]
            for v in range(nv):
                cols = pl.ds((r - v) % nr * width + at, tile)
                for p in range(PIECES):
                    at_x = (pl.ds(0, per) if v == 0 else pl.ds((v - 1) * per, per), slice(None), slice(None), cols)
                    at_y = (pl.ds(v * per, per), slice(None), cols)
                    for k, source, where in (
                        (1 if v == 0 else 0, at_x, at_x),
                        (2, (pl.ds(1, no - 1), *at_y), (slice(None), *at_y)),
                        (3, (0, *at_y), at_y),
                    ):
                        out, result = outs[4 * p + k], results[4 * p + k]
                        sent.append(
                            pltpu.make_async_copy(
                                out.at[source], result.at[where], out_sems.at[len(sent)]
                            )
                        )
                        sent[-1].start()
        for copy in sent:
            copy.wait()

    shapes = [
        jax.ShapeDtypeStruct((groups - per, no, small, total), BF16),
        jax.ShapeDtypeStruct((per, no, small, total), F32),
        jax.ShapeDtypeStruct((no - 1, groups, small, total), BF16),
        jax.ShapeDtypeStruct((groups, small, total), F32),
    ] * PIECES
    every = (no, groups, small, total)
    held = [(shapes[0].shape, BF16), (shapes[1].shape, F32), (every, BF16), (every, F32)] * PIECES
    outs = pl.pallas_call(
        body,
        out_shape=[pltpu.HBM(x.shape, x.dtype) for x in shapes],
        in_specs=[SMEM] + [ANY] * n + [VMEM] * 2,
        out_specs=[HBM] * len(shapes),
        scratch_shapes=[pltpu.VMEM(x, d) for x, d in held]
        + [pltpu.VMEM((1, rows, width), BF16)] * n
        + [
            pltpu.VMEM((groups, rows, rows), BF16),
            pltpu.SemaphoreType.DMA((n,)),
            pltpu.SemaphoreType.DMA((tiles * nv * PIECES * 3,)),
        ],
        cost_estimate=cost(0, *shapes),
        compiler_params=params(vectors.size),
        name="last_sums",
    )(o.reshape(1), *side, vectors, sums)
    return [outs[4 * p : 4 * p + 4] for p in range(PIECES)]


def per_device(na, nv, no, factors, trials):
    nq, rows, width = factors.shape
    nm, _, cols = trials.shape
    nz = na // CORES
    a, v, o = (lax.axis_index(name) for name in ("aux", "vir", "outer"))
    z, c = a // CORES, a % CORES
    half_m, take = nm // CORES, nq // nv
    block, total = CORES * cols, nv * width
    own = rows // no
    groups = nv * half_m
    early_steps = take - 1
    last_steps = take - early_steps

    mine = part(trials, o, own, 1).astype(BF16)
    others = [shift(mine, "vir", nv, -r) for r in range(1, nv)]

    def sends(source, first, size):
        return [
            lax.dynamic_slice_in_dim(source, (v - r) % nv * take + first, size, 0)
            for r in range(1, nv)
        ]

    def along_vir(group):
        return [shift(x, "vir", nv, -r - 1) for r, x in enumerate(group)]

    come = None
    if early_steps:
        group, others = lax.optimization_barrier((sends(factors, 0, early_steps), others))
        come = along_vir(group)

    both = jnp.concatenate([mine] + others, axis=0).reshape(nv, CORES, half_m, own, cols)
    given = sibling(lax.dynamic_index_in_dim(both, 1 - c, 1, False), na)
    kept = lax.dynamic_index_in_dim(both, c, 1, False)
    whole = jnp.where(
        c == 0,
        jnp.concatenate([kept, given], axis=-1),
        jnp.concatenate([given, kept], axis=-1),
    ).reshape(groups, own, block)
    later, whole = lax.optimization_barrier((factors, whole))

    blocks = []
    for t in sorted(range(nz), key=lambda t: min(t, nz - t)):
        if min(t, nz - t) == 2:
            whole, _ = lax.optimization_barrier((whole, blocks[no - 1][0]))
        got = whole if t == 0 else shift(whole, "aux", na, t, CORES)
        blocks.append((got, 0, nz, t))
        for s in range(1, no):
            blocks.append((shift(got, "outer", no, -s), 0, nz + s, t))
    where = jnp.stack(
        [((z - t) % nz * block - v * width) % total for t in range(nz)]
        + [(o + s) % no * own for s in range(no)]
    ).astype(jnp.int32)
    later, _ = lax.optimization_barrier((factors, blocks[no - 1][0]))
    held = (come, sends(later, early_steps, last_steps), [b[0] for b in blocks])
    come, group, _ = lax.optimization_barrier(held)
    come_last = along_vir(group)
    vectors = assemble(where, blocks, groups, rows, total)

    kept = lax.dynamic_slice_in_dim(later, v * take, take, 0)
    shown = sibling(kept, na)
    early = None
    if early_steps:
        got = come
        their = [[sibling(g, na)] for g in got]
        early = early_sums(
            [[[kept]] + [[g] for g in got], [[shown]] + their], early_steps, vectors
        )
    got, early = lax.optimization_barrier((come_last, early))
    sides = [[kept] + got, [shown] + [sibling(g, na) for g in got]]
    firsts = [early_steps] + [0] * (nv - 1)
    sums = own_sums(sides[0], firsts, vectors, early)

    out = []
    for p in last_sums(o, sides[1], firsts, vectors, sums, no, nv):
        send_x, keep_x, send_y, keep_y = p
        one = keep_x
        for r in range(1, nv):
            sent = send_x[(r - 1) * half_m : r * half_m]
            one += shift(sent, "vir", nv, r).astype(F32)
        u_one = lax.dynamic_index_in_dim(one, o, 1, False)
        for s in range(1, no):
            sent = lax.dynamic_index_in_dim(one, (o + s) % no, 1, False).astype(BF16)
            u_one += shift(sent, "outer", no, s).astype(F32)
        two = keep_y
        for s in range(1, no):
            two += shift(send_y[s - 1], "outer", no, s).astype(F32)
        u_two = two[:half_m]
        for r in range(1, nv):
            sent = two[r * half_m : (r + 1) * half_m].astype(BF16)
            u_two += shift(sent, "vir", nv, r).astype(F32)
        u = jnp.concatenate([u_one, u_two], axis=1)

        def to(zz):
            return lax.dynamic_slice_in_dim(u, (zz * block - v * width) % total, block, 2)

        got = to(z)
        for t in range(1, nz):
            got += shift(to((z + t) % nz).astype(BF16), "aux", na, t, CORES).astype(F32)
        out.append(got)
    done = jnp.concatenate(out, axis=1)
    there = sibling(part(done, 1 - c, cols, 2), na)
    here = part(done, c, cols, 2)
    return jnp.where(
        c == 0, jnp.concatenate([here, there], axis=0), jnp.concatenate([there, here], axis=0)
    )


def solution(mesh):
    na, nv, no = (mesh.shape[name] for name in ("aux", "vir", "outer"))

    def step(factors, trials):
        nq, rows, width = factors.shape
        nm, _, cols = trials.shape
        fits = na % CORES == 0 and nm % CORES == 0 and nq % nv == 0
        fits = fits and width % (CORES * cols) == 0 and cols % 128 == 0
        fits = fits and rows % (no * PIECES * 2 * 16) == 0
        if fits:
            return per_device(na, nv, no, factors, trials)
        return plain(factors, trials)

    placed = (P(("aux", "outer"), None, "vir"), P("vir", None, "aux"))
    return jax.shard_map(
        step, mesh=mesh, in_specs=placed, out_specs=P("vir", "outer", "aux"), check_vma=False
    )
```

```python
import jax
import jax.numpy as jnp
from jax import lax
from jax.experimental import pallas as pl
from jax.experimental.pallas import tpu as pltpu
from jax.sharding import PartitionSpec as P

CORES = 2
PIECES = 2
VMEM_LIMIT = 30 * 2**20
VMEM_LARGE = 44 * 2**20
F32, BF16 = jnp.float32, jnp.bfloat16
VMEM = pl.BlockSpec(memory_space=pltpu.VMEM)
ANY = pl.BlockSpec(memory_space=pl.ANY)
HBM = pl.BlockSpec(memory_space=pltpu.HBM)
SMEM = pl.BlockSpec(memory_space=pltpu.SMEM)


def plain(factors, trials):
    trial_b = trials.astype(jnp.bfloat16)
    gathered = lax.all_gather(trial_b, "aux", axis=2, tiled=True)
    columns = lax.all_gather(factors, "vir", axis=2, tiled=True)
    pairs = jnp.einsum(
        "qib,mjb->mqij", columns, gathered, preferred_element_type=jnp.float32
    ).astype(jnp.bfloat16)
    stacked = jnp.einsum("mqij,qja->mia", pairs, columns, preferred_element_type=jnp.float32)
    slices = lax.psum_scatter(stacked, "aux", scatter_dimension=2, tiled=True)
    return lax.psum_scatter(slices, "outer", scatter_dimension=1, tiled=True)


def shift(array, axis, size, step, stride=1):
    count = size // stride
    pairs = [
        (i, (i // stride + step) % count * stride + i % stride) for i in range(size)
    ]
    return lax.ppermute(array, axis, pairs)


def sibling(array, size):
    return lax.ppermute(array, "aux", [(i, i ^ 1) for i in range(size)])


def part(array, index, size, axis):
    return lax.dynamic_slice_in_dim(array, index * size, size, axis)


def dot_nt(a, b):
    return lax.dot_general(a, b, (((1,), (1,)), ((), ())), preferred_element_type=F32)


def params(sums=0):
    large = 4 * sums > 8 * 2**20
    return pltpu.CompilerParams(vmem_limit_bytes=VMEM_LARGE if large else VMEM_LIMIT)


def in_hbm(x):
    return pltpu.with_memory_space_constraint(x, pltpu.HBM)


def cost(flops, *arrays):
    moved = sum(x.size * x.dtype.itemsize for x in arrays)
    return pl.CostEstimate(flops=flops, bytes_accessed=moved, transcendentals=0)


def assemble(where, blocks, groups, rows, total):
    shape = jax.ShapeDtypeStruct((groups, rows, total), BF16)

    def body(at, *refs):
        out, sems = refs[-2:]
        copies = []
        for i, (_, first, row_slot, col_slot) in enumerate(blocks):
            many, share, block = refs[i].shape
            row = pl.multiple_of(at[row_slot], share)
            col = pl.multiple_of(at[col_slot], block)
            to = out.at[pl.ds(first, many), pl.ds(row, share), pl.ds(col, block)]
            copies.append(pltpu.make_async_copy(refs[i], to, sems.at[i]))
        for copy in copies:
            copy.start()
        for copy in copies:
            copy.wait()

    return pl.pallas_call(
        body,
        out_shape=shape,
        in_specs=[SMEM] + [ANY] * len(blocks),
        out_specs=ANY,
        scratch_shapes=[pltpu.SemaphoreType.DMA((len(blocks),))],
        cost_estimate=cost(0, shape),
        compiler_params=params(),
        name="assemble",
    )(where, *[in_hbm(b[0]) for b in blocks[:-1]], blocks[-1][0])


def pairs_of(refs, vec, store):
    groups, rows, _ = vec.shape
    count, _, width = refs[0].shape
    for g in range(groups):
        acc = None
        for r, ref in enumerate(refs):
            left = ref[...].reshape(count * rows, width)
            term = dot_nt(left, vec[g, :, r * width : (r + 1) * width])
            acc = term if acc is None else acc + term
        acc = acc.astype(BF16)
        for k in range(count):
            store(g, k, acc[k * rows : (k + 1) * rows])


def early_sums(sides, steps, vectors):
    groups, rows, total = vectors.shape
    nr = len(sides[0])
    width = total // nr
    slots = [pieces for side in sides for pieces in side]
    flat = [p for pieces in slots for p in pieces]
    n, ns = len(flat), len(slots)
    shape = jax.ShapeDtypeStruct((groups, rows, total), F32)
    tile = min(width, 512)
    tiles = total // tile

    def body(*refs):
        vec, out = refs[n : n + 2]
        held, sems = refs[-2:]
        ins = refs[n + 2 : n + 2 + ns]
        copies, i = [], 0
        for slot, pieces in zip(ins, slots):
            group, at = [], 0
            for piece in pieces:
                size = min(piece.shape[0], steps)
                to = slot.at[pl.ds(at, size)]
                group.append(pltpu.make_async_copy(refs[i].at[pl.ds(0, size)], to, sems.at[i]))
                group[-1].start()
                i, at = i + 1, at + size
            copies.append(group)
        for s in range(len(sides)):

            def store(g, k, pair, s=s):
                held[s, g * rows : (g + 1) * rows, k * rows : (k + 1) * rows] = pair

            for group in copies[s * nr : (s + 1) * nr]:
                for copy in group:
                    copy.wait()
            pairs_of(ins[s * nr : (s + 1) * nr], vec, store)
        for i in range(tiles):
            r, at = i * tile // width, i * tile % width
            acc = None
            for s in range(len(sides)):
                right = ins[s * nr + r][:, :, at : at + tile].reshape(steps * rows, tile)
                term = jnp.dot(held[s], right, preferred_element_type=F32)
                acc = term if acc is None else acc + term
            out[:, :, i * tile : (i + 1) * tile] = acc.reshape(groups, rows, tile)

    return pl.pallas_call(
        body,
        out_shape=shape,
        in_specs=[ANY] * n + [VMEM],
        out_specs=VMEM,
        scratch_shapes=[pltpu.VMEM((steps, rows, width), BF16)] * ns
        + [
            pltpu.VMEM((len(sides), groups * rows, steps * rows), BF16),
            pltpu.SemaphoreType.DMA((n,)),
        ],
        cost_estimate=cost(0, vectors),
        compiler_params=params(),
        name="early_sums",
    )(*flat, vectors)


def own_sums(side, firsts, vectors, early):
    groups, rows, total = vectors.shape
    n = len(side)
    width = total // n
    tile = min(width, 1024)
    more = [] if early is None else [early]
    shape = jax.ShapeDtypeStruct((groups, rows, total), F32)

    def body(*refs):
        vec = refs[n]
        out = refs[n + 1 + len(more)]
        before = refs[n + 1] if more else None
        ins = refs[n + 2 + len(more) : 2 * n + 2 + len(more)]
        pairs, sems = refs[-2:]
        copies = [
            pltpu.make_async_copy(refs[i].at[pl.ds(firsts[i], 1)], ins[i], sems.at[i])
            for i in range(n)
        ]
        for copy in copies:
            copy.start()
        for copy in copies:
            copy.wait()

        def store(g, _, pair):
            pairs[g * rows : (g + 1) * rows] = pair

        pairs_of(ins, vec, store)
        for i in range(total // tile):
            r, at = i * tile // width, i * tile % width
            cols = slice(i * tile, (i + 1) * tile)
            got = jnp.dot(pairs[...], ins[r][0, :, at : at + tile], preferred_element_type=F32)
            got = got.reshape(groups, rows, tile)
            out[:, :, cols] = got if before is None else got + before[:, :, cols]

    return pl.pallas_call(
        body,
        out_shape=shape,
        in_specs=[ANY] * n + [VMEM] * (1 + len(more)),
        out_specs=VMEM,
        scratch_shapes=[pltpu.VMEM((1, rows, width), BF16)] * n
        + [pltpu.VMEM((groups * rows, rows), BF16), pltpu.SemaphoreType.DMA((n,))],
        input_output_aliases={n + 1: 0} if more else {},
        cost_estimate=cost(0, vectors),
        compiler_params=params(vectors.size),
        name="own_sums",
    )(*side, vectors, *more)


def last_sums(o, side, firsts, vectors, sums, no, nv):
    groups, rows, total = vectors.shape
    nr = n = len(side)
    width = total // nr
    per = groups // nv
    own = rows // no
    small = own // (PIECES * 2)
    tile = min(width, 1024)
    tiles = total // tile

    def body(*refs):
        me = refs[0][0]
        refs = refs[1:]
        vec, before = refs[n : n + 2]
        results = refs[n + 2 : n + 2 + 4 * PIECES]
        outs = refs[n + 2 + 4 * PIECES : n + 2 + 8 * PIECES]
        ins = refs[-n - 3 : -3]
        their_pair, sems, out_sems = refs[-3:]
        copies = [
            pltpu.make_async_copy(refs[i].at[pl.ds(firsts[i], 1)], ins[i], sems.at[i])
            for i in range(n)
        ]
        for copy in copies:
            copy.start()
        for copy in copies:
            copy.wait()

        def store(g, _, pair):
            their_pair[g] = pair

        pairs_of(ins, vec, store)
        left = their_pair[...].reshape(groups * rows, rows)
        sent = []
        for i in range(tiles):
            r, at = i * tile // width, i * tile % width
            got = jnp.dot(left, ins[r][0, :, at : at + tile], preferred_element_type=F32)
            got = got.reshape(groups, rows, tile) + before[:, :, i * tile : (i + 1) * tile]
            got = got.reshape(groups, no, PIECES, 2, small, tile)
            for g in range(groups):
                v = g // per
                to = (r - v) % nr * width + at
                cols = slice(to, to + tile)
                for p in range(PIECES):
                    send_x, keep_x, send_y, keep_y = outs[4 * p : 4 * p + 4]
                    for oo in range(no):
                        if v == 0:
                            keep_x[g, oo, :, cols] = got[g, oo, p, 0]
                        else:
                            send_x[g - per, oo, :, cols] = got[g, oo, p, 0].astype(BF16)
            for oo in range(no):
                slot = lax.rem(oo - me + no, no)
                for g in range(groups):
                    to = (r - g // per) % nr * width + at
                    cols = slice(to, to + tile)
                    for p in range(PIECES):
                        outs[4 * p + 2][slot, g, :, cols] = got[g, oo, p, 1].astype(BF16)
                        outs[4 * p + 3][slot, g, :, cols] = got[g, oo, p, 1]
            for v in range(nv):
                cols = pl.ds((r - v) % nr * width + at, tile)
                for p in range(PIECES):
                    at_x = (pl.ds(0, per) if v == 0 else pl.ds((v - 1) * per, per), slice(None), slice(None), cols)
                    at_y = (pl.ds(v * per, per), slice(None), cols)
                    for k, source, where in (
                        (1 if v == 0 else 0, at_x, at_x),
                        (2, (pl.ds(1, no - 1), *at_y), (slice(None), *at_y)),
                        (3, (0, *at_y), at_y),
                    ):
                        out, result = outs[4 * p + k], results[4 * p + k]
                        sent.append(
                            pltpu.make_async_copy(
                                out.at[source], result.at[where], out_sems.at[len(sent)]
                            )
                        )
                        sent[-1].start()
        for copy in sent:
            copy.wait()

    shapes = [
        jax.ShapeDtypeStruct((groups - per, no, small, total), BF16),
        jax.ShapeDtypeStruct((per, no, small, total), F32),
        jax.ShapeDtypeStruct((no - 1, groups, small, total), BF16),
        jax.ShapeDtypeStruct((groups, small, total), F32),
    ] * PIECES
    every = (no, groups, small, total)
    held = [(shapes[0].shape, BF16), (shapes[1].shape, F32), (every, BF16), (every, F32)] * PIECES
    outs = pl.pallas_call(
        body,
        out_shape=[pltpu.HBM(x.shape, x.dtype) for x in shapes],
        in_specs=[SMEM] + [ANY] * n + [VMEM] * 2,
        out_specs=[HBM] * len(shapes),
        scratch_shapes=[pltpu.VMEM(x, d) for x, d in held]
        + [pltpu.VMEM((1, rows, width), BF16)] * n
        + [
            pltpu.VMEM((groups, rows, rows), BF16),
            pltpu.SemaphoreType.DMA((n,)),
            pltpu.SemaphoreType.DMA((tiles * nv * PIECES * 3,)),
        ],
        cost_estimate=cost(0, *shapes),
        compiler_params=params(vectors.size),
        name="last_sums",
    )(o.reshape(1), *side, vectors, sums)
    return [outs[4 * p : 4 * p + 4] for p in range(PIECES)]


def per_device(na, nv, no, factors, trials):
    nq, rows, width = factors.shape
    nm, _, cols = trials.shape
    nz = na // CORES
    a, v, o = (lax.axis_index(name) for name in ("aux", "vir", "outer"))
    z, c = a // CORES, a % CORES
    half_m, take = nm // CORES, nq // nv
    block, total = CORES * cols, nv * width
    own = rows // no
    groups = nv * half_m
    early_steps = take - 1
    last_steps = take - early_steps

    mine = part(trials, o, own, 1).astype(BF16)
    others = [shift(mine, "vir", nv, -r) for r in range(1, nv)]

    def sends(source, first, size):
        return [
            lax.dynamic_slice_in_dim(source, (v - r) % nv * take + first, size, 0)
            for r in range(1, nv)
        ]

    def along_vir(group):
        return [shift(x, "vir", nv, -r - 1) for r, x in enumerate(group)]

    come = None
    if early_steps:
        group, others = lax.optimization_barrier((sends(factors, 0, early_steps), others))
        come = along_vir(group)

    both = jnp.concatenate([mine] + others, axis=0).reshape(nv, CORES, half_m, own, cols)
    given = sibling(lax.dynamic_index_in_dim(both, 1 - c, 1, False), na)
    kept = lax.dynamic_index_in_dim(both, c, 1, False)
    whole = jnp.where(
        c == 0,
        jnp.concatenate([kept, given], axis=-1),
        jnp.concatenate([given, kept], axis=-1),
    ).reshape(groups, own, block)
    later, whole = lax.optimization_barrier((factors, whole))

    blocks = []
    for t in sorted(range(nz), key=lambda t: min(t, nz - t)):
        if min(t, nz - t) == 2:
            whole, _ = lax.optimization_barrier((whole, blocks[no - 1][0]))
        got = whole if t == 0 else shift(whole, "aux", na, t, CORES)
        blocks.append((got, 0, nz, t))
        for s in range(1, no):
            blocks.append((shift(got, "outer", no, -s), 0, nz + s, t))
    where = jnp.stack(
        [((z - t) % nz * block - v * width) % total for t in range(nz)]
        + [(o + s) % no * own for s in range(no)]
    ).astype(jnp.int32)
    later, _ = lax.optimization_barrier((factors, blocks[no - 1][0]))
    held = (come, sends(later, early_steps, last_steps), [b[0] for b in blocks])
    come, group, _ = lax.optimization_barrier(held)
    come_last = along_vir(group)
    vectors = assemble(where, blocks, groups, rows, total)

    kept = lax.dynamic_slice_in_dim(later, v * take, take, 0)
    shown = sibling(kept, na)
    early = None
    if early_steps:
        got = come
        their = [[sibling(g, na)] for g in got]
        early = early_sums(
            [[[kept]] + [[g] for g in got], [[shown]] + their], early_steps, vectors
        )
    got, early = lax.optimization_barrier((come_last, early))
    sides = [[kept] + got, [shown] + [sibling(g, na) for g in got]]
    firsts = [early_steps] + [0] * (nv - 1)
    sums = own_sums(sides[0], firsts, vectors, early)

    out = []
    for p in last_sums(o, sides[1], firsts, vectors, sums, no, nv):
        send_x, keep_x, send_y, keep_y = p
        one = keep_x
        for r in range(1, nv):
            sent = send_x[(r - 1) * half_m : r * half_m]
            one += shift(sent, "vir", nv, r).astype(F32)
        u_one = lax.dynamic_index_in_dim(one, o, 1, False)
        for s in range(1, no):
            sent = lax.dynamic_index_in_dim(one, (o + s) % no, 1, False).astype(BF16)
            u_one += shift(sent, "outer", no, s).astype(F32)
        two = keep_y
        for s in range(1, no):
            two += shift(send_y[s - 1], "outer", no, s).astype(F32)
        u_two = two[:half_m]
        for r in range(1, nv):
            sent = two[r * half_m : (r + 1) * half_m].astype(BF16)
            u_two += shift(sent, "vir", nv, r).astype(F32)
        u = jnp.concatenate([u_one, u_two], axis=1)

        def to(zz):
            return lax.dynamic_slice_in_dim(u, (zz * block - v * width) % total, block, 2)

        got = to(z)
        for t in sorted(range(1, nz), key=lambda t: -min(t, nz - t)):
            got += shift(to((z + t) % nz).astype(BF16), "aux", na, t, CORES).astype(F32)
        out.append(got)
    done = jnp.concatenate(out, axis=1)
    there = sibling(part(done, 1 - c, cols, 2), na)
    here = part(done, c, cols, 2)
    return jnp.where(
        c == 0, jnp.concatenate([here, there], axis=0), jnp.concatenate([there, here], axis=0)
    )


def solution(mesh):
    na, nv, no = (mesh.shape[name] for name in ("aux", "vir", "outer"))

    def step(factors, trials):
        nq, rows, width = factors.shape
        nm, _, cols = trials.shape
        fits = na % CORES == 0 and nm % CORES == 0 and nq % nv == 0
        fits = fits and width % (CORES * cols) == 0 and cols % 128 == 0
        fits = fits and rows % (no * PIECES * 2 * 16) == 0
        if fits:
            return per_device(na, nv, no, factors, trials)
        return plain(factors, trials)

    placed = (P(("aux", "outer"), None, "vir"), P("vir", None, "aux"))
    return jax.shard_map(
        step, mesh=mesh, in_specs=placed, out_specs=P("vir", "outer", "aux"), check_vma=False
    )
```

```python
import jax
import jax.numpy as jnp
from jax import lax
from jax.experimental import pallas as pl
from jax.experimental.pallas import tpu as pltpu
from jax.sharding import PartitionSpec as P

CORES = 2
PIECES = 2
VMEM_LIMIT = 30 * 2**20
VMEM_LARGE = 44 * 2**20
F32, BF16 = jnp.float32, jnp.bfloat16
VMEM = pl.BlockSpec(memory_space=pltpu.VMEM)
ANY = pl.BlockSpec(memory_space=pl.ANY)
HBM = pl.BlockSpec(memory_space=pltpu.HBM)
SMEM = pl.BlockSpec(memory_space=pltpu.SMEM)


def plain(factors, trials):
    trial_b = trials.astype(jnp.bfloat16)
    gathered = lax.all_gather(trial_b, "aux", axis=2, tiled=True)
    columns = lax.all_gather(factors, "vir", axis=2, tiled=True)
    pairs = jnp.einsum(
        "qib,mjb->mqij", columns, gathered, preferred_element_type=jnp.float32
    ).astype(jnp.bfloat16)
    stacked = jnp.einsum("mqij,qja->mia", pairs, columns, preferred_element_type=jnp.float32)
    slices = lax.psum_scatter(stacked, "aux", scatter_dimension=2, tiled=True)
    return lax.psum_scatter(slices, "outer", scatter_dimension=1, tiled=True)


def shift(array, axis, size, step, stride=1):
    count = size // stride
    pairs = [
        (i, (i // stride + step) % count * stride + i % stride) for i in range(size)
    ]
    return lax.ppermute(array, axis, pairs)


def sibling(array, size):
    return lax.ppermute(array, "aux", [(i, i ^ 1) for i in range(size)])


def part(array, index, size, axis):
    return lax.dynamic_slice_in_dim(array, index * size, size, axis)


def dot_nt(a, b):
    return lax.dot_general(a, b, (((1,), (1,)), ((), ())), preferred_element_type=F32)


def params(sums=0):
    large = 4 * sums > 8 * 2**20
    return pltpu.CompilerParams(vmem_limit_bytes=VMEM_LARGE if large else VMEM_LIMIT)


def in_hbm(x):
    return pltpu.with_memory_space_constraint(x, pltpu.HBM)


def cost(flops, *arrays):
    moved = sum(x.size * x.dtype.itemsize for x in arrays)
    return pl.CostEstimate(flops=flops, bytes_accessed=moved, transcendentals=0)


def assemble(where, blocks, groups, rows, total):
    shape = jax.ShapeDtypeStruct((groups, rows, total), BF16)

    def body(at, *refs):
        out, sems = refs[-2:]
        copies = []
        for i, (_, first, row_slot, col_slot) in enumerate(blocks):
            many, share, block = refs[i].shape
            row = pl.multiple_of(at[row_slot], share)
            col = pl.multiple_of(at[col_slot], block)
            to = out.at[pl.ds(first, many), pl.ds(row, share), pl.ds(col, block)]
            copies.append(pltpu.make_async_copy(refs[i], to, sems.at[i]))
        for copy in copies:
            copy.start()
        for copy in copies:
            copy.wait()

    return pl.pallas_call(
        body,
        out_shape=shape,
        in_specs=[SMEM] + [ANY] * len(blocks),
        out_specs=ANY,
        scratch_shapes=[pltpu.SemaphoreType.DMA((len(blocks),))],
        cost_estimate=cost(0, shape),
        compiler_params=params(),
        name="assemble",
    )(where, *[in_hbm(b[0]) for b in blocks[:-1]], blocks[-1][0])


def pairs_of(refs, vec, store):
    groups, rows, _ = vec.shape
    count, _, width = refs[0].shape
    for g in range(groups):
        acc = None
        for r, ref in enumerate(refs):
            left = ref[...].reshape(count * rows, width)
            term = dot_nt(left, vec[g, :, r * width : (r + 1) * width])
            acc = term if acc is None else acc + term
        acc = acc.astype(BF16)
        for k in range(count):
            store(g, k, acc[k * rows : (k + 1) * rows])


def early_sums(sides, steps, vectors):
    groups, rows, total = vectors.shape
    nr = len(sides[0])
    width = total // nr
    slots = [pieces for side in sides for pieces in side]
    flat = [p for pieces in slots for p in pieces]
    n, ns = len(flat), len(slots)
    shape = jax.ShapeDtypeStruct((groups, rows, total), F32)
    tile = min(width, 512)
    tiles = total // tile

    def body(*refs):
        vec, out = refs[n : n + 2]
        held, sems = refs[-2:]
        ins = refs[n + 2 : n + 2 + ns]
        copies, i = [], 0
        for slot, pieces in zip(ins, slots):
            group, at = [], 0
            for piece in pieces:
                size = min(piece.shape[0], steps)
                to = slot.at[pl.ds(at, size)]
                group.append(pltpu.make_async_copy(refs[i].at[pl.ds(0, size)], to, sems.at[i]))
                group[-1].start()
                i, at = i + 1, at + size
            copies.append(group)
        for s in range(len(sides)):

            def store(g, k, pair, s=s):
                held[s, g * rows : (g + 1) * rows, k * rows : (k + 1) * rows] = pair

            for group in copies[s * nr : (s + 1) * nr]:
                for copy in group:
                    copy.wait()
            pairs_of(ins[s * nr : (s + 1) * nr], vec, store)
        for i in range(tiles):
            r, at = i * tile // width, i * tile % width
            acc = None
            for s in range(len(sides)):
                right = ins[s * nr + r][:, :, at : at + tile].reshape(steps * rows, tile)
                term = jnp.dot(held[s], right, preferred_element_type=F32)
                acc = term if acc is None else acc + term
            out[:, :, i * tile : (i + 1) * tile] = acc.reshape(groups, rows, tile)

    return pl.pallas_call(
        body,
        out_shape=shape,
        in_specs=[ANY] * n + [VMEM],
        out_specs=VMEM,
        scratch_shapes=[pltpu.VMEM((steps, rows, width), BF16)] * ns
        + [
            pltpu.VMEM((len(sides), groups * rows, steps * rows), BF16),
            pltpu.SemaphoreType.DMA((n,)),
        ],
        cost_estimate=cost(0, vectors),
        compiler_params=params(),
        name="early_sums",
    )(*flat, vectors)


def own_sums(side, firsts, vectors, early):
    groups, rows, total = vectors.shape
    n = len(side)
    width = total // n
    tile = min(width, 1024)
    more = [] if early is None else [early]
    shape = jax.ShapeDtypeStruct((groups, rows, total), F32)

    def body(*refs):
        vec = refs[n]
        out = refs[n + 1 + len(more)]
        before = refs[n + 1] if more else None
        ins = refs[n + 2 + len(more) : 2 * n + 2 + len(more)]
        pairs, sems = refs[-2:]
        copies = [
            pltpu.make_async_copy(refs[i].at[pl.ds(firsts[i], 1)], ins[i], sems.at[i])
            for i in range(n)
        ]
        for copy in copies:
            copy.start()
        for copy in copies:
            copy.wait()

        def store(g, _, pair):
            pairs[g * rows : (g + 1) * rows] = pair

        pairs_of(ins, vec, store)
        for i in range(total // tile):
            r, at = i * tile // width, i * tile % width
            cols = slice(i * tile, (i + 1) * tile)
            got = jnp.dot(pairs[...], ins[r][0, :, at : at + tile], preferred_element_type=F32)
            got = got.reshape(groups, rows, tile)
            out[:, :, cols] = got if before is None else got + before[:, :, cols]

    return pl.pallas_call(
        body,
        out_shape=shape,
        in_specs=[ANY] * n + [VMEM] * (1 + len(more)),
        out_specs=VMEM,
        scratch_shapes=[pltpu.VMEM((1, rows, width), BF16)] * n
        + [pltpu.VMEM((groups * rows, rows), BF16), pltpu.SemaphoreType.DMA((n,))],
        input_output_aliases={n + 1: 0} if more else {},
        cost_estimate=cost(0, vectors),
        compiler_params=params(vectors.size),
        name="own_sums",
    )(*side, vectors, *more)


def last_sums(o, side, firsts, vectors, sums, no, nv):
    groups, rows, total = vectors.shape
    nr = n = len(side)
    width = total // nr
    per = groups // nv
    own = rows // no
    small = own // (PIECES * 2)
    tile = min(width, 512)
    tiles = total // tile

    def body(*refs):
        me = refs[0][0]
        refs = refs[1:]
        vec, before = refs[n : n + 2]
        results = refs[n + 2 : n + 2 + 4 * PIECES]
        outs = refs[n + 2 + 4 * PIECES : n + 2 + 8 * PIECES]
        ins = refs[-n - 3 : -3]
        their_pair, sems, out_sems = refs[-3:]
        copies = [
            pltpu.make_async_copy(refs[i].at[pl.ds(firsts[i], 1)], ins[i], sems.at[i])
            for i in range(n)
        ]
        for copy in copies:
            copy.start()
        for copy in copies:
            copy.wait()

        def store(g, _, pair):
            their_pair[g] = pair

        pairs_of(ins, vec, store)
        left = their_pair[...].reshape(groups * rows, rows)
        sent = []
        for i in range(tiles):
            r, at = i * tile // width, i * tile % width
            got = jnp.dot(left, ins[r][0, :, at : at + tile], preferred_element_type=F32)
            got = got.reshape(groups, rows, tile) + before[:, :, i * tile : (i + 1) * tile]
            got = got.reshape(groups, no, PIECES, 2, small, tile)
            for g in range(groups):
                v = g // per
                to = (r - v) % nr * width + at
                cols = slice(to, to + tile)
                for p in range(PIECES):
                    send_x, keep_x, send_y, keep_y = outs[4 * p : 4 * p + 4]
                    for oo in range(no):
                        if v == 0:
                            keep_x[g, oo, :, cols] = got[g, oo, p, 0]
                        else:
                            send_x[g - per, oo, :, cols] = got[g, oo, p, 0].astype(BF16)
            for oo in range(no):
                slot = lax.rem(oo - me + no, no)
                for g in range(groups):
                    to = (r - g // per) % nr * width + at
                    cols = slice(to, to + tile)
                    for p in range(PIECES):
                        outs[4 * p + 2][slot, g, :, cols] = got[g, oo, p, 1].astype(BF16)
                        outs[4 * p + 3][slot, g, :, cols] = got[g, oo, p, 1]
            for v in range(nv):
                cols = pl.ds((r - v) % nr * width + at, tile)
                for p in range(PIECES):
                    at_x = (pl.ds(0, per) if v == 0 else pl.ds((v - 1) * per, per), slice(None), slice(None), cols)
                    at_y = (pl.ds(v * per, per), slice(None), cols)
                    for k, source, where in (
                        (1 if v == 0 else 0, at_x, at_x),
                        (2, (pl.ds(1, no - 1), *at_y), (slice(None), *at_y)),
                        (3, (0, *at_y), at_y),
                    ):
                        out, result = outs[4 * p + k], results[4 * p + k]
                        sent.append(
                            pltpu.make_async_copy(
                                out.at[source], result.at[where], out_sems.at[len(sent)]
                            )
                        )
                        sent[-1].start()
        for copy in sent:
            copy.wait()

    shapes = [
        jax.ShapeDtypeStruct((groups - per, no, small, total), BF16),
        jax.ShapeDtypeStruct((per, no, small, total), F32),
        jax.ShapeDtypeStruct((no - 1, groups, small, total), BF16),
        jax.ShapeDtypeStruct((groups, small, total), F32),
    ] * PIECES
    every = (no, groups, small, total)
    held = [(shapes[0].shape, BF16), (shapes[1].shape, F32), (every, BF16), (every, F32)] * PIECES
    outs = pl.pallas_call(
        body,
        out_shape=[pltpu.HBM(x.shape, x.dtype) for x in shapes],
        in_specs=[SMEM] + [ANY] * n + [VMEM] * 2,
        out_specs=[HBM] * len(shapes),
        scratch_shapes=[pltpu.VMEM(x, d) for x, d in held]
        + [pltpu.VMEM((1, rows, width), BF16)] * n
        + [
            pltpu.VMEM((groups, rows, rows), BF16),
            pltpu.SemaphoreType.DMA((n,)),
            pltpu.SemaphoreType.DMA((tiles * nv * PIECES * 3,)),
        ],
        cost_estimate=cost(0, *shapes),
        compiler_params=params(vectors.size),
        name="last_sums",
    )(o.reshape(1), *side, vectors, sums)
    return [outs[4 * p : 4 * p + 4] for p in range(PIECES)]


def per_device(na, nv, no, factors, trials):
    nq, rows, width = factors.shape
    nm, _, cols = trials.shape
    nz = na // CORES
    a, v, o = (lax.axis_index(name) for name in ("aux", "vir", "outer"))
    z, c = a // CORES, a % CORES
    half_m, take = nm // CORES, nq // nv
    block, total = CORES * cols, nv * width
    own = rows // no
    groups = nv * half_m
    early_steps = take - 1
    last_steps = take - early_steps

    mine = part(trials, o, own, 1).astype(BF16)
    others = [shift(mine, "vir", nv, -r) for r in range(1, nv)]

    def sends(source, first, size):
        return [
            lax.dynamic_slice_in_dim(source, (v - r) % nv * take + first, size, 0)
            for r in range(1, nv)
        ]

    def along_vir(group):
        return [shift(x, "vir", nv, -r - 1) for r, x in enumerate(group)]

    come = None
    if early_steps:
        group, others = lax.optimization_barrier((sends(factors, 0, early_steps), others))
        come = along_vir(group)

    both = jnp.concatenate([mine] + others, axis=0).reshape(nv, CORES, half_m, own, cols)
    given = sibling(lax.dynamic_index_in_dim(both, 1 - c, 1, False), na)
    kept = lax.dynamic_index_in_dim(both, c, 1, False)
    whole = jnp.where(
        c == 0,
        jnp.concatenate([kept, given], axis=-1),
        jnp.concatenate([given, kept], axis=-1),
    ).reshape(groups, own, block)
    later, whole = lax.optimization_barrier((factors, whole))

    blocks = []
    for t in sorted(range(nz), key=lambda t: min(t, nz - t)):
        if min(t, nz - t) == 2:
            whole, _ = lax.optimization_barrier((whole, blocks[no - 1][0]))
        got = whole if t == 0 else shift(whole, "aux", na, t, CORES)
        blocks.append((got, 0, nz, t))
        for s in range(1, no):
            blocks.append((shift(got, "outer", no, -s), 0, nz + s, t))
    where = jnp.stack(
        [((z - t) % nz * block - v * width) % total for t in range(nz)]
        + [(o + s) % no * own for s in range(no)]
    ).astype(jnp.int32)
    later, _ = lax.optimization_barrier((factors, blocks[no - 1][0]))
    held = (come, sends(later, early_steps, last_steps), [b[0] for b in blocks])
    come, group, _ = lax.optimization_barrier(held)
    come_last = along_vir(group)
    vectors = assemble(where, blocks, groups, rows, total)

    kept = lax.dynamic_slice_in_dim(later, v * take, take, 0)
    shown = sibling(kept, na)
    early = None
    if early_steps:
        got = come
        their = [[sibling(g, na)] for g in got]
        early = early_sums(
            [[[kept]] + [[g] for g in got], [[shown]] + their], early_steps, vectors
        )
    got, early = lax.optimization_barrier((come_last, early))
    sides = [[kept] + got, [shown] + [sibling(g, na) for g in got]]
    firsts = [early_steps] + [0] * (nv - 1)
    sums = own_sums(sides[0], firsts, vectors, early)

    out = []
    for p in last_sums(o, sides[1], firsts, vectors, sums, no, nv):
        send_x, keep_x, send_y, keep_y = p
        one = keep_x
        for r in range(1, nv):
            sent = send_x[(r - 1) * half_m : r * half_m]
            one += shift(sent, "vir", nv, r).astype(F32)
        u_one = lax.dynamic_index_in_dim(one, o, 1, False)
        for s in range(1, no):
            sent = lax.dynamic_index_in_dim(one, (o + s) % no, 1, False).astype(BF16)
            u_one += shift(sent, "outer", no, s).astype(F32)
        two = keep_y
        for s in range(1, no):
            two += shift(send_y[s - 1], "outer", no, s).astype(F32)
        u_two = two[:half_m]
        for r in range(1, nv):
            sent = two[r * half_m : (r + 1) * half_m].astype(BF16)
            u_two += shift(sent, "vir", nv, r).astype(F32)
        u = jnp.concatenate([u_one, u_two], axis=1)

        def to(zz):
            return lax.dynamic_slice_in_dim(u, (zz * block - v * width) % total, block, 2)

        got = to(z)
        for t in range(1, nz):
            got += shift(to((z + t) % nz).astype(BF16), "aux", na, t, CORES).astype(F32)
        out.append(got)
    done = jnp.concatenate(out, axis=1)
    there = sibling(part(done, 1 - c, cols, 2), na)
    here = part(done, c, cols, 2)
    return jnp.where(
        c == 0, jnp.concatenate([here, there], axis=0), jnp.concatenate([there, here], axis=0)
    )


def solution(mesh):
    na, nv, no = (mesh.shape[name] for name in ("aux", "vir", "outer"))

    def step(factors, trials):
        nq, rows, width = factors.shape
        nm, _, cols = trials.shape
        fits = na % CORES == 0 and nm % CORES == 0 and nq % nv == 0
        fits = fits and width % (CORES * cols) == 0 and cols % 128 == 0
        fits = fits and rows % (no * PIECES * 2 * 16) == 0
        if fits:
            return per_device(na, nv, no, factors, trials)
        return plain(factors, trials)

    placed = (P(("aux", "outer"), None, "vir"), P("vir", None, "aux"))
    return jax.shard_map(
        step, mesh=mesh, in_specs=placed, out_specs=P("vir", "outer", "aux"), check_vma=False
    )
```
